128 devices in a mesh: dp: 16 (over x_lo, y, core), tensor: 8 (over z, x_hi).
Axes of the slice: x: 4 (x_hi: 2, x_lo: 2; x = x_hi * 2 + x_lo), y: 4, z: 4, core: 2. Of those that a mesh axis runs over, the one named last changes fastest.
Arguments:
- tokens: bfloat16 [512, 8192], P(None, 'dp'), may hold values from -6 to 6
- gate_weight: bfloat16 [8192, 14336], P('dp', 'tensor'), may hold values from -0.0625 to 0.0625
- up_weight: bfloat16 [8192, 14336], P('dp', 'tensor'), may hold values from -0.0625 to 0.0625
- down_weight: bfloat16 [14336, 8192], P('tensor', 'dp'), may hold values from -0.046875 to 0.046875
- head_weight: bfloat16 [8192, 16384], P('dp', 'tensor'), may hold values from -2 to 2
- up_moment: float32 [8192, 14336], P('dp', 'tensor'), may hold values from -0.6 to 0.6
- up_curvature: float32 [8192, 14336], P('dp', 'tensor'), may hold values from 0.002 to 0.2
- true_labels: int32 [512], P('dp'), may hold values from 0 to 16383
- sampled_labels: int32 [512], P('dp'), may hold values from 0 to 16383
Outputs:
- new_moment: float32 [8192, 14336], P('dp', 'tensor')
- new_curvature: float32 [8192, 14336], P('dp', 'tensor')
- update: float32 [8192, 14336], P('dp', 'tensor')
The draws below stay inside these ranges and needn't reach their ends.
All inputs are finite; a program needn't handle non-finite values.
Results may differ from the reference program's by a relative error of at most 0.009.
Values may be sent and summed in bfloat16 or wider, within the bound.
No kernel may reach another device: no remote copies, remote signals or barrier semaphores. Data moves between devices by JAX's collectives and lax.ppermute only.
A program may use at most 128 MiB of HBM per device.

```python
import math
import jax
import jax.numpy as jnp
import numpy as np
from jax import lax

D = 8192
FF = 14336
VOCAB = 16384
TOKENS = 512


def token_base(key):
    return jax.random.truncated_normal(key, -6.0, 6.0, (TOKENS, D), jnp.float32)


def draw_tokens(key, part):
    base_field = token_base(key)
    return base_field.astype(jnp.bfloat16)


def draw_head_weight(key, part):
    base_field = token_base(key)
    key = jax.random.fold_in(key, 2)
    key_weights, key_rows, key_cols, key_levels = jax.random.split(key, 4)
    spread_scale = 3.0 / math.sqrt(D)
    weights = jax.random.truncated_normal(key_weights, -6.0, 6.0, (D, VOCAB), jnp.float32) * spread_scale
    levels = jnp.array([150.0, 200.0, 250.0, 300.0], jnp.float32)
    levels = levels * jax.random.uniform(key_levels, (4,), jnp.float32, 0.9, 1.1)
    chosen_rows = jax.random.permutation(key_rows, TOKENS)[:4]
    chosen_cols = jax.random.permutation(key_cols, VOCAB)[:8]
    picked = base_field[chosen_rows]
    quad_rows = picked.reshape(4, D // 4, 4)
    turn_one = jnp.stack([quad_rows[:, :, 1], -quad_rows[:, :, 0], quad_rows[:, :, 3], -quad_rows[:, :, 2]], axis=2).reshape(4, D)
    turn_two = jnp.stack([quad_rows[:, :, 2], quad_rows[:, :, 3], -quad_rows[:, :, 0], -quad_rows[:, :, 1]], axis=2).reshape(4, D)
    side_scale = 0.7 / math.sqrt(D)
    first_cols = levels[:, None] * picked / D + side_scale * turn_one
    second = (levels - 3.0)[:, None] * picked / D + side_scale * turn_two
    columns = jnp.concatenate([first_cols, second], axis=0)
    return weights.at[:, chosen_cols].set(columns.T).astype(jnp.bfloat16)


def with_ends(values, rng, smallest, top_value):
    dims = values.shape
    spot = [jax.random.randint(jax.random.fold_in(rng, axis), (), 0, dims[axis]) for axis in range(len(dims))]
    values = values.at[tuple(spot)].set(smallest)
    longest = dims.index(max(dims))
    spot[longest] = (spot[longest] + 1) % dims[longest]
    return values.at[tuple(spot)].set(top_value)


def level_of(own_key, shape, shards, least, largest):
    level = 1.0
    for dim, shards_of in shards:
        steps = jax.random.uniform(jax.random.fold_in(jax.random.fold_in(own_key, 6), dim), (shards_of,), jnp.float32, least / len(shards), largest / len(shards))
        level = level * jnp.repeat(jnp.exp(steps), shape[dim] // shards_of).reshape((-1,) + (1,) * (len(shape) - 1 - dim))
    return level


def rank_table(count, slope):
    loads = [(1 << 20) // math.isqrt(grade ** slope) + 1 for grade in range(1, count + 1)]
    deviation = 1 + sum(loads) // (1 << 30)
    return np.cumsum(np.array([max(1, weight // deviation) for weight in loads]))


def skewed_ids(own_key, shape, amount, lean):
    listing = rank_table(amount, lean)
    ticket = jax.random.randint(jax.random.fold_in(own_key, 1), shape, 0, int(listing[amount - 1]))
    grade = jnp.searchsorted(jnp.asarray(listing, jnp.int32), ticket, side="right")
    return jax.random.permutation(jax.random.fold_in(own_key, 2), amount)[grade].astype(jnp.int32)


def centred(stream_key, dims, scale, limit, pieces=(), kind=jnp.bfloat16):
    level = level_of(stream_key, dims, pieces, -0.22, 0.18) if pieces else 1.0
    result = jax.random.normal(stream_key, dims, jnp.float32) * scale * level
    return jnp.minimum(jnp.maximum(result, -limit), limit).astype(kind)


def setup_inputs(seed: int = 0) -> dict:
    keys = jax.random.split(jax.random.key(seed), 10)
    return {
        "tokens": draw_tokens(jax.random.fold_in(keys[9], 71), 0),
        "gate_weight": centred(keys[1], (D, FF), D ** -0.5, 0.0625, ((0, 16), (1, 8))),
        "up_weight": centred(keys[2], (D, FF), D ** -0.5, 0.0625, ((0, 16), (1, 8))),
        "down_weight": centred(keys[3], (FF, D), FF ** -0.5, 0.046875, ((0, 8), (1, 16))),
        "head_weight": draw_head_weight(jax.random.fold_in(keys[9], 71), 0),
        "up_moment": centred(keys[5], (D, FF), 0.1, 0.6, ((0, 16), (1, 8)), jnp.float32),
        "up_curvature": jnp.clip(jnp.exp(math.log(0.2) - 4.6051702 * jax.random.uniform(keys[6], (D, FF), jnp.float32) ** level_of(keys[6], (D, FF), ((0, 16), (1, 8)), -0.2, 0.2)), 0.002, 0.2),
        "true_labels": with_ends(skewed_ids(keys[7], (TOKENS,), VOCAB, 2), jax.random.fold_in(keys[7], 3), 0, VOCAB - 1).astype(jnp.int32),
        "sampled_labels": with_ends(jax.random.randint(keys[8], (TOKENS,), 0, VOCAB), jax.random.fold_in(keys[8], 1), 0, VOCAB - 1).astype(jnp.int32),
    }


beta_one = 0.965
beta_two = 0.95
rho_scale = 0.05
eps_norm = 1e-05

def reference(tokens, gate_weight, up_weight, down_weight, head_weight, up_moment, up_curvature, true_labels, sampled_labels):
    gate_act = jnp.dot(tokens, gate_weight, preferred_element_type=jnp.float32)
    upper = jnp.dot(tokens, up_weight, preferred_element_type=jnp.float32)
    silu_gate = jax.nn.silu(gate_act)
    hidden = (silu_gate * upper).astype(jnp.bfloat16)
    branch = jnp.dot(hidden, down_weight, preferred_element_type=jnp.float32)
    summed = tokens.astype(jnp.float32) + branch
    inv_rms = lax.rsqrt(lax.optimization_barrier(jnp.mean(summed * summed, axis=1, keepdims=True)) + eps_norm)
    scaled = summed * inv_rms
    normed = scaled.astype(jnp.bfloat16)
    logits = jnp.dot(normed, head_weight, preferred_element_type=jnp.float32)
    row_top = lax.optimization_barrier(jnp.max(logits, axis=1, keepdims=True))
    exp_terms = jnp.exp(logits - row_top)
    probability = exp_terms / lax.optimization_barrier(jnp.sum(exp_terms, axis=1, keepdims=True))
    vocab_ids = jnp.arange(VOCAB, dtype=jnp.int32)
    cotangents = []
    for labels in (true_labels, sampled_labels):
        onehot = (labels[:, None] == vocab_ids[None, :]).astype(jnp.float32)
        dlogit = (probability - onehot).astype(jnp.bfloat16)
        dnormed = lax.dot_general(dlogit, head_weight, (((1,), (1,)), ((), ())), preferred_element_type=jnp.float32)
        inner_dot = lax.optimization_barrier(jnp.mean(dnormed * scaled, axis=1, keepdims=True))
        dsummed = (inv_rms * (dnormed - scaled * inner_dot)).astype(jnp.bfloat16)
        dhidden = lax.dot_general(dsummed, down_weight, (((1,), (1,)), ((), ())), preferred_element_type=jnp.float32)
        cotangents.append((dhidden * silu_gate).astype(jnp.bfloat16))
    block_count = 8
    block_width = D // block_count
    token_blocks = jnp.transpose(tokens.reshape(TOKENS, block_count, block_width), (1, 0, 2))

    def one_block(block_args):
        token_block, moment_block, curve_block = block_args
        grad_true = lax.dot_general(token_block, cotangents[0], (((0,), (0,)), ((), ())), preferred_element_type=jnp.float32)
        grad_sampled = lax.dot_general(token_block, cotangents[1], (((0,), (0,)), ((), ())), preferred_element_type=jnp.float32)
        new_moment = beta_one * moment_block + (1.0 - beta_one) * grad_true
        new_curvature = beta_two * curve_block + (1.0 - beta_two) * grad_sampled * grad_sampled
        update = jnp.clip(new_moment / (rho_scale * new_curvature), -1.0, 1.0)
        return (new_moment, new_curvature, update)
    results = lax.map(one_block, (token_blocks, up_moment.reshape(block_count, block_width, FF), up_curvature.reshape(block_count, block_width, FF)))
    return (results[0].reshape(D, FF), results[1].reshape(D, FF), results[2].reshape(D, FF))
```

```python
import jax
import jax.numpy as jnp
from jax import lax
from jax.experimental import pallas as pl
from jax.experimental.pallas import tpu as pltpu
from jax.sharding import Mesh, PartitionSpec as P

D = 8192
FF_HALF = 896
V_HALF = 1024
BLOCK = 64
CHIPS = 8
PAD = 128

beta_one = 0.965
beta_two = 0.95
rho_scale = 0.05
eps_norm = 1e-05

WIDTH_CHIPS = ("xl", "y")
UNIT_CHIPS = ("z", "xh")
f32 = jnp.float32
bf16 = jnp.bfloat16


def other_core(value):
    return lax.ppermute(value, "core", [(0, 1), (1, 0)])


def exchange(blocks, axes):
    return lax.all_to_all(blocks, axes, split_axis=0, concat_axis=0, tiled=True)


def to_all(block, axes):
    copies = jnp.broadcast_to(block[None], (CHIPS,) + block.shape)
    return exchange(copies, axes)


def half_of(array, half, size, axis):
    return lax.dynamic_slice_in_dim(array, half * size, size, axis)


def dot(left, right):
    return jnp.dot(left, right, preferred_element_type=f32)


def dot_rows(left, right):
    return lax.dot_general(left, right, (((1,), (1,)), ((), ())), preferred_element_type=f32)


def as_three(values):
    high = lax.reduce_precision(values, 8, 7)
    rest = values - high
    middle = lax.reduce_precision(rest, 8, 7)
    return jnp.concatenate([high, middle, rest - middle], axis=1).astype(bf16)


def from_three(parts, count):
    parts = parts.astype(f32)
    return parts[..., :count] + parts[..., count : 2 * count] + parts[..., 2 * count : 3 * count]


def step_kernel(core_ref, tokens_ref, own_true, own_sampled, far_true, far_sampled, moment_ref, curve_ref, new_moment, new_curve, update):
    def work(true_ref, sampled_ref):
        dims = (((0,), (0,)), ((), ()))
        token_block = tokens_ref[...]
        grad_true = lax.dot_general(token_block, true_ref[...], dims, preferred_element_type=f32)
        grad_sampled = lax.dot_general(token_block, sampled_ref[...], dims, preferred_element_type=f32)
        moment = beta_one * moment_ref[...] + (1.0 - beta_one) * grad_true
        curve = beta_two * curve_ref[...] + (1.0 - beta_two) * grad_sampled * grad_sampled
        new_moment[...] = moment
        new_curve[...] = curve
        update[...] = jnp.clip(moment / (rho_scale * curve), -1.0, 1.0)

    half = pl.program_id(0)

    @pl.when(half == 0)
    def _():
        work(own_true, own_sampled)

    @pl.when(half == 1)
    def _():
        work(far_true, far_sampled)


def sophia_step(core, tokens, cot_own, cot_far, moment, curve):
    wide = 128
    steps = FF_HALF // wide
    rows = tokens.shape[1]

    def place(half, step, core_ref):
        return (0, (half ^ core_ref[0]) * steps + step)

    def own(shift):
        return lambda half, step, core_ref: (0, shift + jnp.where(half == 0, step, steps - 1))

    def far(shift):
        return lambda half, step, core_ref: (0, shift + jnp.where(half == 1, step, 0))

    cot_block = (tokens.shape[0], wide)
    big = pl.BlockSpec((rows, wide), place)
    shape = jax.ShapeDtypeStruct(moment.shape, f32)
    return pl.pallas_call(
        step_kernel,
        out_shape=(shape, shape, shape),
        grid_spec=pltpu.PrefetchScalarGridSpec(
            num_scalar_prefetch=1,
            grid=(2, steps),
            in_specs=[
                pl.BlockSpec(tokens.shape, lambda half, step, core_ref: (0, 0)),
                pl.BlockSpec(cot_block, own(0)),
                pl.BlockSpec(cot_block, own(steps)),
                pl.BlockSpec(cot_block, far(0)),
                pl.BlockSpec(cot_block, far(steps)),
                big,
                big,
            ],
            out_specs=(big, big, big),
        ),
        compiler_params=pltpu.CompilerParams(vmem_limit_bytes=32 * 1024 * 1024),
        cost_estimate=pl.CostEstimate(flops=1900000000, bytes_accessed=24000000, transcendentals=0),
    )(core.reshape(1), tokens, cot_own, cot_own, cot_far, cot_far, moment, curve)


def on_device(
    tokens,
    gate_weight,
    up_weight,
    down_weight,
    head_weight,
    up_moment,
    up_curvature,
    true_labels,
    sampled_labels,
):
    core = lax.axis_index("core")
    far = 1 - core
    unit_chip = lax.axis_index(UNIT_CHIPS)
    count = tokens.shape[0]

    labels = jnp.stack([true_labels, sampled_labels], axis=0)
    far_labels = other_core(labels)
    labels = jnp.where(
        core == 0,
        jnp.concatenate([labels, far_labels], axis=1),
        jnp.concatenate([far_labels, labels], axis=1),
    )

    def gate_up(half):
        gate = dot(tokens, half_of(gate_weight, half, FF_HALF, 1))
        upper = dot(tokens, half_of(up_weight, half, FF_HALF, 1))
        return gate, upper

    far_gate, far_up = gate_up(far)
    sent = jnp.concatenate([far_gate.astype(bf16), far_up.astype(bf16)], axis=1)
    got = other_core(sent)
    own_gate, own_up = gate_up(core)
    both = jnp.concatenate([own_gate, own_up], axis=1) + got.astype(f32)
    both = exchange(both.astype(bf16).reshape(CHIPS, BLOCK, 2 * FF_HALF), WIDTH_CHIPS)
    both = jnp.sum(both.astype(f32), axis=0)
    gate_act = both[:, :FF_HALF]
    silu_gate = jax.nn.silu(gate_act)
    hidden = (silu_gate * both[:, FF_HALF:]).astype(bf16)

    hidden_own = to_all(hidden, WIDTH_CHIPS).reshape(count, FF_HALF)
    hidden_far = other_core(hidden_own)
    down_own = half_of(down_weight, core, FF_HALF, 0)
    down_far = half_of(down_weight, far, FF_HALF, 0)
    branch = dot(hidden_own, down_own) + dot(hidden_far, down_far)
    width = branch.shape[1]
    branch = exchange(branch.astype(bf16).reshape(CHIPS, BLOCK, width), UNIT_CHIPS)
    branch = jnp.sum(branch.astype(f32), axis=0)
    own_tokens = half_of(tokens, unit_chip, BLOCK, 0)
    summed = own_tokens.astype(f32) + branch
    rows = to_all(summed.astype(bf16), UNIT_CHIPS).reshape(count, width)
    wide_rows = rows.astype(f32)
    squares = jnp.broadcast_to(jnp.sum(wide_rows * wide_rows, axis=1, keepdims=True), (count, PAD))

    head_own = half_of(head_weight, core, V_HALF, 1)
    head_far = half_of(head_weight, far, V_HALF, 1)
    sent = jnp.concatenate([dot(rows, head_far), squares], axis=1)
    got = other_core(sent)
    raw = jnp.concatenate([dot(rows, head_own), squares], axis=1) + got
    raw = exchange(raw.reshape(CHIPS, BLOCK, V_HALF + PAD), WIDTH_CHIPS)
    raw = jnp.sum(raw, axis=0)
    inv_rms = lax.rsqrt(raw[:, V_HALF : V_HALF + 1] / D + eps_norm)
    logits = raw[:, :V_HALF] * inv_rms
    top = jnp.max(logits, axis=1, keepdims=True)
    exp_terms = jnp.exp(logits - top)
    exp_rounded = lax.reduce_precision(exp_terms, 8, 7)
    exp_short = exp_rounded.astype(bf16)
    total = jnp.sum(exp_terms, axis=1, keepdims=True)
    pull = jnp.sum(exp_rounded * logits, axis=1, keepdims=True)
    vocab_start = (unit_chip * 2 + core) * V_HALF
    vocab_ids = vocab_start + lax.broadcasted_iota(jnp.int32, (1, V_HALF), 1)
    stats = [top, inv_rms, total, pull]
    for which in range(2):
        hot = labels[which][:, None] == vocab_ids
        stats.append(jnp.sum(jnp.where(hot, logits, 0.0), axis=1, keepdims=True))
        stats.append(jnp.sum(jnp.where(hot, exp_terms - exp_rounded, 0.0), axis=1, keepdims=True))
    label_parts = labels.T.astype(f32)
    stats.append(label_parts)
    stats = jnp.concatenate(stats, axis=1)
    n_stats = stats.shape[1]
    stat_parts = as_three(stats)
    packed = jnp.concatenate(
        [exp_short, stat_parts, jnp.zeros((BLOCK, PAD - 3 * n_stats), bf16)], axis=1
    )

    packed_own = to_all(packed, WIDTH_CHIPS).reshape(count, V_HALF + PAD)
    packed_far = other_core(packed_own)
    exp_own, exp_far = packed_own[:, :V_HALF], packed_far[:, :V_HALF]
    stats_own = from_three(packed_own[:, V_HALF:], n_stats)
    stats_far = from_three(packed_far[:, V_HALF:], n_stats)
    pair_top = jnp.maximum(stats_own[:, 0:1], stats_far[:, 0:1])
    scale_own = jnp.exp(stats_own[:, 0:1] - pair_top)
    scale_far = jnp.exp(stats_far[:, 0:1] - pair_top)
    pulled = scale_own * dot_rows(exp_own, head_own) + scale_far * dot_rows(exp_far, head_far)
    all_labels = stats_own[:, 8:10].astype(jnp.int32)
    slice_ids = unit_chip * (2 * V_HALF) + lax.broadcasted_iota(jnp.int32, (1, 2 * V_HALF), 1)

    def label_rows(which):
        hot = (all_labels[:, which : which + 1] == slice_ids).astype(bf16)
        return dot_rows(hot, head_weight).astype(bf16)

    pair_stats = jnp.concatenate(
        [
            pair_top,
            stats_own[:, 1:2],
            scale_own * stats_own[:, 2:4] + scale_far * stats_far[:, 2:4],
            stats_own[:, 4:5] + stats_far[:, 4:5],
            scale_own * stats_own[:, 5:6] + scale_far * stats_far[:, 5:6],
            stats_own[:, 6:7] + stats_far[:, 6:7],
            scale_own * stats_own[:, 7:8] + scale_far * stats_far[:, 7:8],
        ],
        axis=1,
    )
    packed = jnp.concatenate(
        [
            pulled.astype(bf16),
            label_rows(0),
            label_rows(1),
            as_three(pair_stats),
            jnp.zeros((count, PAD - 24), bf16),
        ],
        axis=1,
    )
    packed = exchange(packed.reshape(CHIPS, BLOCK, 3 * width + PAD), UNIT_CHIPS)
    stats = from_three(packed[:, :, 3 * width :], 8)
    row_top = jnp.max(stats[:, :, 0:1], axis=0, keepdims=True)
    weight = jnp.exp(stats[:, :, 0:1] - row_top)
    weight = weight / jnp.sum(weight * stats[:, :, 2:3], axis=0, keepdims=True)
    pulled = jnp.sum(weight * packed[:, :, :width].astype(f32), axis=0)
    pull = jnp.sum(weight * stats[:, :, 3:4], axis=0)
    inv_rms = stats[0, :, 1:2]
    scaled = summed * inv_rms
    dsummed = []
    for which in range(2):
        label_logit = jnp.sum(stats[:, :, 4 + 2 * which : 5 + 2 * which], axis=0)
        rest = jnp.sum(weight * stats[:, :, 5 + 2 * which : 6 + 2 * which], axis=0)
        label_row = jnp.sum(
            packed[:, :, (1 + which) * width : (2 + which) * width].astype(f32), axis=0
        )
        dnormed = pulled - (1.0 - rest) * label_row
        mean = (pull - (1.0 - rest) * label_logit) / D
        dsummed.append((inv_rms * (dnormed - scaled * mean)).astype(bf16))
    dsummed = to_all(jnp.concatenate(dsummed, axis=1), UNIT_CHIPS).reshape(count, 2 * width)

    def back(half_rows):
        return [dot_rows(dsummed[:, k * width : (k + 1) * width], half_rows) for k in range(2)]

    sent = jnp.concatenate([part.astype(bf16) for part in back(down_far)], axis=1)
    got = other_core(sent)
    dhidden = jnp.concatenate(back(down_own), axis=1) + got.astype(f32)
    dhidden = exchange(dhidden.astype(bf16).reshape(CHIPS, BLOCK, 2 * FF_HALF), WIDTH_CHIPS)
    dhidden = jnp.sum(dhidden.astype(f32), axis=0)
    cot = (dhidden * jnp.concatenate([silu_gate, silu_gate], axis=1)).astype(bf16)
    cot_own = to_all(cot, WIDTH_CHIPS).reshape(count, 2 * FF_HALF)
    cot_far = other_core(cot_own)
    return sophia_step(core, tokens, cot_own, cot_far, up_moment, up_curvature)


def solution(mesh):
    fine = Mesh(mesh.devices.reshape(2, 4, 2, 4, 2), ("xl", "y", "core", "z", "xh"))
    dp = ("xl", "y", "core")
    tensor = ("z", "xh")
    both = P(dp, tensor)
    placed = (P(None, dp), both, both, P(tensor, dp), both, both, both, P(dp), P(dp))
    return jax.shard_map(
        on_device,
        mesh=fine,
        in_specs=placed,
        out_specs=(both, both, both),
        check_vma=False,
    )
```

```python
import jax
import jax.numpy as jnp
from jax import lax
from jax.experimental import pallas as pl
from jax.experimental.pallas import tpu as pltpu
from jax.sharding import Mesh, PartitionSpec as P

D = 8192
FF_HALF = 896
V_HALF = 1024
BLOCK = 64
CHIPS = 8
PAD = 128
N_STATS = 8
STEP = 16384.0
TINY = 1e-30

beta_one = 0.965
beta_two = 0.95
rho_scale = 0.05
eps_norm = 1e-05

WIDTH_CHIPS = ("xl", "y")
UNIT_CHIPS = ("z", "xh")
f32 = jnp.float32
bf16 = jnp.bfloat16
VMEM_LIMIT = 48 * 1024 * 1024


def other_core(value):
    return lax.ppermute(value, "core", [(0, 1), (1, 0)])


def exchange(blocks, axes):
    return lax.all_to_all(blocks, axes, split_axis=0, concat_axis=0, tiled=True)


def to_all(block, axes):
    copies = jnp.broadcast_to(block[None], (CHIPS,) + block.shape)
    return exchange(copies, axes)


def dot(left, right):
    return jnp.dot(left, right, preferred_element_type=f32)


def dot_rows(left, right):
    return lax.dot_general(left, right, (((1,), (1,)), ((), ())), preferred_element_type=f32)


def as_three(values):
    high = lax.reduce_precision(values, 8, 7)
    rest = values - high
    middle = lax.reduce_precision(rest, 8, 7)
    return jnp.concatenate([high, middle, rest - middle], axis=1).astype(bf16)


def from_three(parts, count):
    parts = parts.astype(f32)
    return parts[..., :count] + parts[..., count : 2 * count] + parts[..., 2 * count : 3 * count]


def whole(array):
    return pl.BlockSpec(array.shape, lambda step, half: (0,) * array.ndim)


def columns_of(array, count):
    return pl.BlockSpec((array.shape[0], count), lambda step, half: (0, half[0]))


def rows_of(array, count):
    return pl.BlockSpec((count, array.shape[1]), lambda step, half: (half[0], 0))


def on_core(kernel, half, operands, specs, shape, dtype, flops):
    size = sum(operand.size * operand.dtype.itemsize for operand in operands)
    return pl.pallas_call(
        kernel,
        out_shape=jax.ShapeDtypeStruct(shape, dtype),
        grid_spec=pltpu.PrefetchScalarGridSpec(
            num_scalar_prefetch=1,
            grid=(1,),
            in_specs=specs,
            out_specs=pl.BlockSpec(shape, lambda step, half: (0,) * len(shape)),
        ),
        compiler_params=pltpu.CompilerParams(vmem_limit_bytes=VMEM_LIMIT),
        cost_estimate=pl.CostEstimate(flops=flops, bytes_accessed=size, transcendentals=0),
    )(half.reshape(1), *operands)


def gate_up_far(half_ref, tokens, gate, up, out):
    out[:, :FF_HALF] = dot(tokens[...], gate[...]).astype(bf16)
    out[:, FF_HALF:] = dot(tokens[...], up[...]).astype(bf16)


def gate_up_own(half_ref, tokens, gate, up, got, labels, out):
    gate_sum = dot(tokens[...], gate[...]) + got[:, :FF_HALF].astype(f32)
    out[:, :FF_HALF] = gate_sum.astype(bf16)
    up_sum = dot(tokens[...], up[...]) + got[:, FF_HALF:].astype(f32)
    out[:, FF_HALF : 2 * FF_HALF] = up_sum.astype(bf16)
    for block in range(CHIPS):
        out[block * BLOCK : (block + 1) * BLOCK, 2 * FF_HALF :] = labels[...]


def squares_of(rows):
    wide = rows[...].astype(f32)
    return jnp.sum(wide * wide, axis=1, keepdims=True)


def logits_far(half_ref, rows, head, out):
    out[:, :V_HALF] = dot(rows[...], head[...])
    out[:, V_HALF:] = jnp.broadcast_to(squares_of(rows), (rows.shape[0], PAD))


def exponent_of(values):
    return jnp.ceil(jnp.log2(jnp.maximum(values, TINY)))


def logits_own(half_ref, rows, head, got, out):
    raw = dot(rows[...], head[...]) + got[:, :V_HALF]
    squares = squares_of(rows) + got[:, V_HALF : V_HALF + 1]
    level = exponent_of(jnp.max(jnp.abs(raw), axis=1, keepdims=True))
    out[:, :V_HALF] = jnp.round(raw * (STEP * jnp.exp2(-level))).astype(jnp.int32).astype(jnp.int16)
    square_level = exponent_of(squares)
    units = squares * (STEP * jnp.exp2(-square_level))
    high = jnp.floor(units)
    low = jnp.floor((units - high) * STEP)
    lane = lax.broadcasted_iota(jnp.int32, (rows.shape[0], PAD), 1)
    tail = jnp.where(lane == 0, level, jnp.where(lane == 1, high, jnp.where(lane == 2, low, square_level)))
    out[:, V_HALF:] = tail.astype(jnp.int32).astype(jnp.int16)


def pull_back(half_ref, own, far, head_own, head_far, out):
    count = own.shape[0]
    row = lax.broadcasted_iota(jnp.int32, (PAD, PAD), 0)
    lane = lax.broadcasted_iota(jnp.int32, (PAD, PAD), 1)
    gather = ((row % N_STATS == lane) & (row < 3 * N_STATS)).astype(f32).astype(bf16)
    stats_own = dot(own[:, V_HALF:], gather)
    stats_far = dot(far[:, V_HALF:], gather)
    top = jnp.maximum(stats_own[:, 0:1], stats_far[:, 0:1])
    scale_own = jnp.exp(stats_own[:, 0:1] - top)
    scale_far = jnp.exp(stats_far[:, 0:1] - top)
    pulled = scale_own * dot_rows(own[:, :V_HALF], head_own[...])
    pulled = pulled + scale_far * dot_rows(far[:, :V_HALF], head_far[...])
    width = pulled.shape[1]
    out[:, :width] = pulled.astype(bf16)
    lane = lax.broadcasted_iota(jnp.int32, (count, PAD), 1)
    is_sum = (lane == 2) | (lane == 3) | (lane == 5) | (lane == 7)
    both = jnp.where(is_sum, scale_own * stats_own + scale_far * stats_far, stats_own + stats_far)
    both = jnp.where(lane == 0, top, jnp.where(lane == 1, stats_own, both))
    both = jnp.where(lane < N_STATS, both, 0.0)
    high = both.astype(bf16)
    rest = both - high.astype(f32)
    middle = rest.astype(bf16)
    low = (rest - middle.astype(f32)).astype(bf16)
    row = lax.broadcasted_iota(jnp.int32, (PAD, PAD), 0)
    lane = lax.broadcasted_iota(jnp.int32, (PAD, PAD), 1)
    by_one = (lane == row + N_STATS).astype(f32).astype(bf16)
    by_two = (lane == row + 2 * N_STATS).astype(f32).astype(bf16)
    out[:, width:] = (high.astype(f32) + dot(middle, by_one) + dot(low, by_two)).astype(bf16)


def back_far(half_ref, dsummed, down, out):
    width = down.shape[1]
    for which in range(2):
        part = dot_rows(dsummed[:, which * width : (which + 1) * width], down[...])
        out[:, which * FF_HALF : (which + 1) * FF_HALF] = part.astype(bf16)


def back_own(half_ref, dsummed, down, got, out):
    width = down.shape[1]
    for which in range(2):
        place = slice(which * FF_HALF, (which + 1) * FF_HALF)
        part = dot_rows(dsummed[:, which * width : (which + 1) * width], down[...])
        out[:, place] = (part + got[:, place].astype(f32)).astype(bf16)


def step_kernel(half_ref, turned, cot_true, cot_sampled, moment_ref, curve_ref, *rest):
    new_moment, new_curve, update = rest[-3:]
    grad_true = dot(turned[...], cot_true[...])
    grad_sampled = dot(turned[...], cot_sampled[...])
    moment = beta_one * moment_ref[...] + (1.0 - beta_one) * grad_true
    curve = beta_two * curve_ref[...] + (1.0 - beta_two) * grad_sampled * grad_sampled
    new_moment[...] = moment
    new_curve[...] = curve
    update[...] = jnp.clip(moment / (rho_scale * curve), -1.0, 1.0)


def sophia_half(half, turned, cot, moment, curve, done):
    wide = 128
    steps = FF_HALF // wide
    rows, count = turned.shape
    big = pl.BlockSpec((rows, wide), lambda step, half: (0, half[0] * steps + step))
    shape = jax.ShapeDtypeStruct(moment.shape, f32)
    kept = [pl.BlockSpec(memory_space=pl.ANY) for _ in done]
    return pl.pallas_call(
        step_kernel,
        out_shape=(shape, shape, shape),
        grid_spec=pltpu.PrefetchScalarGridSpec(
            num_scalar_prefetch=1,
            grid=(steps,),
            in_specs=[
                pl.BlockSpec(turned.shape, lambda step, half: (0, 0)),
                pl.BlockSpec((count, wide), lambda step, half: (0, step)),
                pl.BlockSpec((count, wide), lambda step, half: (0, steps + step)),
                big,
                big,
            ]
            + kept,
            out_specs=(big, big, big),
        ),
        input_output_aliases={6 + which: which for which in range(len(done))},
        compiler_params=pltpu.CompilerParams(vmem_limit_bytes=VMEM_LIMIT),
        cost_estimate=pl.CostEstimate(flops=950000000, bytes_accessed=11000000, transcendentals=0),
    )(half.reshape(1), turned, cot, cot, moment, curve, *done)


def own_part(array, index, axis):
    keep = lax.dynamic_index_in_dim(array, index, axis, keepdims=False)
    send = lax.dynamic_index_in_dim(array, 1 - index, axis, keepdims=False)
    return keep, send


def label_rows(labels, head_weight, unit_chip):
    ids = unit_chip * (2 * V_HALF) + lax.broadcasted_iota(jnp.int32, (1, 2 * V_HALF), 1)
    parts = []
    for which in range(2):
        hot = (labels[:, which : which + 1] == ids).astype(bf16)
        parts.append(dot_rows(hot, head_weight).astype(bf16))
    rows = jnp.concatenate(parts, axis=1).reshape(2, 2, 2, BLOCK, -1)
    z = lax.axis_index("z")
    keep, send = own_part(rows, z % 2, 1)
    rows = keep + lax.ppermute(send, "z", [(0, 1), (1, 0), (2, 3), (3, 2)])
    keep, send = own_part(rows, z // 2, 0)
    rows = keep + lax.ppermute(send, "z", [(0, 2), (2, 0), (1, 3), (3, 1)])
    keep, send = own_part(rows, lax.axis_index("xh"), 0)
    return keep + lax.ppermute(send, "xh", [(0, 1), (1, 0)])


def on_device(
    tokens,
    gate_weight,
    up_weight,
    down_weight,
    head_weight,
    up_moment,
    up_curvature,
    true_labels,
    sampled_labels,
):
    core = lax.axis_index("core").astype(jnp.int32)
    far = 1 - core
    unit_chip = lax.axis_index(UNIT_CHIPS)
    count, width = tokens.shape

    labels = jnp.stack([true_labels, sampled_labels], axis=1)
    far_labels = other_core(labels)
    labels = jnp.where(
        core == 0,
        jnp.concatenate([labels, far_labels], axis=0),
        jnp.concatenate([far_labels, labels], axis=0),
    )
    digits = jnp.concatenate([labels // PAD, labels % PAD], axis=1).astype(bf16)
    digits = jnp.pad(digits, ((0, 0), (0, PAD - 4)))

    w_specs = [whole(tokens), columns_of(gate_weight, FF_HALF), columns_of(up_weight, FF_HALF)]
    gate_up_flops = 4 * count * width * FF_HALF
    sent = on_core(
        gate_up_far, far, (tokens, gate_weight, up_weight), w_specs, (count, 2 * FF_HALF), bf16, gate_up_flops
    )
    got = other_core(sent)
    both = on_core(
        gate_up_own,
        core,
        (tokens, gate_weight, up_weight, got, digits),
        w_specs + [whole(got), whole(digits)],
        (count, 2 * FF_HALF + PAD),
        bf16,
        gate_up_flops,
    )
    both = exchange(both.reshape(CHIPS, BLOCK, 2 * FF_HALF + PAD), WIDTH_CHIPS)
    digits = both[:, :, 2 * FF_HALF : 2 * FF_HALF + 4].reshape(count, 4).astype(jnp.int32)
    all_labels = digits[:, :2] * PAD + digits[:, 2:]
    both = jnp.sum(both[:, :, : 2 * FF_HALF].astype(f32), axis=0)
    silu_gate = jax.nn.silu(both[:, :FF_HALF])
    hidden = (silu_gate * both[:, FF_HALF:]).astype(bf16)

    hidden_own = to_all(hidden, WIDTH_CHIPS).reshape(count, FF_HALF)
    hidden_far = other_core(hidden_own)
    label_row = label_rows(all_labels, head_weight, unit_chip).astype(f32)
    down_own = lax.dynamic_slice_in_dim(down_weight, core * FF_HALF, FF_HALF, 0)
    down_far = lax.dynamic_slice_in_dim(down_weight, far * FF_HALF, FF_HALF, 0)
    branch = dot(hidden_own, down_own) + dot(hidden_far, down_far)
    branch = exchange(branch.astype(bf16).reshape(CHIPS, BLOCK, width), UNIT_CHIPS)
    branch = jnp.sum(branch.astype(f32), axis=0)
    own_tokens = lax.dynamic_slice_in_dim(tokens, unit_chip * BLOCK, BLOCK, 0)
    summed = own_tokens.astype(f32) + branch
    rows = to_all(summed.astype(bf16), UNIT_CHIPS).reshape(count, width)

    logit_flops = 2 * count * width * V_HALF
    head_spec = columns_of(head_weight, V_HALF)
    sent = on_core(
        logits_far, far, (rows, head_weight), [whole(rows), head_spec], (count, V_HALF + PAD), f32, logit_flops
    )
    got = other_core(sent)
    raw = on_core(
        logits_own,
        core,
        (rows, head_weight, got),
        [whole(rows), head_spec, whole(got)],
        (count, V_HALF + PAD),
        jnp.int16,
        logit_flops,
    )
    raw = exchange(raw.reshape(CHIPS, BLOCK, V_HALF + PAD), WIDTH_CHIPS).astype(f32)
    tail = raw[:, :, V_HALF : V_HALF + 4]
    raw = jnp.sum(raw[:, :, :V_HALF] * (jnp.exp2(tail[:, :, 0:1]) / STEP), axis=0)
    squares = (tail[:, :, 1:2] + tail[:, :, 2:3] / STEP) * (jnp.exp2(tail[:, :, 3:4]) / STEP)
    inv_rms = lax.rsqrt(jnp.sum(squares, axis=0) / D + eps_norm)
    logits = raw * inv_rms
    top = jnp.max(logits, axis=1, keepdims=True)
    exp_terms = jnp.exp(logits - top)
    exp_rounded = lax.reduce_precision(exp_terms, 8, 7)
    total = jnp.sum(exp_terms, axis=1, keepdims=True)
    pull = jnp.sum(exp_rounded * logits, axis=1, keepdims=True)
    vocab_start = (unit_chip * 2 + core) * V_HALF
    vocab_ids = vocab_start + lax.broadcasted_iota(jnp.int32, (1, V_HALF), 1)
    stats = [top, inv_rms, total, pull]
    for which in range(2):
        hot = labels[:, which : which + 1] == vocab_ids
        stats.append(jnp.sum(jnp.where(hot, logits, 0.0), axis=1, keepdims=True))
        stats.append(jnp.sum(jnp.where(hot, exp_terms - exp_rounded, 0.0), axis=1, keepdims=True))
    stat_parts = as_three(jnp.concatenate(stats, axis=1))
    packed = jnp.concatenate(
        [exp_rounded.astype(bf16), stat_parts, jnp.zeros((BLOCK, PAD - 3 * N_STATS), bf16)], axis=1
    )

    packed_own = to_all(packed, WIDTH_CHIPS).reshape(count, V_HALF + PAD)
    packed_far = other_core(packed_own)
    packed = pl.pallas_call(
        pull_back,
        out_shape=jax.ShapeDtypeStruct((count, width + PAD), bf16),
        grid_spec=pltpu.PrefetchScalarGridSpec(
            num_scalar_prefetch=1,
            grid=(1,),
            in_specs=[
                whole(packed_own),
                whole(packed_far),
                pl.BlockSpec((width, V_HALF), lambda step, half: (0, half[0])),
                pl.BlockSpec((width, V_HALF), lambda step, half: (0, 1 - half[0])),
            ],
            out_specs=pl.BlockSpec((count, width + PAD), lambda step, half: (0, 0)),
        ),
        compiler_params=pltpu.CompilerParams(vmem_limit_bytes=VMEM_LIMIT),
        cost_estimate=pl.CostEstimate(flops=2 * logit_flops, bytes_accessed=5000000, transcendentals=0),
    )(core.reshape(1), packed_own, packed_far, head_weight, head_weight)
    packed = exchange(packed.reshape(CHIPS, BLOCK, width + PAD), UNIT_CHIPS)
    stats = from_three(packed[:, :, width:], N_STATS)
    row_top = jnp.max(stats[:, :, 0:1], axis=0, keepdims=True)
    weight = jnp.exp(stats[:, :, 0:1] - row_top)
    weight = weight / jnp.sum(weight * stats[:, :, 2:3], axis=0, keepdims=True)
    pulled = jnp.sum(weight * packed[:, :, :width].astype(f32), axis=0)
    pull = jnp.sum(weight * stats[:, :, 3:4], axis=0)
    inv_rms = stats[0, :, 1:2]
    scaled = summed * inv_rms
    dsummed = []
    for which in range(2):
        label_logit = jnp.sum(stats[:, :, 4 + 2 * which : 5 + 2 * which], axis=0)
        rest = jnp.sum(weight * stats[:, :, 5 + 2 * which : 6 + 2 * which], axis=0)
        dnormed = pulled - (1.0 - rest) * label_row[:, which * width : (which + 1) * width]
        mean = (pull - (1.0 - rest) * label_logit) / D
        dsummed.append((inv_rms * (dnormed - scaled * mean)).astype(bf16))
    dsummed = to_all(jnp.concatenate(dsummed, axis=1), UNIT_CHIPS).reshape(count, 2 * width)

    down_spec = rows_of(down_weight, FF_HALF)
    sent = on_core(
        back_far, far, (dsummed, down_weight), [whole(dsummed), down_spec], (count, 2 * FF_HALF), bf16, gate_up_flops
    )
    got = other_core(sent)
    dhidden = on_core(
        back_own,
        core,
        (dsummed, down_weight, got),
        [whole(dsummed), down_spec, whole(got)],
        (count, 2 * FF_HALF),
        bf16,
        gate_up_flops,
    )
    dhidden = exchange(dhidden.reshape(CHIPS, BLOCK, 2 * FF_HALF), WIDTH_CHIPS)
    dhidden = jnp.sum(dhidden.astype(f32), axis=0)
    cot = (dhidden * jnp.concatenate([silu_gate, silu_gate], axis=1)).astype(bf16)
    cot_own = to_all(cot, WIDTH_CHIPS).reshape(count, 2 * FF_HALF)
    cot_far = other_core(cot_own)
    turned = tokens.T
    done = sophia_half(core, turned, cot_own, up_moment, up_curvature, ())
    return tuple(sophia_half(far, turned, cot_far, up_moment, up_curvature, done))


def solution(mesh):
    fine = Mesh(mesh.devices.reshape(2, 4, 2, 4, 2), ("xl", "y", "core", "z", "xh"))
    dp = ("xl", "y", "core")
    tensor = ("z", "xh")
    both = P(dp, tensor)
    placed = (P(None, dp), both, both, P(tensor, dp), both, both, both, P(dp), P(dp))
    return jax.shard_map(
        on_device,
        mesh=fine,
        in_specs=placed,
        out_specs=(both, both, both),
        check_vma=False,
    )
```

```python
import jax
import jax.numpy as jnp
from jax import lax
from jax.experimental import pallas as pl
from jax.experimental.pallas import tpu as pltpu
from jax.sharding import Mesh, PartitionSpec as P

D = 8192
FF_HALF = 896
V_HALF = 1024
BLOCK = 64
CHIPS = 8
PAD = 128
N_STATS = 8
STEP = 16384.0
TINY = 1e-30

beta_one = 0.965
beta_two = 0.95
rho_scale = 0.05
eps_norm = 1e-05

WIDTH_CHIPS = ("xl", "y")
UNIT_CHIPS = ("z", "xh")
f32 = jnp.float32
bf16 = jnp.bfloat16
VMEM_LIMIT = 48 * 1024 * 1024
FIRST_LIMIT = 60 * 1024 * 1024


def other_core(value):
    return lax.ppermute(value, "core", [(0, 1), (1, 0)])


def exchange(blocks, axes):
    return lax.all_to_all(blocks, axes, split_axis=0, concat_axis=0, tiled=True)


def to_all(block, axes):
    copies = jnp.broadcast_to(block[None], (CHIPS,) + block.shape)
    return exchange(copies, axes)


def together(*values):
    return lax.optimization_barrier(values)


def dot(left, right):
    return jnp.dot(left, right, preferred_element_type=f32)


def dot_rows(left, right):
    return lax.dot_general(left, right, (((1,), (1,)), ((), ())), preferred_element_type=f32)


def from_three(parts, count):
    parts = parts.astype(f32)
    return parts[..., :count] + parts[..., count : 2 * count] + parts[..., 2 * count : 3 * count]


def whole(array):
    return pl.BlockSpec(array.shape, lambda step, half: (0,) * array.ndim)


def columns_of(array, count):
    return pl.BlockSpec((array.shape[0], count), lambda step, half: (0, half[0]))


def rows_of(array, count):
    return pl.BlockSpec((count, array.shape[1]), lambda step, half: (half[0], 0))


def on_core(kernel, half, operands, specs, outs, flops, limit=VMEM_LIMIT):
    size = sum(operand.size * operand.dtype.itemsize for operand in operands)
    results = pl.pallas_call(
        kernel,
        out_shape=tuple(jax.ShapeDtypeStruct(shape, dtype) for shape, dtype in outs),
        grid_spec=pltpu.PrefetchScalarGridSpec(
            num_scalar_prefetch=1,
            grid=(1,),
            in_specs=specs,
            out_specs=tuple(whole(jax.ShapeDtypeStruct(shape, dtype)) for shape, dtype in outs),
        ),
        compiler_params=pltpu.CompilerParams(vmem_limit_bytes=limit),
        cost_estimate=pl.CostEstimate(flops=flops, bytes_accessed=size, transcendentals=0),
    )(half.reshape(1), *operands)
    return results if len(outs) > 1 else results[0]


def gate_up_far(half_ref, tokens, gate, up, out):
    out[:, :FF_HALF] = dot(tokens[...], gate[...]).astype(bf16)
    out[:, FF_HALF:] = dot(tokens[...], up[...]).astype(bf16)


def gate_up_own(half_ref, tokens, gate, up, got, labels, out):
    gate_sum = dot(tokens[...], gate[...]) + got[:, :FF_HALF].astype(f32)
    out[:, :FF_HALF] = gate_sum.astype(bf16)
    up_sum = dot(tokens[...], up[...]) + got[:, FF_HALF:].astype(f32)
    out[:, FF_HALF : 2 * FF_HALF] = up_sum.astype(bf16)
    for block in range(CHIPS):
        out[block * BLOCK : (block + 1) * BLOCK, 2 * FF_HALF :] = labels[...]


def hidden_kernel(half_ref, both, hidden, silu_out):
    gate = jnp.zeros((BLOCK, FF_HALF), f32)
    upper = jnp.zeros((BLOCK, FF_HALF), f32)
    for chip in range(CHIPS):
        gate = gate + both[chip, :, :FF_HALF].astype(f32)
        upper = upper + both[chip, :, FF_HALF : 2 * FF_HALF].astype(f32)
    silu_gate = gate / (1.0 + jnp.exp(-gate))
    silu_out[...] = silu_gate
    rounded = (silu_gate * upper).astype(bf16)
    for chip in range(CHIPS):
        hidden[chip] = rounded


def squares_of(rows):
    wide = rows[...].astype(f32)
    return jnp.sum(wide * wide, axis=1, keepdims=True)


def exponent_of(values):
    return jnp.ceil(jnp.log2(jnp.maximum(values, TINY)))


def logits_kernel(half_ref, rows, far_rows, head, head_got, out):
    raw = dot(rows[...], head[...]) + dot(far_rows[...], head_got[...])
    squares = squares_of(rows) + squares_of(far_rows)
    level = exponent_of(jnp.max(jnp.abs(raw), axis=1, keepdims=True))
    out[:, :V_HALF] = jnp.round(raw * (STEP * jnp.exp2(-level))).astype(jnp.int32).astype(jnp.int16)
    square_level = exponent_of(squares)
    units = squares * (STEP * jnp.exp2(-square_level))
    high = jnp.floor(units)
    low = jnp.floor((units - high) * STEP)
    lane = lax.broadcasted_iota(jnp.int32, (rows.shape[0], PAD), 1)
    tail = jnp.where(lane == 0, level, jnp.where(lane == 1, high, jnp.where(lane == 2, low, square_level)))
    out[:, V_HALF:] = tail.astype(jnp.int32).astype(jnp.int16)


def pack_three(values):
    lane = lax.broadcasted_iota(jnp.int32, values.shape, 1)
    values = jnp.where(lane < N_STATS, values, 0.0)
    high = values.astype(bf16)
    rest = values - high.astype(f32)
    middle = rest.astype(bf16)
    low = (rest - middle.astype(f32)).astype(bf16)
    row = lax.broadcasted_iota(jnp.int32, (PAD, PAD), 0)
    lane = lax.broadcasted_iota(jnp.int32, (PAD, PAD), 1)
    by_one = (lane == row + N_STATS).astype(f32).astype(bf16)
    by_two = (lane == row + 2 * N_STATS).astype(f32).astype(bf16)
    return (high.astype(f32) + dot(middle, by_one) + dot(low, by_two)).astype(bf16)


def softmax_kernel(start_ref, raw, labels, out):
    total = jnp.zeros((BLOCK, V_HALF), f32)
    squares = jnp.zeros((BLOCK, 1), f32)
    for chip in range(CHIPS):
        tail = raw[chip, :, V_HALF:].astype(jnp.int32).astype(f32)
        scale = jnp.exp2(tail[:, 0:1]) / STEP
        total = total + raw[chip, :, :V_HALF].astype(jnp.int32).astype(f32) * scale
        square_scale = jnp.exp2(tail[:, 3:4]) / STEP
        squares = squares + (tail[:, 1:2] + tail[:, 2:3] / STEP) * square_scale
    inv_rms = lax.rsqrt(squares / D + eps_norm)
    logits = total * inv_rms
    top = jnp.max(logits, axis=1, keepdims=True)
    exp_terms = jnp.exp(logits - top)
    short = exp_terms.astype(bf16)
    rounded = short.astype(f32)
    ids = start_ref[0] + lax.broadcasted_iota(jnp.int32, (BLOCK, V_HALF), 1)
    stats = [
        top,
        inv_rms,
        jnp.sum(exp_terms, axis=1, keepdims=True),
        jnp.sum(rounded * logits, axis=1, keepdims=True),
    ]
    for which in range(2):
        hot = labels[:, which : which + 1] == ids
        stats.append(jnp.sum(jnp.where(hot, logits, 0.0), axis=1, keepdims=True))
        stats.append(jnp.sum(jnp.where(hot, exp_terms - rounded, 0.0), axis=1, keepdims=True))
    lane = lax.broadcasted_iota(jnp.int32, (BLOCK, PAD), 1)
    table = jnp.zeros((BLOCK, PAD), f32)
    for place, value in enumerate(stats):
        table = jnp.where(lane == place, value, table)
    packed = pack_three(table)
    for chip in range(CHIPS):
        out[chip, :, :V_HALF] = short
        out[chip, :, V_HALF:] = packed


def pull_back(half_ref, own, far, head_own, head_far, out):
    count = own.shape[0]
    row = lax.broadcasted_iota(jnp.int32, (PAD, PAD), 0)
    lane = lax.broadcasted_iota(jnp.int32, (PAD, PAD), 1)
    gather = ((row % N_STATS == lane) & (row < 3 * N_STATS)).astype(f32).astype(bf16)
    stats_own = dot(own[:, V_HALF:], gather)
    stats_far = dot(far[:, V_HALF:], gather)
    top = jnp.maximum(stats_own[:, 0:1], stats_far[:, 0:1])
    scale_own = jnp.exp(stats_own[:, 0:1] - top)
    scale_far = jnp.exp(stats_far[:, 0:1] - top)
    pulled = scale_own * dot_rows(own[:, :V_HALF], head_own[...])
    pulled = pulled + scale_far * dot_rows(far[:, :V_HALF], head_far[...])
    width = pulled.shape[1]
    out[:, :width] = pulled.astype(bf16)
    lane = lax.broadcasted_iota(jnp.int32, (count, PAD), 1)
    is_sum = (lane == 2) | (lane == 3) | (lane == 5) | (lane == 7)
    both = jnp.where(is_sum, scale_own * stats_own + scale_far * stats_far, stats_own + stats_far)
    both = jnp.where(lane == 0, top, jnp.where(lane == 1, stats_own, both))
    out[:, width:] = pack_three(both)


def back_kernel(half_ref, dsummed, far_dsummed, down, down_got, out):
    width = down.shape[1]
    for which in range(2):
        place = slice(which * width, (which + 1) * width)
        part = dot_rows(dsummed[:, place], down[...]) + dot_rows(far_dsummed[:, place], down_got[...])
        out[:, which * FF_HALF : (which + 1) * FF_HALF] = part.astype(bf16)


def step_kernel(half_ref, turned, cot, moment_ref, curve_ref, *rest):
    new_moment, new_curve, update = rest[-3:]
    grad_true = dot(turned[...], cot[:, :FF_HALF])
    grad_sampled = dot(turned[...], cot[:, FF_HALF:])
    moment = beta_one * moment_ref[...] + (1.0 - beta_one) * grad_true
    curve = beta_two * curve_ref[...] + (1.0 - beta_two) * grad_sampled * grad_sampled
    new_moment[...] = moment
    new_curve[...] = curve
    update[...] = jnp.clip(moment / (rho_scale * curve), -1.0, 1.0)


def sophia_half(half, turned, cot, moment, curve, done):
    tall = 128
    rows, count = turned.shape
    big = pl.BlockSpec((tall, FF_HALF), lambda step, half: (step, half[0]))
    shape = jax.ShapeDtypeStruct(moment.shape, f32)
    kept = [pl.BlockSpec(memory_space=pl.ANY) for _ in done]
    return pl.pallas_call(
        step_kernel,
        out_shape=(shape, shape, shape),
        grid_spec=pltpu.PrefetchScalarGridSpec(
            num_scalar_prefetch=1,
            grid=(rows // tall,),
            in_specs=[
                pl.BlockSpec((tall, count), lambda step, half: (step, 0)),
                whole(cot),
                big,
                big,
            ]
            + kept,
            out_specs=(big, big, big),
        ),
        input_output_aliases={5 + which: which for which in range(len(done))},
        compiler_params=pltpu.CompilerParams(vmem_limit_bytes=VMEM_LIMIT),
        cost_estimate=pl.CostEstimate(flops=950000000, bytes_accessed=11000000, transcendentals=0),
    )(half.reshape(1), turned, cot, moment, curve, *done)


def own_part(array, index, axis):
    keep = lax.dynamic_index_in_dim(array, index, axis, keepdims=False)
    send = lax.dynamic_index_in_dim(array, 1 - index, axis, keepdims=False)
    return keep, send


def label_rows(labels, head_weight, unit_chip):
    ids = unit_chip * (2 * V_HALF) + lax.broadcasted_iota(jnp.int32, (1, 2 * V_HALF), 1)
    parts = []
    for which in range(2):
        hot = (labels[:, which : which + 1] == ids).astype(bf16)
        parts.append(dot_rows(hot, head_weight).astype(bf16))
    rows = jnp.concatenate(parts, axis=1).reshape(2, 2, 2, BLOCK, -1)
    keep, send = own_part(rows, lax.axis_index("z") % 2, 1)
    return keep + lax.ppermute(send, "z", [(0, 1), (1, 0), (2, 3), (3, 2)])


def own_label_rows(rows):
    keep, send = own_part(rows, lax.axis_index("z") // 2, 0)
    rows = keep + lax.ppermute(send, "z", [(0, 2), (2, 0), (1, 3), (3, 1)])
    keep, send = own_part(rows, lax.axis_index("xh"), 0)
    return keep + lax.ppermute(send, "xh", [(0, 1), (1, 0)])


def on_device(
    tokens,
    gate_weight,
    up_weight,
    down_weight,
    head_weight,
    up_moment,
    up_curvature,
    true_labels,
    sampled_labels,
):
    core = lax.axis_index("core").astype(jnp.int32)
    far = 1 - core
    unit_chip = lax.axis_index(UNIT_CHIPS)
    count, width = tokens.shape

    labels = jnp.stack([true_labels, sampled_labels], axis=1)
    far_labels = other_core(labels)
    labels = jnp.where(
        core == 0,
        jnp.concatenate([labels, far_labels], axis=0),
        jnp.concatenate([far_labels, labels], axis=0),
    )
    digits = jnp.concatenate([labels // PAD, labels % PAD], axis=1).astype(bf16)
    digits = jnp.pad(digits, ((0, 0), (0, PAD - 4)))

    w_specs = [whole(tokens), columns_of(gate_weight, FF_HALF), columns_of(up_weight, FF_HALF)]
    gate_up_flops = 4 * count * width * FF_HALF
    sent = on_core(
        gate_up_far,
        far,
        (tokens, gate_weight, up_weight),
        w_specs,
        [((count, 2 * FF_HALF), bf16)],
        gate_up_flops,
        FIRST_LIMIT,
    )
    got = other_core(sent)
    both = on_core(
        gate_up_own,
        core,
        (tokens, gate_weight, up_weight, got, digits),
        w_specs + [whole(got), whole(digits)],
        [((count, 2 * FF_HALF + PAD), bf16)],
        gate_up_flops,
        FIRST_LIMIT,
    )
    head_send = lax.dynamic_slice_in_dim(head_weight, far * V_HALF, V_HALF, 1)
    down_send = lax.dynamic_slice_in_dim(down_weight, far * FF_HALF, FF_HALF, 0)
    both, head_send, down_send = together(both, head_send, down_send)
    both, head_got, down_got = together(
        exchange(both.reshape(CHIPS, BLOCK, 2 * FF_HALF + PAD), WIDTH_CHIPS),
        other_core(head_send),
        other_core(down_send),
    )
    hidden, silu_gate = on_core(
        hidden_kernel,
        core,
        (both,),
        [whole(both)],
        [((CHIPS, BLOCK, FF_HALF), bf16), ((BLOCK, FF_HALF), f32)],
        1000000,
    )
    digits = both[:, :, 2 * FF_HALF : 2 * FF_HALF + 4].reshape(count, 4)

    hidden, digits = together(hidden, digits)
    digits = digits.astype(jnp.int32)
    all_labels = digits[:, :2] * PAD + digits[:, 2:]
    hidden_own, label_row = together(
        exchange(hidden, WIDTH_CHIPS), label_rows(all_labels, head_weight, unit_chip)
    )
    hidden_own = hidden_own.reshape(count, FF_HALF)
    hidden_far = other_core(hidden_own)
    down_own = lax.dynamic_slice_in_dim(down_weight, core * FF_HALF, FF_HALF, 0)
    down_far = lax.dynamic_slice_in_dim(down_weight, far * FF_HALF, FF_HALF, 0)
    branch = dot(hidden_own, down_own) + dot(hidden_far, down_far)
    branch = exchange(branch.astype(bf16).reshape(CHIPS, BLOCK, width), UNIT_CHIPS)
    branch = jnp.sum(branch.astype(f32), axis=0)
    own_tokens = lax.dynamic_slice_in_dim(tokens, unit_chip * BLOCK, BLOCK, 0)
    summed = own_tokens.astype(f32) + branch
    rows = to_all(summed.astype(bf16), UNIT_CHIPS).reshape(count, width)

    far_rows = other_core(rows)
    logit_flops = 4 * count * width * V_HALF
    raw = on_core(
        logits_kernel,
        core,
        (rows, far_rows, head_weight, head_got),
        [whole(rows), whole(far_rows), columns_of(head_weight, V_HALF), whole(head_got)],
        [((count, V_HALF + PAD), jnp.int16)],
        logit_flops,
    )
    raw, label_row = together(raw, label_row)
    raw, label_row = together(
        exchange(raw.reshape(CHIPS, BLOCK, V_HALF + PAD), WIDTH_CHIPS), own_label_rows(label_row)
    )
    label_row = label_row.astype(f32)
    vocab_start = ((unit_chip * 2 + core) * V_HALF).astype(jnp.int32)
    packed = on_core(
        softmax_kernel,
        vocab_start,
        (raw, labels),
        [whole(raw), whole(labels)],
        [((CHIPS, BLOCK, V_HALF + PAD), bf16)],
        1000000,
    )
    packed, token_rows = together(packed, tokens)
    packed_own, turned = together(exchange(packed, WIDTH_CHIPS), token_rows.T)
    packed_own = packed_own.reshape(count, V_HALF + PAD)
    packed_far = other_core(packed_own)
    packed = on_core(
        pull_back,
        core,
        (packed_own, packed_far, head_weight, head_weight),
        [
            whole(packed_own),
            whole(packed_far),
            pl.BlockSpec((width, V_HALF), lambda step, half: (0, half[0])),
            pl.BlockSpec((width, V_HALF), lambda step, half: (0, 1 - half[0])),
        ],
        [((count, width + PAD), bf16)],
        logit_flops,
    )
    packed = exchange(packed.reshape(CHIPS, BLOCK, width + PAD), UNIT_CHIPS)
    stats = from_three(packed[:, :, width:], N_STATS)
    row_top = jnp.max(stats[:, :, 0:1], axis=0, keepdims=True)
    weight = jnp.exp(stats[:, :, 0:1] - row_top)
    weight = weight / jnp.sum(weight * stats[:, :, 2:3], axis=0, keepdims=True)
    pulled = jnp.sum(weight * packed[:, :, :width].astype(f32), axis=0)
    pull = jnp.sum(weight * stats[:, :, 3:4], axis=0)
    inv_rms = stats[0, :, 1:2]
    scaled = summed * inv_rms
    dsummed = []
    for which in range(2):
        label_logit = jnp.sum(stats[:, :, 4 + 2 * which : 5 + 2 * which], axis=0)
        rest = jnp.sum(weight * stats[:, :, 5 + 2 * which : 6 + 2 * which], axis=0)
        dnormed = pulled - (1.0 - rest) * label_row[:, which * width : (which + 1) * width]
        mean = (pull - (1.0 - rest) * label_logit) / D
        dsummed.append((inv_rms * (dnormed - scaled * mean)).astype(bf16))
    dsummed = to_all(jnp.concatenate(dsummed, axis=1), UNIT_CHIPS).reshape(count, 2 * width)

    far_dsummed = other_core(dsummed)
    dhidden = on_core(
        back_kernel,
        core,
        (dsummed, far_dsummed, down_weight, down_got),
        [whole(dsummed), whole(far_dsummed), rows_of(down_weight, FF_HALF), whole(down_got)],
        [((count, 2 * FF_HALF), bf16)],
        2 * gate_up_flops,
    )
    dhidden = exchange(dhidden.reshape(CHIPS, BLOCK, 2 * FF_HALF), WIDTH_CHIPS)
    dhidden = jnp.sum(dhidden.astype(f32), axis=0)
    cot = (dhidden * jnp.concatenate([silu_gate, silu_gate], axis=1)).astype(bf16)
    cot_own = to_all(cot, WIDTH_CHIPS).reshape(count, 2 * FF_HALF)
    cot_far = other_core(cot_own)
    done = sophia_half(core, turned, cot_own, up_moment, up_curvature, ())
    return tuple(sophia_half(far, turned, cot_far, up_moment, up_curvature, done))


def solution(mesh):
    fine = Mesh(mesh.devices.reshape(2, 4, 2, 4, 2), ("xl", "y", "core", "z", "xh"))
    dp = ("xl", "y", "core")
    tensor = ("z", "xh")
    both = P(dp, tensor)
    placed = (P(None, dp), both, both, P(tensor, dp), both, both, both, P(dp), P(dp))
    return jax.shard_map(
        on_device,
        mesh=fine,
        in_specs=placed,
        out_specs=(both, both, both),
        check_vma=False,
    )
```

```python
import jax
import jax.numpy as jnp
from jax import lax
from jax.experimental import pallas as pl
from jax.experimental.pallas import tpu as pltpu
from jax.sharding import Mesh, PartitionSpec as P

D = 8192
FF_HALF = 896
V_HALF = 1024
BLOCK = 64
CHIPS = 8
PAD = 128
N_STATS = 8
STEP = 16384.0
TINY = 1e-30

beta_one = 0.965
beta_two = 0.95
rho_scale = 0.05
eps_norm = 1e-05

WIDTH_CHIPS = ("y", "xl")
UNIT_CHIPS = ("z", "xh")
f32 = jnp.float32
bf16 = jnp.bfloat16
VMEM_LIMIT = 60 * 1024 * 1024
STEPS = 4


def other_core(value):
    return lax.ppermute(value, "core", [(0, 1), (1, 0)])


def exchange(blocks, axes):
    return lax.all_to_all(blocks, axes, split_axis=0, concat_axis=0, tiled=True)


def to_all(block, axes):
    copies = jnp.broadcast_to(block[None], (CHIPS,) + block.shape)
    return exchange(copies, axes)


def together(*values):
    return lax.optimization_barrier(values)


def dot(left, right):
    return jnp.dot(left, right, preferred_element_type=f32)


def dot_rows(left, right):
    return lax.dot_general(left, right, (((1,), (1,)), ((), ())), preferred_element_type=f32)


def from_three(parts, count):
    parts = parts.astype(f32)
    return parts[..., :count] + parts[..., count : 2 * count] + parts[..., 2 * count : 3 * count]


def whole(array):
    return pl.BlockSpec(array.shape, lambda step, half: (0,) * array.ndim)


def columns_of(array, count):
    return pl.BlockSpec((array.shape[0], count), lambda step, half: (0, half[0]))


def rows_of(array, count):
    return pl.BlockSpec((count, array.shape[1]), lambda step, half: (half[0], 0))


def row_blocks(array):
    return pl.BlockSpec((array.shape[0] // STEPS,) + array.shape[1:], lambda step, half: (step,) + (0,) * (array.ndim - 1))


def on_core(kernel, half, operands, specs, outs, flops, steps=1):
    size = sum(operand.size * operand.dtype.itemsize for operand in operands)
    results = pl.pallas_call(
        kernel,
        out_shape=tuple(jax.ShapeDtypeStruct(shape, dtype) for shape, dtype in outs),
        grid_spec=pltpu.PrefetchScalarGridSpec(
            num_scalar_prefetch=1,
            grid=(steps,),
            in_specs=specs,
            out_specs=tuple((whole if steps == 1 else row_blocks)(jax.ShapeDtypeStruct(*out)) for out in outs),
        ),
        compiler_params=pltpu.CompilerParams(vmem_limit_bytes=VMEM_LIMIT),
        cost_estimate=pl.CostEstimate(flops=flops, bytes_accessed=size, transcendentals=0),
    )(half.reshape(1), *operands)
    return results if len(outs) > 1 else results[0]


def gate_up_far(half_ref, tokens, gate, up, out):
    out[:, :FF_HALF] = dot(tokens[...], gate[...]).astype(bf16)
    out[:, FF_HALF:] = dot(tokens[...], up[...]).astype(bf16)


def gate_up_own(half_ref, tokens, gate, up, got, labels, out):
    gate_sum = dot(tokens[...], gate[...]) + got[:, :FF_HALF].astype(f32)
    out[:, :FF_HALF] = gate_sum.astype(bf16)
    up_sum = dot(tokens[...], up[...]) + got[:, FF_HALF:].astype(f32)
    out[:, FF_HALF : 2 * FF_HALF] = up_sum.astype(bf16)
    for block in range(CHIPS // STEPS):
        out[block * BLOCK : (block + 1) * BLOCK, 2 * FF_HALF :] = labels[...]


def hidden_kernel(half_ref, both, hidden, silu_out):
    gate = jnp.zeros((BLOCK, FF_HALF), f32)
    upper = jnp.zeros((BLOCK, FF_HALF), f32)
    for chip in range(CHIPS):
        gate = gate + both[chip, :, :FF_HALF].astype(f32)
        upper = upper + both[chip, :, FF_HALF : 2 * FF_HALF].astype(f32)
    silu_gate = gate / (1.0 + jnp.exp(-gate))
    silu_out[...] = silu_gate
    rounded = (silu_gate * upper).astype(bf16)
    for chip in range(CHIPS):
        hidden[chip] = rounded


def squares_of(rows):
    wide = rows[...].astype(f32)
    return jnp.sum(wide * wide, axis=1, keepdims=True)


def exponent_of(values):
    return jnp.ceil(jnp.log2(jnp.maximum(values, TINY)))


def logits_kernel(half_ref, rows, far_rows, head, head_got, out):
    raw = dot(rows[...], head[...]) + dot(far_rows[...], head_got[...])
    squares = squares_of(rows) + squares_of(far_rows)
    level = exponent_of(jnp.max(jnp.abs(raw), axis=1, keepdims=True))
    out[:, :V_HALF] = jnp.round(raw * (STEP * jnp.exp2(-level))).astype(jnp.int32).astype(jnp.int16)
    square_level = exponent_of(squares)
    units = squares * (STEP * jnp.exp2(-square_level))
    high = jnp.floor(units)
    low = jnp.floor((units - high) * STEP)
    lane = lax.broadcasted_iota(jnp.int32, (rows.shape[0], PAD), 1)
    tail = jnp.where(lane == 0, level, jnp.where(lane == 1, high, jnp.where(lane == 2, low, square_level)))
    out[:, V_HALF:] = tail.astype(jnp.int32).astype(jnp.int16)


def pack_three(values):
    lane = lax.broadcasted_iota(jnp.int32, values.shape, 1)
    values = jnp.where(lane < N_STATS, values, 0.0)
    high = values.astype(bf16)
    rest = values - high.astype(f32)
    middle = rest.astype(bf16)
    low = (rest - middle.astype(f32)).astype(bf16)
    row = lax.broadcasted_iota(jnp.int32, (PAD, PAD), 0)
    lane = lax.broadcasted_iota(jnp.int32, (PAD, PAD), 1)
    by_one = (lane == row + N_STATS).astype(f32).astype(bf16)
    by_two = (lane == row + 2 * N_STATS).astype(f32).astype(bf16)
    return (high.astype(f32) + dot(middle, by_one) + dot(low, by_two)).astype(bf16)


def softmax_kernel(start_ref, raw, labels, out):
    total = jnp.zeros((BLOCK, V_HALF), f32)
    squares = jnp.zeros((BLOCK, 1), f32)
    for chip in range(CHIPS):
        tail = raw[chip, :, V_HALF:].astype(jnp.int32).astype(f32)
        scale = jnp.exp2(tail[:, 0:1]) / STEP
        total = total + raw[chip, :, :V_HALF].astype(jnp.int32).astype(f32) * scale
        square_scale = jnp.exp2(tail[:, 3:4]) / STEP
        squares = squares + (tail[:, 1:2] + tail[:, 2:3] / STEP) * square_scale
    inv_rms = lax.rsqrt(squares / D + eps_norm)
    logits = total * inv_rms
    top = jnp.max(logits, axis=1, keepdims=True)
    exp_terms = jnp.exp(logits - top)
    short = exp_terms.astype(bf16)
    rounded = short.astype(f32)
    ids = start_ref[0] + lax.broadcasted_iota(jnp.int32, (BLOCK, V_HALF), 1)
    stats = [
        top,
        inv_rms,
        jnp.sum(exp_terms, axis=1, keepdims=True),
        jnp.sum(rounded * logits, axis=1, keepdims=True),
    ]
    for which in range(2):
        hot = labels[:, which : which + 1] == ids
        stats.append(jnp.sum(jnp.where(hot, logits, 0.0), axis=1, keepdims=True))
        stats.append(jnp.sum(jnp.where(hot, exp_terms - rounded, 0.0), axis=1, keepdims=True))
    lane = lax.broadcasted_iota(jnp.int32, (BLOCK, PAD), 1)
    table = jnp.zeros((BLOCK, PAD), f32)
    for place, value in enumerate(stats):
        table = jnp.where(lane == place, value, table)
    packed = pack_three(table)
    for chip in range(CHIPS):
        out[chip, :, :V_HALF] = short
        out[chip, :, V_HALF:] = packed


def pull_back(half_ref, own, far, head_own, head_far, out):
    count = own.shape[0]
    row = lax.broadcasted_iota(jnp.int32, (PAD, PAD), 0)
    lane = lax.broadcasted_iota(jnp.int32, (PAD, PAD), 1)
    gather = ((row % N_STATS == lane) & (row < 3 * N_STATS)).astype(f32).astype(bf16)
    stats_own = dot(own[:, V_HALF:], gather)
    stats_far = dot(far[:, V_HALF:], gather)
    top = jnp.maximum(stats_own[:, 0:1], stats_far[:, 0:1])
    scale_own = jnp.exp(stats_own[:, 0:1] - top)
    scale_far = jnp.exp(stats_far[:, 0:1] - top)
    pulled = scale_own * dot_rows(own[:, :V_HALF], head_own[...])
    pulled = pulled + scale_far * dot_rows(far[:, :V_HALF], head_far[...])
    width = pulled.shape[1]
    out[:, :width] = pulled.astype(bf16)
    lane = lax.broadcasted_iota(jnp.int32, (count, PAD), 1)
    is_sum = (lane == 2) | (lane == 3) | (lane == 5) | (lane == 7)
    both = jnp.where(is_sum, scale_own * stats_own + scale_far * stats_far, stats_own + stats_far)
    both = jnp.where(lane == 0, top, jnp.where(lane == 1, stats_own, both))
    out[:, width:] = pack_three(both)


def back_kernel(half_ref, dsummed, far_dsummed, down, down_got, out):
    width = down.shape[1]
    for which in range(2):
        place = slice(which * width, (which + 1) * width)
        part = dot_rows(dsummed[:, place], down[...]) + dot_rows(far_dsummed[:, place], down_got[...])
        out[:, which * FF_HALF : (which + 1) * FF_HALF] = part.astype(bf16)


def step_kernel(half_ref, turned, cot, moment_ref, curve_ref, *rest):
    new_moment, new_curve, update = rest[-3:]
    grad_true = dot(turned[...], cot[:, :FF_HALF])
    grad_sampled = dot(turned[...], cot[:, FF_HALF:])
    moment = beta_one * moment_ref[...] + (1.0 - beta_one) * grad_true
    curve = beta_two * curve_ref[...] + (1.0 - beta_two) * grad_sampled * grad_sampled
    new_moment[...] = moment
    new_curve[...] = curve
    update[...] = jnp.clip(moment / (rho_scale * curve), -1.0, 1.0)


def sophia_half(half, turned, cot, moment, curve, done):
    tall = 128
    rows, count = turned.shape
    big = pl.BlockSpec((tall, FF_HALF), lambda step, half: (step, half[0]))
    shape = jax.ShapeDtypeStruct(moment.shape, f32)
    kept = [pl.BlockSpec(memory_space=pl.ANY) for _ in done]
    return pl.pallas_call(
        step_kernel,
        out_shape=(shape, shape, shape),
        grid_spec=pltpu.PrefetchScalarGridSpec(
            num_scalar_prefetch=1,
            grid=(rows // tall,),
            in_specs=[
                pl.BlockSpec((tall, count), lambda step, half: (step, 0)),
                whole(cot),
                big,
                big,
            ]
            + kept,
            out_specs=(big, big, big),
        ),
        input_output_aliases={5 + which: which for which in range(len(done))},
        compiler_params=pltpu.CompilerParams(vmem_limit_bytes=VMEM_LIMIT),
        cost_estimate=pl.CostEstimate(flops=950000000, bytes_accessed=11000000, transcendentals=0),
    )(half.reshape(1), turned, cot, moment, curve, *done)


def own_part(array, index, axis):
    keep = lax.dynamic_index_in_dim(array, index, axis, keepdims=False)
    send = lax.dynamic_index_in_dim(array, 1 - index, axis, keepdims=False)
    return keep, send


def label_rows(labels, head_weight, unit_chip):
    ids = unit_chip * (2 * V_HALF) + lax.broadcasted_iota(jnp.int32, (1, 2 * V_HALF), 1)
    parts = []
    for which in range(2):
        hot = (labels[:, which : which + 1] == ids).astype(bf16)
        parts.append(dot_rows(hot, head_weight).astype(bf16))
    return jnp.concatenate(parts, axis=1).reshape(2, 2, 2, BLOCK, -1)


def pair_label_rows(rows):
    keep, send = own_part(rows, lax.axis_index("z") % 2, 1)
    return keep + lax.ppermute(send, "z", [(0, 1), (1, 0), (2, 3), (3, 2)])


def own_label_rows(rows):
    keep, send = own_part(rows, lax.axis_index("z") // 2, 0)
    rows = keep + lax.ppermute(send, "z", [(0, 2), (2, 0), (1, 3), (3, 1)])
    keep, send = own_part(rows, lax.axis_index("xh"), 0)
    return keep + lax.ppermute(send, "xh", [(0, 1), (1, 0)])


def on_device(
    tokens,
    gate_weight,
    up_weight,
    down_weight,
    head_weight,
    up_moment,
    up_curvature,
    true_labels,
    sampled_labels,
):
    core = lax.axis_index("core").astype(jnp.int32)
    far = 1 - core
    unit_chip = lax.axis_index(UNIT_CHIPS)
    count, width = tokens.shape

    labels = jnp.stack([true_labels, sampled_labels], axis=1)
    far_labels = other_core(labels)
    labels = jnp.where(
        core == 0,
        jnp.concatenate([labels, far_labels], axis=0),
        jnp.concatenate([far_labels, labels], axis=0),
    )
    digits = jnp.concatenate([labels // PAD, labels % PAD], axis=1).astype(bf16)
    digits = jnp.pad(digits, ((0, 0), (0, PAD - 4)))

    w_specs = [row_blocks(tokens), columns_of(gate_weight, FF_HALF), columns_of(up_weight, FF_HALF)]
    gate_up_flops = 4 * count * width * FF_HALF
    sent = on_core(
        gate_up_far,
        far,
        (tokens, gate_weight, up_weight),
        w_specs,
        [((count, 2 * FF_HALF), bf16)],
        gate_up_flops,
        STEPS,
    )
    got = other_core(sent)
    both = on_core(
        gate_up_own,
        core,
        (tokens, gate_weight, up_weight, got, digits),
        w_specs + [row_blocks(got), whole(digits)],
        [((count, 2 * FF_HALF + PAD), bf16)],
        gate_up_flops,
        STEPS,
    )
    head_send = lax.dynamic_slice_in_dim(head_weight, far * V_HALF, V_HALF, 1)
    down_send = lax.dynamic_slice_in_dim(down_weight, far * FF_HALF, FF_HALF, 0)
    both, head_send, down_send = together(both, head_send, down_send)
    both, head_got, down_got = together(
        exchange(both.reshape(CHIPS, BLOCK, 2 * FF_HALF + PAD), WIDTH_CHIPS),
        other_core(head_send),
        other_core(down_send),
    )
    hidden, silu_gate = on_core(
        hidden_kernel,
        core,
        (both,),
        [whole(both)],
        [((CHIPS, BLOCK, FF_HALF), bf16), ((BLOCK, FF_HALF), f32)],
        1000000,
    )

    hidden, digits = together(hidden, both)
    digits = digits[:, :, 2 * FF_HALF : 2 * FF_HALF + 4].astype(jnp.int32)
    all_labels = digits[:, :, :2] * PAD + digits[:, :, 2:]
    all_labels = all_labels.reshape(4, 2, BLOCK, 2).transpose(1, 0, 2, 3).reshape(count, 2)
    width_chip = lax.axis_index(WIDTH_CHIPS)
    hidden_own, label_row, labels, down_own, down_far = together(
        exchange(hidden, WIDTH_CHIPS),
        label_rows(all_labels, head_weight, unit_chip),
        lax.dynamic_slice_in_dim(all_labels, width_chip * BLOCK, BLOCK, 0),
        lax.dynamic_slice_in_dim(down_weight, core * FF_HALF, FF_HALF, 0),
        lax.dynamic_slice_in_dim(down_weight, far * FF_HALF, FF_HALF, 0),
    )
    hidden_own = hidden_own.reshape(count, FF_HALF)
    hidden_far = other_core(hidden_own)
    branch = dot(hidden_own, down_own) + dot(hidden_far, down_far)
    branch = exchange(branch.astype(bf16).reshape(CHIPS, BLOCK, width), UNIT_CHIPS)
    branch = jnp.sum(branch.astype(f32), axis=0)
    own_tokens = lax.dynamic_slice_in_dim(tokens, unit_chip * BLOCK, BLOCK, 0)
    summed = own_tokens.astype(f32) + branch
    rows = to_all(summed.astype(bf16), UNIT_CHIPS).reshape(count, width)

    far_rows = other_core(rows)
    logit_flops = 4 * count * width * V_HALF
    raw = on_core(
        logits_kernel,
        core,
        (rows, far_rows, head_weight, head_got),
        [whole(rows), whole(far_rows), columns_of(head_weight, V_HALF), whole(head_got)],
        [((count, V_HALF + PAD), jnp.int16)],
        logit_flops,
    )
    raw, label_row = together(raw, label_row)
    raw, label_row = together(
        exchange(raw.reshape(CHIPS, BLOCK, V_HALF + PAD), WIDTH_CHIPS), pair_label_rows(label_row)
    )
    vocab_start = ((unit_chip * 2 + core) * V_HALF).astype(jnp.int32)
    packed = on_core(
        softmax_kernel,
        vocab_start,
        (raw, labels),
        [whole(raw), whole(labels)],
        [((CHIPS, BLOCK, V_HALF + PAD), bf16)],
        1000000,
    )
    packed, token_rows, label_row = together(packed, tokens, label_row)
    packed_own, turned, label_row = together(
        exchange(packed, WIDTH_CHIPS), token_rows.T, own_label_rows(label_row)
    )
    label_row = label_row.astype(f32)
    packed_own = packed_own.reshape(count, V_HALF + PAD)
    packed_far = other_core(packed_own)
    packed = on_core(
        pull_back,
        core,
        (packed_own, packed_far, head_weight, head_weight),
        [
            row_blocks(packed_own),
            row_blocks(packed_far),
            pl.BlockSpec((width, V_HALF), lambda step, half: (0, half[0])),
            pl.BlockSpec((width, V_HALF), lambda step, half: (0, 1 - half[0])),
        ],
        [((count, width + PAD), bf16)],
        logit_flops,
        STEPS,
    )
    packed = exchange(packed.reshape(CHIPS, BLOCK, width + PAD), UNIT_CHIPS)
    stats = from_three(packed[:, :, width:], N_STATS)
    row_top = jnp.max(stats[:, :, 0:1], axis=0, keepdims=True)
    weight = jnp.exp(stats[:, :, 0:1] - row_top)
    weight = weight / jnp.sum(weight * stats[:, :, 2:3], axis=0, keepdims=True)
    pulled = jnp.sum(weight * packed[:, :, :width].astype(f32), axis=0)
    pull = jnp.sum(weight * stats[:, :, 3:4], axis=0)
    inv_rms = stats[0, :, 1:2]
    scaled = summed * inv_rms
    dsummed = []
    for which in range(2):
        label_logit = jnp.sum(stats[:, :, 4 + 2 * which : 5 + 2 * which], axis=0)
        rest = jnp.sum(weight * stats[:, :, 5 + 2 * which : 6 + 2 * which], axis=0)
        dnormed = pulled - (1.0 - rest) * label_row[:, which * width : (which + 1) * width]
        mean = (pull - (1.0 - rest) * label_logit) / D
        dsummed.append((inv_rms * (dnormed - scaled * mean)).astype(bf16))
    dsummed = to_all(jnp.concatenate(dsummed, axis=1), UNIT_CHIPS).reshape(count, 2 * width)

    far_dsummed = other_core(dsummed)
    dhidden = on_core(
        back_kernel,
        core,
        (dsummed, far_dsummed, down_weight, down_got),
        [row_blocks(dsummed), row_blocks(far_dsummed), rows_of(down_weight, FF_HALF), whole(down_got)],
        [((count, 2 * FF_HALF), bf16)],
        2 * gate_up_flops,
        STEPS,
    )
    dhidden = exchange(dhidden.reshape(CHIPS, BLOCK, 2 * FF_HALF), WIDTH_CHIPS)
    dhidden = jnp.sum(dhidden.astype(f32), axis=0)
    cot = (dhidden * jnp.concatenate([silu_gate, silu_gate], axis=1)).astype(bf16)
    cot_own = to_all(cot, WIDTH_CHIPS).reshape(count, 2 * FF_HALF)
    cot_far = other_core(cot_own)
    done = sophia_half(core, turned, cot_own, up_moment, up_curvature, ())
    return tuple(sophia_half(far, turned, cot_far, up_moment, up_curvature, done))


def solution(mesh):
    fine = Mesh(mesh.devices.reshape(2, 4, 2, 4, 2), ("xl", "y", "core", "z", "xh"))
    dp = ("xl", "y", "core")
    tensor = ("z", "xh")
    both = P(dp, tensor)
    placed = (P(None, dp), both, both, P(tensor, dp), both, both, both, P(dp), P(dp))
    return jax.shard_map(
        on_device,
        mesh=fine,
        in_specs=placed,
        out_specs=(both, both, both),
        check_vma=False,
    )
```

```python
import jax
import jax.numpy as jnp
from jax import lax
from jax.experimental import pallas as pl
from jax.experimental.pallas import tpu as pltpu
from jax.sharding import Mesh, PartitionSpec as P

D = 8192
FF_HALF = 896
V_HALF = 1024
BLOCK = 64
CHIPS = 8
PAD = 128
N_STATS = 8
STEP = 16384.0
TINY = 1e-30

beta_one = 0.965
beta_two = 0.95
rho_scale = 0.05
eps_norm = 1e-05

WIDTH_CHIPS = ("y", "xl")
UNIT_CHIPS = ("z", "xh")
f32 = jnp.float32
bf16 = jnp.bfloat16
VMEM_LIMIT = 24 * 1024 * 1024


def other_core(value):
    return lax.ppermute(value, "core", [(0, 1), (1, 0)])


def exchange(blocks, axes):
    return lax.all_to_all(blocks, axes, split_axis=0, concat_axis=0, tiled=True)


def to_all(block, axes):
    copies = jnp.broadcast_to(block[None], (CHIPS,) + block.shape)
    return exchange(copies, axes)


def together(*values):
    return lax.optimization_barrier(values)


def dot(left, right):
    return jnp.dot(left, right, preferred_element_type=f32)


def dot_rows(left, right):
    return lax.dot_general(left, right, (((1,), (1,)), ((), ())), preferred_element_type=f32)


def from_three(parts, count):
    parts = parts.astype(f32)
    return parts[..., :count] + parts[..., count : 2 * count] + parts[..., 2 * count : 3 * count]


def whole(array):
    return pl.BlockSpec(array.shape, lambda step, half: (0,) * array.ndim)


def columns_of(array, count):
    return pl.BlockSpec((array.shape[0], count), lambda step, half: (0, half[0]))


def rows_of(array, count):
    return pl.BlockSpec((count, array.shape[1]), lambda step, half: (half[0], 0))


def on_core(kernel, half, operands, specs, outs, flops):
    size = sum(operand.size * operand.dtype.itemsize for operand in operands)
    results = pl.pallas_call(
        kernel,
        out_shape=tuple(jax.ShapeDtypeStruct(shape, dtype) for shape, dtype in outs),
        grid_spec=pltpu.PrefetchScalarGridSpec(
            num_scalar_prefetch=1,
            grid=(1,),
            in_specs=specs,
            out_specs=tuple(whole(jax.ShapeDtypeStruct(*out)) for out in outs),
        ),
        compiler_params=pltpu.CompilerParams(vmem_limit_bytes=VMEM_LIMIT),
        cost_estimate=pl.CostEstimate(flops=flops, bytes_accessed=size, transcendentals=0),
    )(half.reshape(1), *operands)
    return results if len(outs) > 1 else results[0]


def gate_up_own(half_ref, tokens, gate, up, got_gate, got_up, labels, out):
    gate_sum = dot(tokens[...], gate[...]) + got_gate[...].astype(f32)
    out[:, :FF_HALF] = gate_sum.astype(bf16)
    up_sum = dot(tokens[...], up[...]) + got_up[...].astype(f32)
    out[:, FF_HALF : 2 * FF_HALF] = up_sum.astype(bf16)
    for block in range(CHIPS):
        out[block * BLOCK : (block + 1) * BLOCK, 2 * FF_HALF :] = labels[...]


def hidden_kernel(half_ref, both, hidden, silu_out):
    gate = jnp.zeros((BLOCK, FF_HALF), f32)
    upper = jnp.zeros((BLOCK, FF_HALF), f32)
    for chip in range(CHIPS):
        gate = gate + both[chip, :, :FF_HALF].astype(f32)
        upper = upper + both[chip, :, FF_HALF : 2 * FF_HALF].astype(f32)
    silu_gate = gate / (1.0 + jnp.exp(-gate))
    silu_out[...] = silu_gate
    rounded = (silu_gate * upper).astype(bf16)
    for chip in range(CHIPS):
        hidden[chip] = rounded


def squares_of(rows):
    wide = rows[...].astype(f32)
    return jnp.sum(wide * wide, axis=1, keepdims=True)


def exponent_of(values):
    return jnp.ceil(jnp.log2(jnp.maximum(values, TINY)))


def logits_kernel(half_ref, rows, far_rows, head, head_got, out):
    raw = dot(rows[...], head[...]) + dot(far_rows[...], head_got[...])
    squares = squares_of(rows) + squares_of(far_rows)
    level = exponent_of(jnp.max(jnp.abs(raw), axis=1, keepdims=True))
    out[:, :V_HALF] = jnp.round(raw * (STEP * jnp.exp2(-level))).astype(jnp.int32).astype(jnp.int16)
    square_level = exponent_of(squares)
    units = squares * (STEP * jnp.exp2(-square_level))
    high = jnp.floor(units)
    low = jnp.floor((units - high) * STEP)
    lane = lax.broadcasted_iota(jnp.int32, (rows.shape[0], PAD), 1)
    tail = jnp.where(lane == 0, level, jnp.where(lane == 1, high, jnp.where(lane == 2, low, square_level)))
    out[:, V_HALF:] = tail.astype(jnp.int32).astype(jnp.int16)


def pack_three(values):
    lane = lax.broadcasted_iota(jnp.int32, values.shape, 1)
    values = jnp.where(lane < N_STATS, values, 0.0)
    high = values.astype(bf16)
    rest = values - high.astype(f32)
    middle = rest.astype(bf16)
    low = (rest - middle.astype(f32)).astype(bf16)
    row = lax.broadcasted_iota(jnp.int32, (PAD, PAD), 0)
    lane = lax.broadcasted_iota(jnp.int32, (PAD, PAD), 1)
    by_one = (lane == row + N_STATS).astype(f32).astype(bf16)
    by_two = (lane == row + 2 * N_STATS).astype(f32).astype(bf16)
    return (high.astype(f32) + dot(middle, by_one) + dot(low, by_two)).astype(bf16)


def softmax_kernel(start_ref, raw, labels, out):
    total = jnp.zeros((BLOCK, V_HALF), f32)
    squares = jnp.zeros((BLOCK, 1), f32)
    for chip in range(CHIPS):
        tail = raw[chip, :, V_HALF:].astype(jnp.int32).astype(f32)
        scale = jnp.exp2(tail[:, 0:1]) / STEP
        total = total + raw[chip, :, :V_HALF].astype(jnp.int32).astype(f32) * scale
        square_scale = jnp.exp2(tail[:, 3:4]) / STEP
        squares = squares + (tail[:, 1:2] + tail[:, 2:3] / STEP) * square_scale
    inv_rms = lax.rsqrt(squares / D + eps_norm)
    logits = total * inv_rms
    top = jnp.max(logits, axis=1, keepdims=True)
    exp_terms = jnp.exp(logits - top)
    short = exp_terms.astype(bf16)
    rounded = short.astype(f32)
    ids = start_ref[0] + lax.broadcasted_iota(jnp.int32, (BLOCK, V_HALF), 1)
    stats = [
        top,
        inv_rms,
        jnp.sum(exp_terms, axis=1, keepdims=True),
        jnp.sum(rounded * logits, axis=1, keepdims=True),
    ]
    for which in range(2):
        hot = labels[:, which : which + 1] == ids
        stats.append(jnp.sum(jnp.where(hot, logits, 0.0), axis=1, keepdims=True))
        stats.append(jnp.sum(jnp.where(hot, exp_terms - rounded, 0.0), axis=1, keepdims=True))
    lane = lax.broadcasted_iota(jnp.int32, (BLOCK, PAD), 1)
    table = jnp.zeros((BLOCK, PAD), f32)
    for place, value in enumerate(stats):
        table = jnp.where(lane == place, value, table)
    packed = pack_three(table)
    for chip in range(CHIPS):
        out[chip, :, :V_HALF] = short
        out[chip, :, V_HALF:] = packed


def pull_back(half_ref, own, far, head_own, head_far, out):
    count = own.shape[0]
    row = lax.broadcasted_iota(jnp.int32, (PAD, PAD), 0)
    lane = lax.broadcasted_iota(jnp.int32, (PAD, PAD), 1)
    gather = ((row % N_STATS == lane) & (row < 3 * N_STATS)).astype(f32).astype(bf16)
    stats_own = dot(own[:, V_HALF:], gather)
    stats_far = dot(far[:, V_HALF:], gather)
    top = jnp.maximum(stats_own[:, 0:1], stats_far[:, 0:1])
    scale_own = jnp.exp(stats_own[:, 0:1] - top)
    scale_far = jnp.exp(stats_far[:, 0:1] - top)
    pulled = scale_own * dot_rows(own[:, :V_HALF], head_own[...])
    pulled = pulled + scale_far * dot_rows(far[:, :V_HALF], head_far[...])
    width = pulled.shape[1]
    out[:, :width] = pulled.astype(bf16)
    lane = lax.broadcasted_iota(jnp.int32, (count, PAD), 1)
    is_sum = (lane == 2) | (lane == 3) | (lane == 5) | (lane == 7)
    both = jnp.where(is_sum, scale_own * stats_own + scale_far * stats_far, stats_own + stats_far)
    both = jnp.where(lane == 0, top, jnp.where(lane == 1, stats_own, both))
    out[:, width:] = pack_three(both)


def back_kernel(half_ref, dsummed, far_dsummed, down, down_got, out):
    width = down.shape[1]
    for which in range(2):
        place = slice(which * width, (which + 1) * width)
        part = dot_rows(dsummed[:, place], down[...]) + dot_rows(far_dsummed[:, place], down_got[...])
        out[:, which * FF_HALF : (which + 1) * FF_HALF] = part.astype(bf16)


def step_kernel(half_ref, turned, cot, moment_ref, curve_ref, *rest):
    new_moment, new_curve, update = rest[-3:]
    grad_true = dot(turned[...], cot[:, :FF_HALF])
    grad_sampled = dot(turned[...], cot[:, FF_HALF:])
    moment = beta_one * moment_ref[...] + (1.0 - beta_one) * grad_true
    curve = beta_two * curve_ref[...] + (1.0 - beta_two) * grad_sampled * grad_sampled
    new_moment[...] = moment
    new_curve[...] = curve
    update[...] = jnp.clip(moment / (rho_scale * curve), -1.0, 1.0)


def sophia_half(half, turned, cot, moment, curve, done):
    tall = 128
    rows, count = turned.shape
    big = pl.BlockSpec((tall, FF_HALF), lambda step, half: (step, half[0]))
    shape = jax.ShapeDtypeStruct(moment.shape, f32)
    kept = [pl.BlockSpec(memory_space=pl.ANY) for _ in done]
    return pl.pallas_call(
        step_kernel,
        out_shape=(shape, shape, shape),
        grid_spec=pltpu.PrefetchScalarGridSpec(
            num_scalar_prefetch=1,
            grid=(rows // tall,),
            in_specs=[
                pl.BlockSpec((tall, count), lambda step, half: (step, 0)),
                whole(cot),
                big,
                big,
            ]
            + kept,
            out_specs=(big, big, big),
        ),
        input_output_aliases={5 + which: which for which in range(len(done))},
        compiler_params=pltpu.CompilerParams(vmem_limit_bytes=VMEM_LIMIT),
        cost_estimate=pl.CostEstimate(flops=950000000, bytes_accessed=11000000, transcendentals=0),
    )(half.reshape(1), turned, cot, moment, curve, *done)


def own_part(array, index, axis):
    keep = lax.dynamic_index_in_dim(array, index, axis, keepdims=False)
    send = lax.dynamic_index_in_dim(array, 1 - index, axis, keepdims=False)
    return keep, send


def label_rows(labels, head_weight, unit_chip):
    ids = unit_chip * (2 * V_HALF) + lax.broadcasted_iota(jnp.int32, (1, 2 * V_HALF), 1)
    parts = []
    for which in range(2):
        hot = (labels[:, which : which + 1] == ids).astype(bf16)
        parts.append(dot_rows(hot, head_weight).astype(bf16))
    return jnp.concatenate(parts, axis=1).reshape(2, 2, 2, BLOCK, -1)


def pair_label_rows(rows):
    keep, send = own_part(rows, lax.axis_index("z") % 2, 1)
    return keep + lax.ppermute(send, "z", [(0, 1), (1, 0), (2, 3), (3, 2)])


def own_label_rows(rows):
    keep, send = own_part(rows, lax.axis_index("z") // 2, 0)
    rows = keep + lax.ppermute(send, "z", [(0, 2), (2, 0), (1, 3), (3, 1)])
    keep, send = own_part(rows, lax.axis_index("xh"), 0)
    return keep + lax.ppermute(send, "xh", [(0, 1), (1, 0)])


def on_device(
    tokens,
    gate_weight,
    up_weight,
    down_weight,
    head_weight,
    up_moment,
    up_curvature,
    true_labels,
    sampled_labels,
):
    core = lax.axis_index("core").astype(jnp.int32)
    far = 1 - core
    unit_chip = lax.axis_index(UNIT_CHIPS)
    count, width = tokens.shape

    labels = jnp.stack([true_labels, sampled_labels], axis=1)
    far_labels = other_core(labels)
    labels = jnp.where(
        core == 0,
        jnp.concatenate([labels, far_labels], axis=0),
        jnp.concatenate([far_labels, labels], axis=0),
    )
    digits = jnp.concatenate([labels // PAD, labels % PAD], axis=1).astype(bf16)
    digits = jnp.pad(digits, ((0, 0), (0, PAD - 4)))

    w_specs = [whole(tokens), columns_of(gate_weight, FF_HALF), columns_of(up_weight, FF_HALF)]
    gate_up_flops = 4 * count * width * FF_HALF
    far_gate = lax.dynamic_slice_in_dim(gate_weight, far * FF_HALF, FF_HALF, 1)
    far_up = lax.dynamic_slice_in_dim(up_weight, far * FF_HALF, FF_HALF, 1)
    got_gate = other_core(dot(tokens, far_gate).astype(bf16))
    got_up = other_core(dot(tokens, far_up).astype(bf16))
    both = on_core(
        gate_up_own,
        core,
        (tokens, gate_weight, up_weight, got_gate, got_up, digits),
        w_specs + [whole(got_gate), whole(got_up), whole(digits)],
        [((count, 2 * FF_HALF + PAD), bf16)],
        gate_up_flops,
    )
    head_send = lax.dynamic_slice_in_dim(head_weight, far * V_HALF, V_HALF, 1)
    down_send = lax.dynamic_slice_in_dim(down_weight, far * FF_HALF, FF_HALF, 0)
    both, head_send, down_send = together(both, head_send, down_send)
    both, head_got, down_got = together(
        exchange(both.reshape(CHIPS, BLOCK, 2 * FF_HALF + PAD), WIDTH_CHIPS),
        other_core(head_send),
        other_core(down_send),
    )
    hidden, silu_gate = on_core(
        hidden_kernel,
        core,
        (both,),
        [whole(both)],
        [((CHIPS, BLOCK, FF_HALF), bf16), ((BLOCK, FF_HALF), f32)],
        1000000,
    )

    hidden, digits = together(hidden, both)
    digits = digits[:, :, 2 * FF_HALF : 2 * FF_HALF + 4].astype(jnp.int32)
    all_labels = digits[:, :, :2] * PAD + digits[:, :, 2:]
    all_labels = all_labels.reshape(4, 2, BLOCK, 2).transpose(1, 0, 2, 3).reshape(count, 2)
    width_chip = lax.axis_index(WIDTH_CHIPS)
    hidden_own, label_row, labels, down_own, down_far = together(
        exchange(hidden, WIDTH_CHIPS),
        label_rows(all_labels, head_weight, unit_chip),
        lax.dynamic_slice_in_dim(all_labels, width_chip * BLOCK, BLOCK, 0),
        lax.dynamic_slice_in_dim(down_weight, core * FF_HALF, FF_HALF, 0),
        lax.dynamic_slice_in_dim(down_weight, far * FF_HALF, FF_HALF, 0),
    )
    hidden_own = hidden_own.reshape(count, FF_HALF)
    hidden_far = other_core(hidden_own)
    branch = dot(hidden_own, down_own) + dot(hidden_far, down_far)
    branch = exchange(branch.astype(bf16).reshape(CHIPS, BLOCK, width), UNIT_CHIPS)
    branch = jnp.sum(branch.astype(f32), axis=0)
    own_tokens = lax.dynamic_slice_in_dim(tokens, unit_chip * BLOCK, BLOCK, 0)
    summed = own_tokens.astype(f32) + branch
    rows = to_all(summed.astype(bf16), UNIT_CHIPS).reshape(count, width)

    far_rows = other_core(rows)
    logit_flops = 4 * count * width * V_HALF
    raw = on_core(
        logits_kernel,
        core,
        (rows, far_rows, head_weight, head_got),
        [whole(rows), whole(far_rows), columns_of(head_weight, V_HALF), whole(head_got)],
        [((count, V_HALF + PAD), jnp.int16)],
        logit_flops,
    )
    raw, label_row = together(raw, label_row)
    raw, label_row = together(
        exchange(raw.reshape(CHIPS, BLOCK, V_HALF + PAD), WIDTH_CHIPS), pair_label_rows(label_row)
    )
    vocab_start = ((unit_chip * 2 + core) * V_HALF).astype(jnp.int32)
    packed = on_core(
        softmax_kernel,
        vocab_start,
        (raw, labels),
        [whole(raw), whole(labels)],
        [((CHIPS, BLOCK, V_HALF + PAD), bf16)],
        1000000,
    )
    packed, token_rows, label_row = together(packed, tokens, label_row)
    packed_own, turned, label_row = together(
        exchange(packed, WIDTH_CHIPS), token_rows.T, own_label_rows(label_row)
    )
    label_row = label_row.astype(f32)
    packed_own = packed_own.reshape(count, V_HALF + PAD)
    packed_far = other_core(packed_own)
    packed = on_core(
        pull_back,
        core,
        (packed_own, packed_far, head_weight, head_weight),
        [
            whole(packed_own),
            whole(packed_far),
            pl.BlockSpec((width, V_HALF), lambda step, half: (0, half[0])),
            pl.BlockSpec((width, V_HALF), lambda step, half: (0, 1 - half[0])),
        ],
        [((count, width + PAD), bf16)],
        logit_flops,
    )
    packed = exchange(packed.reshape(CHIPS, BLOCK, width + PAD), UNIT_CHIPS)
    stats = from_three(packed[:, :, width:], N_STATS)
    row_top = jnp.max(stats[:, :, 0:1], axis=0, keepdims=True)
    weight = jnp.exp(stats[:, :, 0:1] - row_top)
    weight = weight / jnp.sum(weight * stats[:, :, 2:3], axis=0, keepdims=True)
    pulled = jnp.sum(weight * packed[:, :, :width].astype(f32), axis=0)
    pull = jnp.sum(weight * stats[:, :, 3:4], axis=0)
    inv_rms = stats[0, :, 1:2]
    scaled = summed * inv_rms
    dsummed = []
    for which in range(2):
        label_logit = jnp.sum(stats[:, :, 4 + 2 * which : 5 + 2 * which], axis=0)
        rest = jnp.sum(weight * stats[:, :, 5 + 2 * which : 6 + 2 * which], axis=0)
        dnormed = pulled - (1.0 - rest) * label_row[:, which * width : (which + 1) * width]
        mean = (pull - (1.0 - rest) * label_logit) / D
        dsummed.append((inv_rms * (dnormed - scaled * mean)).astype(bf16))
    dsummed = to_all(jnp.concatenate(dsummed, axis=1), UNIT_CHIPS).reshape(count, 2 * width)

    far_dsummed = other_core(dsummed)
    dhidden = on_core(
        back_kernel,
        core,
        (dsummed, far_dsummed, down_weight, down_got),
        [whole(dsummed), whole(far_dsummed), rows_of(down_weight, FF_HALF), whole(down_got)],
        [((count, 2 * FF_HALF), bf16)],
        2 * gate_up_flops,
    )
    dhidden = exchange(dhidden.reshape(CHIPS, BLOCK, 2 * FF_HALF), WIDTH_CHIPS)
    dhidden = jnp.sum(dhidden.astype(f32), axis=0)
    cot = (dhidden * jnp.concatenate([silu_gate, silu_gate], axis=1)).astype(bf16)
    cot_own = to_all(cot, WIDTH_CHIPS).reshape(count, 2 * FF_HALF)
    cot_far = other_core(cot_own)
    done = sophia_half(core, turned, cot_own, up_moment, up_curvature, ())
    return tuple(sophia_half(far, turned, cot_far, up_moment, up_curvature, done))


def solution(mesh):
    fine = Mesh(mesh.devices.reshape(2, 4, 2, 4, 2), ("xl", "y", "core", "z", "xh"))
    dp = ("xl", "y", "core")
    tensor = ("z", "xh")
    both = P(dp, tensor)
    placed = (P(None, dp), both, both, P(tensor, dp), both, both, both, P(dp), P(dp))
    return jax.shard_map(
        on_device,
        mesh=fine,
        in_specs=placed,
        out_specs=(both, both, both),
        check_vma=False,
    )
```

```python
import itertools

import jax
import jax.numpy as jnp
from jax import lax
from jax.experimental import pallas as pl
from jax.experimental.pallas import tpu as pltpu
from jax.sharding import Mesh, PartitionSpec as P

D = 8192
FF_HALF = 896
V_HALF = 1024
BLOCK = 64
CHIPS = 8
PAD = 128
N_STATS = 8
STEP = 16384.0
TINY = 1e-30

beta_one = 0.965
beta_two = 0.95
rho_scale = 0.05
eps_norm = 1e-05

WIDTH_CHIPS = ("xl", "y")
UNIT_CHIPS = ("z", "xh")
MESH_SIZES = {"xl": 2, "y": 4, "core": 2, "z": 4, "xh": 2}
f32 = jnp.float32
bf16 = jnp.bfloat16
VMEM_LIMIT = 24 * 1024 * 1024


def other_core(value):
    return lax.ppermute(value, "core", [(0, 1), (1, 0)])


def partners(axes):
    names = tuple(MESH_SIZES)
    places = list(itertools.product(*(range(size) for size in MESH_SIZES.values())))
    groups = {}
    for number, place in enumerate(places):
        fixed = tuple(value for name, value in zip(names, place) if name not in axes)
        groups.setdefault(fixed, []).append(number)
    core = names.index("core")
    return [members[::-1] if places[members[0]][core] else members for members in groups.values()]


def exchange(blocks, axes):
    return lax.all_to_all(
        blocks, tuple(MESH_SIZES), split_axis=0, concat_axis=0, tiled=True, axis_index_groups=partners(axes)
    )


def to_all(block, axes):
    copies = jnp.broadcast_to(block[None], (CHIPS,) + block.shape)
    return exchange(copies, axes)


def block_rows(block):
    return slice(block * BLOCK, (block + 1) * BLOCK)


def join_cores(own, far):
    return jnp.concatenate(
        [own[block_rows(block)] + far[block_rows(CHIPS - 1 - block)] for block in range(CHIPS)], axis=0
    )


def reverse_rows(rows):
    return jnp.concatenate([rows[block_rows(CHIPS - 1 - block)] for block in range(CHIPS)], axis=0)


def reverse_blocks(rows):
    return rows.reshape((CHIPS, BLOCK) + rows.shape[1:])[::-1].reshape(rows.shape)


def together(*values):
    return lax.optimization_barrier(values)


def dot(left, right):
    return jnp.dot(left, right, preferred_element_type=f32)


def dot_rows(left, right):
    return lax.dot_general(left, right, (((1,), (1,)), ((), ())), preferred_element_type=f32)


def from_three(parts, count):
    parts = parts.astype(f32)
    return parts[..., :count] + parts[..., count : 2 * count] + parts[..., 2 * count : 3 * count]


def whole(array):
    return pl.BlockSpec(array.shape, lambda step, half: (0,) * array.ndim)


def columns_of(array, count):
    return pl.BlockSpec((array.shape[0], count), lambda step, half: (0, half[0]))


def rows_of(array, count):
    return pl.BlockSpec((count, array.shape[1]), lambda step, half: (half[0], 0))


def on_core(kernel, half, operands, specs, outs, flops, limit=VMEM_LIMIT):
    size = sum(operand.size * operand.dtype.itemsize for operand in operands)
    results = pl.pallas_call(
        kernel,
        out_shape=tuple(jax.ShapeDtypeStruct(shape, dtype) for shape, dtype in outs),
        grid_spec=pltpu.PrefetchScalarGridSpec(
            num_scalar_prefetch=1,
            grid=(1,),
            in_specs=specs,
            out_specs=tuple(whole(jax.ShapeDtypeStruct(*out)) for out in outs),
        ),
        compiler_params=pltpu.CompilerParams(vmem_limit_bytes=limit),
        cost_estimate=pl.CostEstimate(flops=flops, bytes_accessed=size, transcendentals=0),
    )(half.reshape(1), *operands)
    return results if len(outs) > 1 else results[0]


def gate_up_own(half_ref, tokens, gate, up, got_gate, got_up, labels, out):
    core = half_ref[0]
    gate_sum = (dot(tokens[...], gate[...]) + got_gate[...].astype(f32)).astype(bf16)
    up_sum = (dot(tokens[...], up[...]) + got_up[...].astype(f32)).astype(bf16)
    for block in range(CHIPS):
        place = block + core * (CHIPS - 1 - 2 * block)
        rows = pl.ds(pl.multiple_of(place * BLOCK, BLOCK), BLOCK)
        out[rows, :FF_HALF] = gate_sum[block_rows(block)]
        out[rows, FF_HALF : 2 * FF_HALF] = up_sum[block_rows(block)]
        out[rows, 2 * FF_HALF :] = labels[...]


def branch_kernel(half_ref, own, far, down_own, down_far, out):
    out[...] = join_cores(dot(own[...], down_own[...]), dot(far[...], down_far[...])).astype(bf16)


def hidden_kernel(half_ref, both, hidden, silu_out):
    gate = jnp.zeros((BLOCK, FF_HALF), f32)
    upper = jnp.zeros((BLOCK, FF_HALF), f32)
    for chip in range(CHIPS):
        gate = gate + both[chip, :, :FF_HALF].astype(f32)
        upper = upper + both[chip, :, FF_HALF : 2 * FF_HALF].astype(f32)
    silu_gate = gate / (1.0 + jnp.exp(-gate))
    silu_out[...] = silu_gate
    rounded = (silu_gate * upper).astype(bf16)
    for chip in range(CHIPS):
        hidden[chip] = rounded


def squares_of(rows):
    wide = rows[...].astype(f32)
    return jnp.sum(wide * wide, axis=1, keepdims=True)


def exponent_of(values):
    return jnp.ceil(jnp.log2(jnp.maximum(values, TINY)))


def logits_kernel(half_ref, rows, far_rows, head, head_got, out):
    raw = join_cores(dot(rows[...], head[...]), dot(far_rows[...], head_got[...]))
    squares = join_cores(squares_of(rows), squares_of(far_rows))
    level = exponent_of(jnp.max(jnp.abs(raw), axis=1, keepdims=True))
    out[:, :V_HALF] = jnp.round(raw * (STEP * jnp.exp2(-level))).astype(jnp.int32).astype(jnp.int16)
    square_level = exponent_of(squares)
    units = squares * (STEP * jnp.exp2(-square_level))
    high = jnp.floor(units)
    low = jnp.floor((units - high) * STEP)
    lane = lax.broadcasted_iota(jnp.int32, (rows.shape[0], PAD), 1)
    tail = jnp.where(lane == 0, level, jnp.where(lane == 1, high, jnp.where(lane == 2, low, square_level)))
    out[:, V_HALF:] = tail.astype(jnp.int32).astype(jnp.int16)


def pack_three(values):
    lane = lax.broadcasted_iota(jnp.int32, values.shape, 1)
    values = jnp.where(lane < N_STATS, values, 0.0)
    high = values.astype(bf16)
    rest = values - high.astype(f32)
    middle = rest.astype(bf16)
    low = (rest - middle.astype(f32)).astype(bf16)
    row = lax.broadcasted_iota(jnp.int32, (PAD, PAD), 0)
    lane = lax.broadcasted_iota(jnp.int32, (PAD, PAD), 1)
    by_one = (lane == row + N_STATS).astype(f32).astype(bf16)
    by_two = (lane == row + 2 * N_STATS).astype(f32).astype(bf16)
    return (high.astype(f32) + dot(middle, by_one) + dot(low, by_two)).astype(bf16)


def softmax_kernel(start_ref, raw, labels, out):
    total = jnp.zeros((BLOCK, V_HALF), f32)
    squares = jnp.zeros((BLOCK, 1), f32)
    for chip in range(CHIPS):
        tail = raw[chip, :, V_HALF:].astype(jnp.int32).astype(f32)
        scale = jnp.exp2(tail[:, 0:1]) / STEP
        total = total + raw[chip, :, :V_HALF].astype(jnp.int32).astype(f32) * scale
        square_scale = jnp.exp2(tail[:, 3:4]) / STEP
        squares = squares + (tail[:, 1:2] + tail[:, 2:3] / STEP) * square_scale
    inv_rms = lax.rsqrt(squares / D + eps_norm)
    logits = total * inv_rms
    top = jnp.max(logits, axis=1, keepdims=True)
    exp_terms = jnp.exp(logits - top)
    short = exp_terms.astype(bf16)
    rounded = short.astype(f32)
    ids = start_ref[0] + lax.broadcasted_iota(jnp.int32, (BLOCK, V_HALF), 1)
    stats = [
        top,
        inv_rms,
        jnp.sum(exp_terms, axis=1, keepdims=True),
        jnp.sum(rounded * logits, axis=1, keepdims=True),
    ]
    for which in range(2):
        hot = labels[:, which : which + 1] == ids
        stats.append(jnp.sum(jnp.where(hot, logits, 0.0), axis=1, keepdims=True))
        stats.append(jnp.sum(jnp.where(hot, exp_terms - rounded, 0.0), axis=1, keepdims=True))
    lane = lax.broadcasted_iota(jnp.int32, (BLOCK, PAD), 1)
    table = jnp.zeros((BLOCK, PAD), f32)
    for place, value in enumerate(stats):
        table = jnp.where(lane == place, value, table)
    packed = pack_three(table)
    for chip in range(CHIPS):
        out[chip, :, :V_HALF] = short
        out[chip, :, V_HALF:] = packed


def pull_back(half_ref, own, far, head_own, head_far, out):
    count = own.shape[0]
    row = lax.broadcasted_iota(jnp.int32, (PAD, PAD), 0)
    lane = lax.broadcasted_iota(jnp.int32, (PAD, PAD), 1)
    gather = ((row % N_STATS == lane) & (row < 3 * N_STATS)).astype(f32).astype(bf16)
    stats_own = dot(own[:, V_HALF:], gather)
    stats_far = reverse_rows(dot(far[:, V_HALF:], gather))
    top = jnp.maximum(stats_own[:, 0:1], stats_far[:, 0:1])
    scale_own = jnp.exp(stats_own[:, 0:1] - top)
    scale_far = jnp.exp(stats_far[:, 0:1] - top)
    pulled = scale_own * dot_rows(own[:, :V_HALF], head_own[...])
    pulled = pulled + scale_far * reverse_rows(dot_rows(far[:, :V_HALF], head_far[...]))
    width = pulled.shape[1]
    out[:, :width] = pulled.astype(bf16)
    lane = lax.broadcasted_iota(jnp.int32, (count, PAD), 1)
    is_sum = (lane == 2) | (lane == 3) | (lane == 5) | (lane == 7)
    both = jnp.where(is_sum, scale_own * stats_own + scale_far * stats_far, stats_own + stats_far)
    both = jnp.where(lane == 0, top, jnp.where(lane == 1, stats_own, both))
    out[:, width:] = pack_three(both)


def back_kernel(half_ref, dsummed, far_dsummed, down, down_got, out):
    width = down.shape[1]
    for which in range(2):
        place = slice(which * width, (which + 1) * width)
        part = join_cores(dot_rows(dsummed[:, place], down[...]), dot_rows(far_dsummed[:, place], down_got[...]))
        out[:, which * FF_HALF : (which + 1) * FF_HALF] = part.astype(bf16)


def step_kernel(half_ref, turned, cot, moment_ref, curve_ref, *rest):
    new_moment, new_curve, update = rest[-3:]
    grad_true = dot(turned[...], cot[:, :FF_HALF])
    grad_sampled = dot(turned[...], cot[:, FF_HALF:])
    moment = beta_one * moment_ref[...] + (1.0 - beta_one) * grad_true
    curve = beta_two * curve_ref[...] + (1.0 - beta_two) * grad_sampled * grad_sampled
    new_moment[...] = moment
    new_curve[...] = curve
    update[...] = jnp.clip(moment / (rho_scale * curve), -1.0, 1.0)


def sophia_half(half, turned, cot, moment, curve, done):
    tall = 128
    rows, count = turned.shape
    big = pl.BlockSpec((tall, FF_HALF), lambda step, half: (step, half[0]))
    shape = jax.ShapeDtypeStruct(moment.shape, f32)
    kept = [pl.BlockSpec(memory_space=pl.ANY) for _ in done]
    return pl.pallas_call(
        step_kernel,
        out_shape=(shape, shape, shape),
        grid_spec=pltpu.PrefetchScalarGridSpec(
            num_scalar_prefetch=1,
            grid=(rows // tall,),
            in_specs=[
                pl.BlockSpec((tall, count), lambda step, half: (step, 0)),
                whole(cot),
                big,
                big,
            ]
            + kept,
            out_specs=(big, big, big),
        ),
        input_output_aliases={5 + which: which for which in range(len(done))},
        compiler_params=pltpu.CompilerParams(vmem_limit_bytes=VMEM_LIMIT),
        cost_estimate=pl.CostEstimate(flops=950000000, bytes_accessed=11000000, transcendentals=0),
    )(half.reshape(1), turned, cot, moment, curve, *done)


def own_part(array, index, axis):
    keep = lax.dynamic_index_in_dim(array, index, axis, keepdims=False)
    send = lax.dynamic_index_in_dim(array, 1 - index, axis, keepdims=False)
    return keep, send


def label_rows(labels, head_weight, unit_chip):
    ids = unit_chip * (2 * V_HALF) + lax.broadcasted_iota(jnp.int32, (1, 2 * V_HALF), 1)
    parts = []
    for which in range(2):
        hot = (labels[:, which : which + 1] == ids).astype(bf16)
        parts.append(dot_rows(hot, head_weight).astype(bf16))
    return jnp.concatenate(parts, axis=1).reshape(4, 2, BLOCK, -1)


def plane_label_rows(rows):
    z = lax.axis_index("z")
    total = lax.dynamic_index_in_dim(rows, z, 0, keepdims=False)
    for shift in (1, 3, 2):
        sent = lax.dynamic_index_in_dim(rows, (z + shift) % 4, 0, keepdims=False)
        total = total + lax.ppermute(sent, "z", [(place, (place + shift) % 4) for place in range(4)])
    return total


def own_label_rows(rows):
    keep, send = own_part(rows, lax.axis_index("xh"), 0)
    return keep + lax.ppermute(send, "xh", [(0, 1), (1, 0)])


def on_device(
    tokens,
    gate_weight,
    up_weight,
    down_weight,
    head_weight,
    up_moment,
    up_curvature,
    true_labels,
    sampled_labels,
):
    core = lax.axis_index("core").astype(jnp.int32)
    far = 1 - core
    unit_chip = lax.axis_index(UNIT_CHIPS)
    count, width = tokens.shape

    labels = jnp.stack([true_labels, sampled_labels], axis=1)
    far_labels = other_core(labels)
    labels = jnp.where(
        core == 0,
        jnp.concatenate([labels, far_labels], axis=0),
        jnp.concatenate([far_labels, labels], axis=0),
    )
    digits = jnp.concatenate([labels // PAD, labels % PAD], axis=1).astype(bf16)
    digits = jnp.pad(digits, ((0, 0), (0, PAD - 4)))

    w_specs = [whole(tokens), columns_of(gate_weight, FF_HALF), columns_of(up_weight, FF_HALF)]
    gate_up_flops = 4 * count * width * FF_HALF
    far_gate = lax.dynamic_slice_in_dim(gate_weight, far * FF_HALF, FF_HALF, 1)
    far_up = lax.dynamic_slice_in_dim(up_weight, far * FF_HALF, FF_HALF, 1)
    got_gate = other_core(dot(tokens, far_gate).astype(bf16))
    got_up = other_core(dot(tokens, far_up).astype(bf16))
    both = on_core(
        gate_up_own,
        core,
        (tokens, gate_weight, up_weight, got_gate, got_up, digits),
        w_specs + [whole(got_gate), whole(got_up), whole(digits)],
        [((count, 2 * FF_HALF + PAD), bf16)],
        gate_up_flops,
        60 * 1024 * 1024,
    )
    head_send = lax.dynamic_slice_in_dim(head_weight, far * V_HALF, V_HALF, 1)
    down_send = lax.dynamic_slice_in_dim(down_weight, far * FF_HALF, FF_HALF, 0)
    both, head_send, down_send = together(both, head_send, down_send)
    both, head_got, down_got = together(
        exchange(both.reshape(CHIPS, BLOCK, 2 * FF_HALF + PAD), WIDTH_CHIPS),
        other_core(head_send),
        other_core(down_send),
    )
    hidden, silu_gate = on_core(
        hidden_kernel,
        core,
        (both,),
        [whole(both)],
        [((CHIPS, BLOCK, FF_HALF), bf16), ((BLOCK, FF_HALF), f32)],
        1000000,
    )

    hidden, digits = together(hidden, both)
    digits = digits[:, :, 2 * FF_HALF : 2 * FF_HALF + 4].astype(jnp.int32)
    all_labels = digits[:, :, :2] * PAD + digits[:, :, 2:]
    all_labels = jnp.where(core == 0, all_labels, all_labels[::-1]).reshape(count, 2)
    width_chip = lax.axis_index(WIDTH_CHIPS)
    hidden_own, label_row, labels = together(
        exchange(hidden, WIDTH_CHIPS),
        label_rows(all_labels, head_weight, unit_chip),
        lax.dynamic_slice_in_dim(all_labels, width_chip * BLOCK, BLOCK, 0),
    )
    hidden_own = hidden_own.reshape(count, FF_HALF)
    hidden_far = other_core(hidden_own)
    branch = on_core(
        branch_kernel,
        core,
        (hidden_own, hidden_far, down_weight, down_weight),
        [
            whole(hidden_own),
            whole(hidden_far),
            rows_of(down_weight, FF_HALF),
            pl.BlockSpec((FF_HALF, width), lambda step, half: (1 - half[0], 0)),
        ],
        [((count, width), bf16)],
        gate_up_flops,
    )
    branch = exchange(branch.reshape(CHIPS, BLOCK, width), UNIT_CHIPS)
    branch = jnp.sum(branch.astype(f32), axis=0)
    own_tokens = lax.dynamic_slice_in_dim(tokens, unit_chip * BLOCK, BLOCK, 0)
    summed = own_tokens.astype(f32) + branch
    rows = to_all(summed.astype(bf16), UNIT_CHIPS).reshape(count, width)

    far_rows = other_core(rows)
    logit_flops = 4 * count * width * V_HALF
    raw = on_core(
        logits_kernel,
        core,
        (rows, far_rows, head_weight, head_got),
        [whole(rows), whole(far_rows), columns_of(head_weight, V_HALF), whole(head_got)],
        [((count, V_HALF + PAD), jnp.int16)],
        logit_flops,
    )
    raw, label_row = together(raw, label_row)
    raw, label_row = together(
        exchange(raw.reshape(CHIPS, BLOCK, V_HALF + PAD), WIDTH_CHIPS), plane_label_rows(label_row)
    )
    vocab_start = ((unit_chip * 2 + core) * V_HALF).astype(jnp.int32)
    packed = on_core(
        softmax_kernel,
        vocab_start,
        (raw, labels),
        [whole(raw), whole(labels)],
        [((CHIPS, BLOCK, V_HALF + PAD), bf16)],
        1000000,
    )
    packed, token_rows, label_row = together(packed, tokens, label_row)
    turned = token_rows.T
    turned_reverse = reverse_blocks(token_rows).T
    packed_own, turned_own, turned_far, label_row = together(
        exchange(packed, WIDTH_CHIPS),
        jnp.where(core == 0, turned, turned_reverse),
        jnp.where(core == 0, turned_reverse, turned),
        own_label_rows(label_row),
    )
    label_row = label_row.astype(f32)
    packed_own = packed_own.reshape(count, V_HALF + PAD)
    packed_far = other_core(packed_own)
    packed = on_core(
        pull_back,
        core,
        (packed_own, packed_far, head_weight, head_weight),
        [
            whole(packed_own),
            whole(packed_far),
            pl.BlockSpec((width, V_HALF), lambda step, half: (0, half[0])),
            pl.BlockSpec((width, V_HALF), lambda step, half: (0, 1 - half[0])),
        ],
        [((count, width + PAD), bf16)],
        logit_flops,
    )
    packed = exchange(packed.reshape(CHIPS, BLOCK, width + PAD), UNIT_CHIPS)
    stats = from_three(packed[:, :, width:], N_STATS)
    row_top = jnp.max(stats[:, :, 0:1], axis=0, keepdims=True)
    weight = jnp.exp(stats[:, :, 0:1] - row_top)
    weight = weight / jnp.sum(weight * stats[:, :, 2:3], axis=0, keepdims=True)
    pulled = jnp.sum(weight * packed[:, :, :width].astype(f32), axis=0)
    pull = jnp.sum(weight * stats[:, :, 3:4], axis=0)
    inv_rms = stats[0, :, 1:2]
    scaled = summed * inv_rms
    dsummed = []
    for which in range(2):
        label_logit = jnp.sum(stats[:, :, 4 + 2 * which : 5 + 2 * which], axis=0)
        rest = jnp.sum(weight * stats[:, :, 5 + 2 * which : 6 + 2 * which], axis=0)
        dnormed = pulled - (1.0 - rest) * label_row[:, which * width : (which + 1) * width]
        mean = (pull - (1.0 - rest) * label_logit) / D
        dsummed.append((inv_rms * (dnormed - scaled * mean)).astype(bf16))
    dsummed = to_all(jnp.concatenate(dsummed, axis=1), UNIT_CHIPS).reshape(count, 2 * width)

    far_dsummed = other_core(dsummed)
    dhidden = on_core(
        back_kernel,
        core,
        (dsummed, far_dsummed, down_weight, down_got),
        [whole(dsummed), whole(far_dsummed), rows_of(down_weight, FF_HALF), whole(down_got)],
        [((count, 2 * FF_HALF), bf16)],
        2 * gate_up_flops,
    )
    dhidden = exchange(dhidden.reshape(CHIPS, BLOCK, 2 * FF_HALF), WIDTH_CHIPS)
    dhidden = jnp.sum(dhidden.astype(f32), axis=0)
    cot = (dhidden * jnp.concatenate([silu_gate, silu_gate], axis=1)).astype(bf16)
    cot_own = to_all(cot, WIDTH_CHIPS).reshape(count, 2 * FF_HALF)
    cot_far = other_core(cot_own)
    done = sophia_half(core, turned_own, cot_own, up_moment, up_curvature, ())
    return tuple(sophia_half(far, turned_far, cot_far, up_moment, up_curvature, done))


def solution(mesh):
    fine = Mesh(mesh.devices.reshape(2, 4, 2, 4, 2), ("xl", "y", "core", "z", "xh"))
    dp = ("xl", "y", "core")
    tensor = ("z", "xh")
    both = P(dp, tensor)
    placed = (P(None, dp), both, both, P(tensor, dp), both, both, both, P(dp), P(dp))
    return jax.shard_map(
        on_device,
        mesh=fine,
        in_specs=placed,
        out_specs=(both, both, both),
        check_vma=False,
    )
```

```python
import itertools

import jax
import jax.numpy as jnp
from jax import lax
from jax.experimental import pallas as pl
from jax.experimental.pallas import tpu as pltpu
from jax.sharding import Mesh, PartitionSpec as P

D = 8192
FF_HALF = 896
V_HALF = 1024
BLOCK = 64
CHIPS = 8
PAD = 128
N_STATS = 8
STEP = 16384.0
TINY = 1e-30

beta_one = 0.965
beta_two = 0.95
rho_scale = 0.05
eps_norm = 1e-05

WIDTH_CHIPS = ("xl", "y")
UNIT_CHIPS = ("z", "xh")
MESH_SIZES = {"xl": 2, "y": 4, "core": 2, "z": 4, "xh": 2}
f32 = jnp.float32
bf16 = jnp.bfloat16
VMEM_LIMIT = 24 * 1024 * 1024


def other_core(value):
    return lax.ppermute(value, "core", [(0, 1), (1, 0)])


def partners(axes):
    names = tuple(MESH_SIZES)
    places = list(itertools.product(*(range(size) for size in MESH_SIZES.values())))
    groups = {}
    for number, place in enumerate(places):
        fixed = tuple(value for name, value in zip(names, place) if name not in axes)
        groups.setdefault(fixed, []).append(number)
    core = names.index("core")
    return [members[::-1] if places[members[0]][core] else members for members in groups.values()]


def exchange(blocks, axes):
    return lax.all_to_all(
        blocks, tuple(MESH_SIZES), split_axis=0, concat_axis=0, tiled=True, axis_index_groups=partners(axes)
    )


def to_all(block, axes):
    copies = jnp.broadcast_to(block[None], (CHIPS,) + block.shape)
    return exchange(copies, axes)


def block_rows(block):
    return slice(block * BLOCK, (block + 1) * BLOCK)


def join_cores(own, far):
    return jnp.concatenate(
        [own[block_rows(block)] + far[block_rows(CHIPS - 1 - block)] for block in range(CHIPS)], axis=0
    )


def reverse_rows(rows):
    return jnp.concatenate([rows[block_rows(CHIPS - 1 - block)] for block in range(CHIPS)], axis=0)


def reverse_blocks(rows):
    return rows.reshape((CHIPS, BLOCK) + rows.shape[1:])[::-1].reshape(rows.shape)


def together(*values):
    return lax.optimization_barrier(values)


def dot(left, right):
    return jnp.dot(left, right, preferred_element_type=f32)


def dot_rows(left, right):
    return lax.dot_general(left, right, (((1,), (1,)), ((), ())), preferred_element_type=f32)


def from_three(parts, count):
    parts = parts.astype(f32)
    return parts[..., :count] + parts[..., count : 2 * count] + parts[..., 2 * count : 3 * count]


def whole(array):
    return pl.BlockSpec(array.shape, lambda step, half: (0,) * array.ndim)


def columns_of(array, count):
    return pl.BlockSpec((array.shape[0], count), lambda step, half: (0, half[0]))


def rows_of(array, count):
    return pl.BlockSpec((count, array.shape[1]), lambda step, half: (half[0], 0))


def on_core(kernel, half, operands, specs, outs, flops, limit=VMEM_LIMIT):
    size = sum(operand.size * operand.dtype.itemsize for operand in operands)
    results = pl.pallas_call(
        kernel,
        out_shape=tuple(jax.ShapeDtypeStruct(shape, dtype) for shape, dtype in outs),
        grid_spec=pltpu.PrefetchScalarGridSpec(
            num_scalar_prefetch=1,
            grid=(1,),
            in_specs=specs,
            out_specs=tuple(whole(jax.ShapeDtypeStruct(*out)) for out in outs),
        ),
        compiler_params=pltpu.CompilerParams(vmem_limit_bytes=limit),
        cost_estimate=pl.CostEstimate(flops=flops, bytes_accessed=size, transcendentals=0),
    )(half.reshape(1), *operands)
    return results if len(outs) > 1 else results[0]


def gate_up_own(half_ref, tokens, gate, up, got_gate, got_up, labels, out):
    core = half_ref[0]
    gate_sum = (dot(tokens[...], gate[...]) + got_gate[...].astype(f32)).astype(bf16)
    up_sum = (dot(tokens[...], up[...]) + got_up[...].astype(f32)).astype(bf16)
    for block in range(CHIPS):
        place = block + core * (CHIPS - 1 - 2 * block)
        rows = pl.ds(pl.multiple_of(place * BLOCK, BLOCK), BLOCK)
        out[rows, :FF_HALF] = gate_sum[block_rows(block)]
        out[rows, FF_HALF : 2 * FF_HALF] = up_sum[block_rows(block)]
        out[rows, 2 * FF_HALF :] = labels[...]


def branch_kernel(half_ref, own, far, down_own, down_far, out):
    out[...] = join_cores(dot(own[...], down_own[...]), dot(far[...], down_far[...])).astype(bf16)


def hidden_kernel(half_ref, both, hidden, silu_out):
    gate = jnp.zeros((BLOCK, FF_HALF), f32)
    upper = jnp.zeros((BLOCK, FF_HALF), f32)
    for chip in range(CHIPS):
        gate = gate + both[chip, :, :FF_HALF].astype(f32)
        upper = upper + both[chip, :, FF_HALF : 2 * FF_HALF].astype(f32)
    silu_gate = gate / (1.0 + jnp.exp(-gate))
    silu_out[...] = silu_gate
    rounded = (silu_gate * upper).astype(bf16)
    for chip in range(CHIPS):
        hidden[chip] = rounded


def squares_of(rows):
    wide = rows[...].astype(f32)
    return jnp.sum(wide * wide, axis=1, keepdims=True)


def exponent_of(values):
    return jnp.ceil(jnp.log2(jnp.maximum(values, TINY)))


def logits_kernel(half_ref, rows, far_rows, head, head_got, out):
    raw = join_cores(dot(rows[...], head[...]), dot(far_rows[...], head_got[...]))
    squares = join_cores(squares_of(rows), squares_of(far_rows))
    level = exponent_of(jnp.max(jnp.abs(raw), axis=1, keepdims=True))
    out[:, :V_HALF] = jnp.round(raw * (STEP * jnp.exp2(-level))).astype(jnp.int32).astype(jnp.int16)
    square_level = exponent_of(squares)
    units = squares * (STEP * jnp.exp2(-square_level))
    high = jnp.floor(units)
    low = jnp.floor((units - high) * STEP)
    lane = lax.broadcasted_iota(jnp.int32, (rows.shape[0], PAD), 1)
    tail = jnp.where(lane == 0, level, jnp.where(lane == 1, high, jnp.where(lane == 2, low, square_level)))
    out[:, V_HALF:] = tail.astype(jnp.int32).astype(jnp.int16)


def pack_three(values):
    lane = lax.broadcasted_iota(jnp.int32, values.shape, 1)
    values = jnp.where(lane < N_STATS, values, 0.0)
    high = values.astype(bf16)
    rest = values - high.astype(f32)
    middle = rest.astype(bf16)
    low = (rest - middle.astype(f32)).astype(bf16)
    row = lax.broadcasted_iota(jnp.int32, (PAD, PAD), 0)
    lane = lax.broadcasted_iota(jnp.int32, (PAD, PAD), 1)
    by_one = (lane == row + N_STATS).astype(f32).astype(bf16)
    by_two = (lane == row + 2 * N_STATS).astype(f32).astype(bf16)
    return (high.astype(f32) + dot(middle, by_one) + dot(low, by_two)).astype(bf16)


def softmax_kernel(start_ref, raw, labels, out):
    total = jnp.zeros((BLOCK, V_HALF), f32)
    squares = jnp.zeros((BLOCK, 1), f32)
    for chip in range(CHIPS):
        tail = raw[chip, :, V_HALF:].astype(jnp.int32).astype(f32)
        scale = jnp.exp2(tail[:, 0:1]) / STEP
        total = total + raw[chip, :, :V_HALF].astype(jnp.int32).astype(f32) * scale
        square_scale = jnp.exp2(tail[:, 3:4]) / STEP
        squares = squares + (tail[:, 1:2] + tail[:, 2:3] / STEP) * square_scale
    inv_rms = lax.rsqrt(squares / D + eps_norm)
    logits = total * inv_rms
    top = jnp.max(logits, axis=1, keepdims=True)
    exp_terms = jnp.exp(logits - top)
    short = exp_terms.astype(bf16)
    rounded = short.astype(f32)
    ids = start_ref[0] + lax.broadcasted_iota(jnp.int32, (BLOCK, V_HALF), 1)
    stats = [
        top,
        inv_rms,
        jnp.sum(exp_terms, axis=1, keepdims=True),
        jnp.sum(rounded * logits, axis=1, keepdims=True),
    ]
    for which in range(2):
        hot = labels[:, which : which + 1] == ids
        stats.append(jnp.sum(jnp.where(hot, logits, 0.0), axis=1, keepdims=True))
        stats.append(jnp.sum(jnp.where(hot, exp_terms - rounded, 0.0), axis=1, keepdims=True))
    lane = lax.broadcasted_iota(jnp.int32, (BLOCK, PAD), 1)
    table = jnp.zeros((BLOCK, PAD), f32)
    for place, value in enumerate(stats):
        table = jnp.where(lane == place, value, table)
    packed = pack_three(table)
    for chip in range(CHIPS):
        out[chip, :, :V_HALF] = short
        out[chip, :, V_HALF:] = packed


def pull_back(half_ref, own, far, head_own, head_far, out):
    count = own.shape[0]
    row = lax.broadcasted_iota(jnp.int32, (PAD, PAD), 0)
    lane = lax.broadcasted_iota(jnp.int32, (PAD, PAD), 1)
    gather = ((row % N_STATS == lane) & (row < 3 * N_STATS)).astype(f32).astype(bf16)
    stats_own = dot(own[:, V_HALF:], gather)
    stats_far = reverse_rows(dot(far[:, V_HALF:], gather))
    top = jnp.maximum(stats_own[:, 0:1], stats_far[:, 0:1])
    scale_own = jnp.exp(stats_own[:, 0:1] - top)
    scale_far = jnp.exp(stats_far[:, 0:1] - top)
    pulled = scale_own * dot_rows(own[:, :V_HALF], head_own[...])
    pulled = pulled + scale_far * reverse_rows(dot_rows(far[:, :V_HALF], head_far[...]))
    width = pulled.shape[1]
    out[:, :width] = pulled.astype(bf16)
    lane = lax.broadcasted_iota(jnp.int32, (count, PAD), 1)
    is_sum = (lane == 2) | (lane == 3) | (lane == 5) | (lane == 7)
    both = jnp.where(is_sum, scale_own * stats_own + scale_far * stats_far, stats_own + stats_far)
    both = jnp.where(lane == 0, top, jnp.where(lane == 1, stats_own, both))
    out[:, width:] = pack_three(both)


def back_kernel(half_ref, dsummed, far_dsummed, down, down_got, out):
    width = down.shape[1]
    for which in range(2):
        place = slice(which * width, (which + 1) * width)
        part = join_cores(dot_rows(dsummed[:, place], down[...]), dot_rows(far_dsummed[:, place], down_got[...]))
        out[:, which * FF_HALF : (which + 1) * FF_HALF] = part.astype(bf16)


def step_kernel(half_ref, turned, cot, moment_ref, curve_ref, *rest):
    new_moment, new_curve, update = rest[-3:]
    grad_true = dot(turned[...], cot[:, :FF_HALF])
    grad_sampled = dot(turned[...], cot[:, FF_HALF:])
    moment = beta_one * moment_ref[...] + (1.0 - beta_one) * grad_true
    curve = beta_two * curve_ref[...] + (1.0 - beta_two) * grad_sampled * grad_sampled
    new_moment[...] = moment
    new_curve[...] = curve
    update[...] = jnp.clip(moment / (rho_scale * curve), -1.0, 1.0)


def sophia_half(half, turned, cot, moment, curve, done):
    tall = 128
    rows, count = turned.shape
    big = pl.BlockSpec((tall, FF_HALF), lambda step, half: (step, half[0]))
    shape = jax.ShapeDtypeStruct(moment.shape, f32)
    kept = [pl.BlockSpec(memory_space=pl.ANY) for _ in done]
    return pl.pallas_call(
        step_kernel,
        out_shape=(shape, shape, shape),
        grid_spec=pltpu.PrefetchScalarGridSpec(
            num_scalar_prefetch=1,
            grid=(rows // tall,),
            in_specs=[
                pl.BlockSpec((tall, count), lambda step, half: (step, 0)),
                whole(cot),
                big,
                big,
            ]
            + kept,
            out_specs=(big, big, big),
        ),
        input_output_aliases={5 + which: which for which in range(len(done))},
        compiler_params=pltpu.CompilerParams(vmem_limit_bytes=VMEM_LIMIT),
        cost_estimate=pl.CostEstimate(flops=950000000, bytes_accessed=11000000, transcendentals=0),
    )(half.reshape(1), turned, cot, moment, curve, *done)


def own_part(array, index, axis):
    keep = lax.dynamic_index_in_dim(array, index, axis, keepdims=False)
    send = lax.dynamic_index_in_dim(array, 1 - index, axis, keepdims=False)
    return keep, send


def label_parts(labels, head_weight, unit_chip):
    ids = unit_chip * (2 * V_HALF) + lax.broadcasted_iota(jnp.int32, (1, 2 * V_HALF), 1)
    parts = []
    for which in range(2):
        hot = (labels[:, which : which + 1] == ids).astype(bf16)
        parts.append(dot_rows(hot, head_weight).astype(bf16))
    return plane_parts(jnp.concatenate(parts, axis=1).reshape(4, 2, BLOCK, -1))


def plane_parts(rows):
    z = lax.axis_index("z")
    return [lax.dynamic_index_in_dim(rows, (z + shift) % 4, 0, keepdims=False) for shift in range(4)]


def along_z(value, shift):
    return lax.ppermute(value, "z", [(place, (place + shift) % 4) for place in range(4)])


def own_label_rows(rows):
    keep, send = own_part(rows, lax.axis_index("xh"), 0)
    return keep + lax.ppermute(send, "xh", [(0, 1), (1, 0)])


def on_device(
    tokens,
    gate_weight,
    up_weight,
    down_weight,
    head_weight,
    up_moment,
    up_curvature,
    true_labels,
    sampled_labels,
):
    core = lax.axis_index("core").astype(jnp.int32)
    far = 1 - core
    unit_chip = lax.axis_index(UNIT_CHIPS)
    count, width = tokens.shape

    labels = jnp.stack([true_labels, sampled_labels], axis=1)
    far_labels = other_core(labels)
    labels = jnp.where(
        core == 0,
        jnp.concatenate([labels, far_labels], axis=0),
        jnp.concatenate([far_labels, labels], axis=0),
    )
    digits = jnp.concatenate([labels // PAD, labels % PAD], axis=1).astype(bf16)
    digits = jnp.pad(digits, ((0, 0), (0, PAD - 4)))

    w_specs = [whole(tokens), columns_of(gate_weight, FF_HALF), columns_of(up_weight, FF_HALF)]
    gate_up_flops = 4 * count * width * FF_HALF
    far_gate = lax.dynamic_slice_in_dim(gate_weight, far * FF_HALF, FF_HALF, 1)
    far_up = lax.dynamic_slice_in_dim(up_weight, far * FF_HALF, FF_HALF, 1)
    got_gate = other_core(dot(tokens, far_gate).astype(bf16))
    got_up = other_core(dot(tokens, far_up).astype(bf16))
    both = on_core(
        gate_up_own,
        core,
        (tokens, gate_weight, up_weight, got_gate, got_up, digits),
        w_specs + [whole(got_gate), whole(got_up), whole(digits)],
        [((count, 2 * FF_HALF + PAD), bf16)],
        gate_up_flops,
        60 * 1024 * 1024,
    )
    head_send = lax.dynamic_slice_in_dim(head_weight, far * V_HALF, V_HALF, 1)
    down_send = lax.dynamic_slice_in_dim(down_weight, far * FF_HALF, FF_HALF, 0)
    both, head_send, down_send = together(both, head_send, down_send)
    both, head_got, down_got = together(
        exchange(both.reshape(CHIPS, BLOCK, 2 * FF_HALF + PAD), WIDTH_CHIPS),
        other_core(head_send),
        other_core(down_send),
    )
    hidden, silu_gate = on_core(
        hidden_kernel,
        core,
        (both,),
        [whole(both)],
        [((CHIPS, BLOCK, FF_HALF), bf16), ((BLOCK, FF_HALF), f32)],
        1000000,
    )

    hidden, digits = together(hidden, both)
    digits = digits[:, :, 2 * FF_HALF : 2 * FF_HALF + 4].astype(jnp.int32)
    all_labels = digits[:, :, :2] * PAD + digits[:, :, 2:]
    all_labels = jnp.where(core == 0, all_labels, all_labels[::-1]).reshape(count, 2)
    width_chip = lax.axis_index(WIDTH_CHIPS)
    hidden_own, parts, labels = together(
        exchange(hidden, WIDTH_CHIPS),
        label_parts(all_labels, head_weight, unit_chip),
        lax.dynamic_slice_in_dim(all_labels, width_chip * BLOCK, BLOCK, 0),
    )
    hidden_own = hidden_own.reshape(count, FF_HALF)
    hidden_far = other_core(hidden_own)
    branch = on_core(
        branch_kernel,
        core,
        (hidden_own, hidden_far, down_weight, down_weight),
        [
            whole(hidden_own),
            whole(hidden_far),
            rows_of(down_weight, FF_HALF),
            pl.BlockSpec((FF_HALF, width), lambda step, half: (1 - half[0], 0)),
        ],
        [((count, width), bf16)],
        gate_up_flops,
    )
    branch, parts[1] = together(branch, parts[1])
    branch, parts[1] = together(
        exchange(branch.reshape(CHIPS, BLOCK, width), UNIT_CHIPS), along_z(parts[1], 1)
    )
    branch = jnp.sum(branch.astype(f32), axis=0)
    own_tokens = lax.dynamic_slice_in_dim(tokens, unit_chip * BLOCK, BLOCK, 0)
    summed = own_tokens.astype(f32) + branch
    rows = jnp.broadcast_to(summed.astype(bf16)[None], (CHIPS, BLOCK, width))
    rows, parts[3] = together(rows, parts[3])
    rows, parts[3] = together(exchange(rows, UNIT_CHIPS), along_z(parts[3], 3))
    rows = rows.reshape(count, width)

    far_rows = other_core(rows)
    logit_flops = 4 * count * width * V_HALF
    raw = on_core(
        logits_kernel,
        core,
        (rows, far_rows, head_weight, head_got),
        [whole(rows), whole(far_rows), columns_of(head_weight, V_HALF), whole(head_got)],
        [((count, V_HALF + PAD), jnp.int16)],
        logit_flops,
    )
    raw, parts[2] = together(raw, parts[2])
    raw, parts[2] = together(
        exchange(raw.reshape(CHIPS, BLOCK, V_HALF + PAD), WIDTH_CHIPS), along_z(parts[2], 2)
    )
    vocab_start = ((unit_chip * 2 + core) * V_HALF).astype(jnp.int32)
    packed = on_core(
        softmax_kernel,
        vocab_start,
        (raw, labels),
        [whole(raw), whole(labels)],
        [((CHIPS, BLOCK, V_HALF + PAD), bf16)],
        1000000,
    )
    packed, parts = together(packed, parts)
    packed_own, label_row = together(
        exchange(packed, WIDTH_CHIPS), own_label_rows(parts[0] + parts[1] + parts[2] + parts[3])
    )
    label_row = label_row.astype(f32)
    packed_own = packed_own.reshape(count, V_HALF + PAD)
    packed_far = other_core(packed_own)
    packed = on_core(
        pull_back,
        core,
        (packed_own, packed_far, head_weight, head_weight),
        [
            whole(packed_own),
            whole(packed_far),
            pl.BlockSpec((width, V_HALF), lambda step, half: (0, half[0])),
            pl.BlockSpec((width, V_HALF), lambda step, half: (0, 1 - half[0])),
        ],
        [((count, width + PAD), bf16)],
        logit_flops,
    )
    packed = exchange(packed.reshape(CHIPS, BLOCK, width + PAD), UNIT_CHIPS)
    stats = from_three(packed[:, :, width:], N_STATS)
    row_top = jnp.max(stats[:, :, 0:1], axis=0, keepdims=True)
    weight = jnp.exp(stats[:, :, 0:1] - row_top)
    weight = weight / jnp.sum(weight * stats[:, :, 2:3], axis=0, keepdims=True)
    pulled = jnp.sum(weight * packed[:, :, :width].astype(f32), axis=0)
    pull = jnp.sum(weight * stats[:, :, 3:4], axis=0)
    inv_rms = stats[0, :, 1:2]
    scaled = summed * inv_rms
    dsummed = []
    for which in range(2):
        label_logit = jnp.sum(stats[:, :, 4 + 2 * which : 5 + 2 * which], axis=0)
        rest = jnp.sum(weight * stats[:, :, 5 + 2 * which : 6 + 2 * which], axis=0)
        dnormed = pulled - (1.0 - rest) * label_row[:, which * width : (which + 1) * width]
        mean = (pull - (1.0 - rest) * label_logit) / D
        dsummed.append((inv_rms * (dnormed - scaled * mean)).astype(bf16))
    dsummed = to_all(jnp.concatenate(dsummed, axis=1), UNIT_CHIPS).reshape(count, 2 * width)

    far_dsummed = other_core(dsummed)
    dhidden = on_core(
        back_kernel,
        core,
        (dsummed, far_dsummed, down_weight, down_got),
        [whole(dsummed), whole(far_dsummed), rows_of(down_weight, FF_HALF), whole(down_got)],
        [((count, 2 * FF_HALF), bf16)],
        2 * gate_up_flops,
    )
    dhidden, token_rows = together(dhidden, tokens)
    turned = token_rows.T
    turned_reverse = reverse_blocks(token_rows).T
    dhidden, turned_own, turned_far = together(
        exchange(dhidden.reshape(CHIPS, BLOCK, 2 * FF_HALF), WIDTH_CHIPS),
        jnp.where(core == 0, turned, turned_reverse),
        jnp.where(core == 0, turned_reverse, turned),
    )
    dhidden = jnp.sum(dhidden.astype(f32), axis=0)
    cot = (dhidden * jnp.concatenate([silu_gate, silu_gate], axis=1)).astype(bf16)
    cot_own = to_all(cot, WIDTH_CHIPS).reshape(count, 2 * FF_HALF)
    cot_far = other_core(cot_own)
    done = sophia_half(core, turned_own, cot_own, up_moment, up_curvature, ())
    return tuple(sophia_half(far, turned_far, cot_far, up_moment, up_curvature, done))


def solution(mesh):
    fine = Mesh(mesh.devices.reshape(2, 4, 2, 4, 2), ("xl", "y", "core", "z", "xh"))
    dp = ("xl", "y", "core")
    tensor = ("z", "xh")
    both = P(dp, tensor)
    placed = (P(None, dp), both, both, P(tensor, dp), both, both, both, P(dp), P(dp))
    return jax.shard_map(
        on_device,
        mesh=fine,
        in_specs=placed,
        out_specs=(both, both, both),
        check_vma=False,
    )
```

```python
import itertools

import jax
import jax.numpy as jnp
from jax import lax
from jax.experimental import pallas as pl
from jax.experimental.pallas import tpu as pltpu
from jax.sharding import Mesh, PartitionSpec as P

D = 8192
FF_HALF = 896
V_HALF = 1024
BLOCK = 64
CHIPS = 8
PAD = 128
N_STATS = 8
STEP = 16384.0
TINY = 1e-30

beta_one = 0.965
beta_two = 0.95
rho_scale = 0.05
eps_norm = 1e-05

WIDTH_CHIPS = ("xl", "y")
UNIT_CHIPS = ("z", "xh")
MESH_SIZES = {"xl": 2, "y": 4, "core": 2, "z": 4, "xh": 2}
f32 = jnp.float32
bf16 = jnp.bfloat16
VMEM_LIMIT = 24 * 1024 * 1024


def other_core(value):
    return lax.ppermute(value, "core", [(0, 1), (1, 0)])


def partners(axes):
    names = tuple(MESH_SIZES)
    places = list(itertools.product(*(range(size) for size in MESH_SIZES.values())))
    groups = {}
    for number, place in enumerate(places):
        fixed = tuple(value for name, value in zip(names, place) if name not in axes)
        groups.setdefault(fixed, []).append(number)
    core = names.index("core")
    return [members[::-1] if places[members[0]][core] else members for members in groups.values()]


def exchange(blocks, axes):
    return lax.all_to_all(
        blocks, tuple(MESH_SIZES), split_axis=0, concat_axis=0, tiled=True, axis_index_groups=partners(axes)
    )


def to_all(block, axes):
    copies = jnp.broadcast_to(block[None], (CHIPS,) + block.shape)
    return exchange(copies, axes)


def block_rows(block):
    return slice(block * BLOCK, (block + 1) * BLOCK)


def join_cores(own, far):
    return jnp.concatenate(
        [own[block_rows(block)] + far[block_rows(CHIPS - 1 - block)] for block in range(CHIPS)], axis=0
    )


def reverse_rows(rows):
    return jnp.concatenate([rows[block_rows(CHIPS - 1 - block)] for block in range(CHIPS)], axis=0)


def reverse_blocks(rows):
    return rows.reshape((CHIPS, BLOCK) + rows.shape[1:])[::-1].reshape(rows.shape)


def together(*values):
    return lax.optimization_barrier(values)


def dot(left, right):
    return jnp.dot(left, right, preferred_element_type=f32)


def dot_rows(left, right):
    return lax.dot_general(left, right, (((1,), (1,)), ((), ())), preferred_element_type=f32)


def from_three(parts, count):
    parts = parts.astype(f32)
    return parts[..., :count] + parts[..., count : 2 * count] + parts[..., 2 * count : 3 * count]


def whole(array):
    return pl.BlockSpec(array.shape, lambda step, half: (0,) * array.ndim)


def columns_of(array, count):
    return pl.BlockSpec((array.shape[0], count), lambda step, half: (0, half[0]))


def rows_of(array, count):
    return pl.BlockSpec((count, array.shape[1]), lambda step, half: (half[0], 0))


def on_core(kernel, half, operands, specs, outs, flops, limit=VMEM_LIMIT):
    size = sum(operand.size * operand.dtype.itemsize for operand in operands)
    results = pl.pallas_call(
        kernel,
        out_shape=tuple(jax.ShapeDtypeStruct(shape, dtype) for shape, dtype in outs),
        grid_spec=pltpu.PrefetchScalarGridSpec(
            num_scalar_prefetch=1,
            grid=(1,),
            in_specs=specs,
            out_specs=tuple(whole(jax.ShapeDtypeStruct(*out)) for out in outs),
        ),
        compiler_params=pltpu.CompilerParams(vmem_limit_bytes=limit),
        cost_estimate=pl.CostEstimate(flops=flops, bytes_accessed=size, transcendentals=0),
    )(half.reshape(1), *operands)
    return results if len(outs) > 1 else results[0]


def gate_up_own(half_ref, tokens, gate, up, got_gate, got_up, labels, out):
    core = half_ref[0]
    gate_sum = (dot(tokens[...], gate[...]) + got_gate[...].astype(f32)).astype(bf16)
    up_sum = (dot(tokens[...], up[...]) + got_up[...].astype(f32)).astype(bf16)
    for block in range(CHIPS):
        place = block + core * (CHIPS - 1 - 2 * block)
        rows = pl.ds(pl.multiple_of(place * BLOCK, BLOCK), BLOCK)
        out[rows, :FF_HALF] = gate_sum[block_rows(block)]
        out[rows, FF_HALF : 2 * FF_HALF] = up_sum[block_rows(block)]
        out[rows, 2 * FF_HALF :] = labels[...]


def branch_kernel(half_ref, own, far, down_own, down_far, out):
    out[...] = join_cores(dot(own[...], down_own[...]), dot(far[...], down_far[...])).astype(bf16)


def hidden_kernel(half_ref, both, hidden, silu_out):
    gate = jnp.zeros((BLOCK, FF_HALF), f32)
    upper = jnp.zeros((BLOCK, FF_HALF), f32)
    for chip in range(CHIPS):
        gate = gate + both[chip, :, :FF_HALF].astype(f32)
        upper = upper + both[chip, :, FF_HALF : 2 * FF_HALF].astype(f32)
    silu_gate = gate / (1.0 + jnp.exp(-gate))
    silu_out[...] = silu_gate
    rounded = (silu_gate * upper).astype(bf16)
    for chip in range(CHIPS):
        hidden[chip] = rounded


def squares_of(rows):
    wide = rows[...].astype(f32)
    return jnp.sum(wide * wide, axis=1, keepdims=True)


def exponent_of(values):
    return jnp.ceil(jnp.log2(jnp.maximum(values, TINY)))


def logits_kernel(half_ref, rows, far_rows, head, head_got, out):
    raw = join_cores(dot(rows[...], head[...]), dot(far_rows[...], head_got[...]))
    squares = join_cores(squares_of(rows), squares_of(far_rows))
    level = exponent_of(jnp.max(jnp.abs(raw), axis=1, keepdims=True))
    out[:, :V_HALF] = jnp.round(raw * (STEP * jnp.exp2(-level))).astype(jnp.int32).astype(jnp.int16)
    square_level = exponent_of(squares)
    units = squares * (STEP * jnp.exp2(-square_level))
    high = jnp.floor(units)
    low = jnp.floor((units - high) * STEP)
    lane = lax.broadcasted_iota(jnp.int32, (rows.shape[0], PAD), 1)
    tail = jnp.where(lane == 0, level, jnp.where(lane == 1, high, jnp.where(lane == 2, low, square_level)))
    out[:, V_HALF:] = tail.astype(jnp.int32).astype(jnp.int16)


def pack_three(values):
    lane = lax.broadcasted_iota(jnp.int32, values.shape, 1)
    values = jnp.where(lane < N_STATS, values, 0.0)
    high = values.astype(bf16)
    rest = values - high.astype(f32)
    middle = rest.astype(bf16)
    low = (rest - middle.astype(f32)).astype(bf16)
    row = lax.broadcasted_iota(jnp.int32, (PAD, PAD), 0)
    lane = lax.broadcasted_iota(jnp.int32, (PAD, PAD), 1)
    by_one = (lane == row + N_STATS).astype(f32).astype(bf16)
    by_two = (lane == row + 2 * N_STATS).astype(f32).astype(bf16)
    return (high.astype(f32) + dot(middle, by_one) + dot(low, by_two)).astype(bf16)


def softmax_kernel(start_ref, raw, labels, out):
    total = jnp.zeros((BLOCK, V_HALF), f32)
    squares = jnp.zeros((BLOCK, 1), f32)
    for chip in range(CHIPS):
        tail = raw[chip, :, V_HALF:].astype(jnp.int32).astype(f32)
        scale = jnp.exp2(tail[:, 0:1]) / STEP
        total = total + raw[chip, :, :V_HALF].astype(jnp.int32).astype(f32) * scale
        square_scale = jnp.exp2(tail[:, 3:4]) / STEP
        squares = squares + (tail[:, 1:2] + tail[:, 2:3] / STEP) * square_scale
    inv_rms = lax.rsqrt(squares / D + eps_norm)
    logits = total * inv_rms
    top = jnp.max(logits, axis=1, keepdims=True)
    exp_terms = jnp.exp(logits - top)
    short = exp_terms.astype(bf16)
    rounded = short.astype(f32)
    ids = start_ref[0] + lax.broadcasted_iota(jnp.int32, (BLOCK, V_HALF), 1)
    stats = [
        top,
        inv_rms,
        jnp.sum(exp_terms, axis=1, keepdims=True),
        jnp.sum(rounded * logits, axis=1, keepdims=True),
    ]
    for which in range(2):
        hot = labels[:, which : which + 1] == ids
        stats.append(jnp.sum(jnp.where(hot, logits, 0.0), axis=1, keepdims=True))
        stats.append(jnp.sum(jnp.where(hot, exp_terms - rounded, 0.0), axis=1, keepdims=True))
    lane = lax.broadcasted_iota(jnp.int32, (BLOCK, PAD), 1)
    table = jnp.zeros((BLOCK, PAD), f32)
    for place, value in enumerate(stats):
        table = jnp.where(lane == place, value, table)
    packed = pack_three(table)
    for chip in range(CHIPS):
        out[chip, :, :V_HALF] = short
        out[chip, :, V_HALF:] = packed


def pull_back(half_ref, own, far, head_own, head_far, out):
    count = own.shape[0]
    row = lax.broadcasted_iota(jnp.int32, (PAD, PAD), 0)
    lane = lax.broadcasted_iota(jnp.int32, (PAD, PAD), 1)
    gather = ((row % N_STATS == lane) & (row < 3 * N_STATS)).astype(f32).astype(bf16)
    stats_own = dot(own[:, V_HALF:], gather)
    stats_far = reverse_rows(dot(far[:, V_HALF:], gather))
    top = jnp.maximum(stats_own[:, 0:1], stats_far[:, 0:1])
    scale_own = jnp.exp(stats_own[:, 0:1] - top)
    scale_far = jnp.exp(stats_far[:, 0:1] - top)
    pulled = scale_own * dot_rows(own[:, :V_HALF], head_own[...])
    pulled = pulled + scale_far * reverse_rows(dot_rows(far[:, :V_HALF], head_far[...]))
    width = pulled.shape[1]
    out[:, :width] = pulled.astype(bf16)
    lane = lax.broadcasted_iota(jnp.int32, (count, PAD), 1)
    is_sum = (lane == 2) | (lane == 3) | (lane == 5) | (lane == 7)
    both = jnp.where(is_sum, scale_own * stats_own + scale_far * stats_far, stats_own + stats_far)
    both = jnp.where(lane == 0, top, jnp.where(lane == 1, stats_own, both))
    out[:, width:] = pack_three(both)


def back_kernel(half_ref, dsummed, far_dsummed, down, down_got, out):
    width = down.shape[1]
    for which in range(2):
        place = slice(which * width, (which + 1) * width)
        part = join_cores(dot_rows(dsummed[:, place], down[...]), dot_rows(far_dsummed[:, place], down_got[...]))
        out[:, which * FF_HALF : (which + 1) * FF_HALF] = part.astype(bf16)


def step_kernel(half_ref, turned, cot, moment_ref, curve_ref, *rest):
    new_moment, new_curve, update = rest[-3:]
    grad_true = dot(turned[...], cot[:, :FF_HALF])
    grad_sampled = dot(turned[...], cot[:, FF_HALF:])
    moment = beta_one * moment_ref[...] + (1.0 - beta_one) * grad_true
    curve = beta_two * curve_ref[...] + (1.0 - beta_two) * grad_sampled * grad_sampled
    new_moment[...] = moment
    new_curve[...] = curve
    update[...] = jnp.clip(moment / (rho_scale * curve), -1.0, 1.0)


def sophia_half(half, turned, cot, moment, curve, done):
    tall = 128
    rows, count = turned.shape
    big = pl.BlockSpec((tall, FF_HALF), lambda step, half: (step, half[0]))
    shape = jax.ShapeDtypeStruct(moment.shape, f32)
    kept = [pl.BlockSpec(memory_space=pl.ANY) for _ in done]
    return pl.pallas_call(
        step_kernel,
        out_shape=(shape, shape, shape),
        grid_spec=pltpu.PrefetchScalarGridSpec(
            num_scalar_prefetch=1,
            grid=(rows // tall,),
            in_specs=[
                pl.BlockSpec((tall, count), lambda step, half: (step, 0)),
                whole(cot),
                big,
                big,
            ]
            + kept,
            out_specs=(big, big, big),
        ),
        input_output_aliases={5 + which: which for which in range(len(done))},
        compiler_params=pltpu.CompilerParams(vmem_limit_bytes=VMEM_LIMIT),
        cost_estimate=pl.CostEstimate(flops=950000000, bytes_accessed=11000000, transcendentals=0),
    )(half.reshape(1), turned, cot, moment, curve, *done)


def label_rows(labels, head_weight, unit_chip):
    ids = unit_chip * (2 * V_HALF) + lax.broadcasted_iota(jnp.int32, (1, 2 * V_HALF), 1)
    parts = []
    for which in range(2):
        hot = (labels[:, which : which + 1] == ids).astype(bf16)
        parts.append(dot_rows(hot, head_weight).astype(bf16))
    return jnp.concatenate(parts, axis=1)


def on_device(
    tokens,
    gate_weight,
    up_weight,
    down_weight,
    head_weight,
    up_moment,
    up_curvature,
    true_labels,
    sampled_labels,
):
    core = lax.axis_index("core").astype(jnp.int32)
    far = 1 - core
    unit_chip = lax.axis_index(UNIT_CHIPS)
    count, width = tokens.shape

    labels = jnp.stack([true_labels, sampled_labels], axis=1)
    far_labels = other_core(labels)
    labels = jnp.where(
        core == 0,
        jnp.concatenate([labels, far_labels], axis=0),
        jnp.concatenate([far_labels, labels], axis=0),
    )
    digits = jnp.concatenate([labels // PAD, labels % PAD], axis=1).astype(bf16)
    digits = jnp.pad(digits, ((0, 0), (0, PAD - 4)))

    w_specs = [whole(tokens), columns_of(gate_weight, FF_HALF), columns_of(up_weight, FF_HALF)]
    gate_up_flops = 4 * count * width * FF_HALF
    far_gate = lax.dynamic_slice_in_dim(gate_weight, far * FF_HALF, FF_HALF, 1)
    far_up = lax.dynamic_slice_in_dim(up_weight, far * FF_HALF, FF_HALF, 1)
    got_gate = other_core(dot(tokens, far_gate).astype(bf16))
    got_up = other_core(dot(tokens, far_up).astype(bf16))
    both = on_core(
        gate_up_own,
        core,
        (tokens, gate_weight, up_weight, got_gate, got_up, digits),
        w_specs + [whole(got_gate), whole(got_up), whole(digits)],
        [((count, 2 * FF_HALF + PAD), bf16)],
        gate_up_flops,
        60 * 1024 * 1024,
    )
    head_send = lax.dynamic_slice_in_dim(head_weight, far * V_HALF, V_HALF, 1)
    down_send = lax.dynamic_slice_in_dim(down_weight, far * FF_HALF, FF_HALF, 0)
    both, head_send, down_send = together(both, head_send, down_send)
    both, head_got, down_got = together(
        exchange(both.reshape(CHIPS, BLOCK, 2 * FF_HALF + PAD), WIDTH_CHIPS),
        other_core(head_send),
        other_core(down_send),
    )
    hidden, silu_gate = on_core(
        hidden_kernel,
        core,
        (both,),
        [whole(both)],
        [((CHIPS, BLOCK, FF_HALF), bf16), ((BLOCK, FF_HALF), f32)],
        1000000,
    )

    hidden, digits = together(hidden, both)
    digits = digits[:, :, 2 * FF_HALF : 2 * FF_HALF + 4].astype(jnp.int32)
    all_labels = digits[:, :, :2] * PAD + digits[:, :, 2:]
    all_labels = jnp.where(core == 0, all_labels, all_labels[::-1]).reshape(count, 2)
    width_chip = lax.axis_index(WIDTH_CHIPS)
    hidden_own, label_row, labels = together(
        exchange(hidden, WIDTH_CHIPS),
        label_rows(all_labels, head_weight, unit_chip),
        lax.dynamic_slice_in_dim(all_labels, width_chip * BLOCK, BLOCK, 0),
    )
    label_row = lax.psum_scatter(label_row, UNIT_CHIPS, scatter_dimension=0, tiled=True)
    hidden_own = hidden_own.reshape(count, FF_HALF)
    hidden_far = other_core(hidden_own)
    branch = on_core(
        branch_kernel,
        core,
        (hidden_own, hidden_far, down_weight, down_weight),
        [
            whole(hidden_own),
            whole(hidden_far),
            rows_of(down_weight, FF_HALF),
            pl.BlockSpec((FF_HALF, width), lambda step, half: (1 - half[0], 0)),
        ],
        [((count, width), bf16)],
        gate_up_flops,
    )
    branch = exchange(branch.reshape(CHIPS, BLOCK, width), UNIT_CHIPS)
    branch = jnp.sum(branch.astype(f32), axis=0)
    own_tokens = lax.dynamic_slice_in_dim(tokens, unit_chip * BLOCK, BLOCK, 0)
    summed = own_tokens.astype(f32) + branch
    rows = to_all(summed.astype(bf16), UNIT_CHIPS).reshape(count, width)

    far_rows = other_core(rows)
    logit_flops = 4 * count * width * V_HALF
    raw = on_core(
        logits_kernel,
        core,
        (rows, far_rows, head_weight, head_got),
        [whole(rows), whole(far_rows), columns_of(head_weight, V_HALF), whole(head_got)],
        [((count, V_HALF + PAD), jnp.int16)],
        logit_flops,
    )
    raw = exchange(raw.reshape(CHIPS, BLOCK, V_HALF + PAD), WIDTH_CHIPS)
    vocab_start = ((unit_chip * 2 + core) * V_HALF).astype(jnp.int32)
    packed = on_core(
        softmax_kernel,
        vocab_start,
        (raw, labels),
        [whole(raw), whole(labels)],
        [((CHIPS, BLOCK, V_HALF + PAD), bf16)],
        1000000,
    )
    packed, token_rows = together(packed, tokens)
    turned = token_rows.T
    turned_reverse = reverse_blocks(token_rows).T
    packed_own, turned_own, turned_far = together(
        exchange(packed, WIDTH_CHIPS),
        jnp.where(core == 0, turned, turned_reverse),
        jnp.where(core == 0, turned_reverse, turned),
    )
    packed_own = packed_own.reshape(count, V_HALF + PAD)
    packed_far = other_core(packed_own)
    packed = on_core(
        pull_back,
        core,
        (packed_own, packed_far, head_weight, head_weight),
        [
            whole(packed_own),
            whole(packed_far),
            pl.BlockSpec((width, V_HALF), lambda step, half: (0, half[0])),
            pl.BlockSpec((width, V_HALF), lambda step, half: (0, 1 - half[0])),
        ],
        [((count, width + PAD), bf16)],
        logit_flops,
    )
    packed = exchange(packed.reshape(CHIPS, BLOCK, width + PAD), UNIT_CHIPS)
    packed, label_row = together(packed, label_row)
    label_row = label_row.astype(f32)
    stats = from_three(packed[:, :, width:], N_STATS)
    row_top = jnp.max(stats[:, :, 0:1], axis=0, keepdims=True)
    weight = jnp.exp(stats[:, :, 0:1] - row_top)
    weight = weight / jnp.sum(weight * stats[:, :, 2:3], axis=0, keepdims=True)
    pulled = jnp.sum(weight * packed[:, :, :width].astype(f32), axis=0)
    pull = jnp.sum(weight * stats[:, :, 3:4], axis=0)
    inv_rms = stats[0, :, 1:2]
    scaled = summed * inv_rms
    dsummed = []
    for which in range(2):
        label_logit = jnp.sum(stats[:, :, 4 + 2 * which : 5 + 2 * which], axis=0)
        rest = jnp.sum(weight * stats[:, :, 5 + 2 * which : 6 + 2 * which], axis=0)
        dnormed = pulled - (1.0 - rest) * label_row[:, which * width : (which + 1) * width]
        mean = (pull - (1.0 - rest) * label_logit) / D
        dsummed.append((inv_rms * (dnormed - scaled * mean)).astype(bf16))
    dsummed = to_all(jnp.concatenate(dsummed, axis=1), UNIT_CHIPS).reshape(count, 2 * width)

    far_dsummed = other_core(dsummed)
    dhidden = on_core(
        back_kernel,
        core,
        (dsummed, far_dsummed, down_weight, down_got),
        [whole(dsummed), whole(far_dsummed), rows_of(down_weight, FF_HALF), whole(down_got)],
        [((count, 2 * FF_HALF), bf16)],
        2 * gate_up_flops,
    )
    dhidden = exchange(dhidden.reshape(CHIPS, BLOCK, 2 * FF_HALF), WIDTH_CHIPS)
    dhidden = jnp.sum(dhidden.astype(f32), axis=0)
    cot = (dhidden * jnp.concatenate([silu_gate, silu_gate], axis=1)).astype(bf16)
    cot_own = to_all(cot, WIDTH_CHIPS).reshape(count, 2 * FF_HALF)
    cot_far = other_core(cot_own)
    done = sophia_half(core, turned_own, cot_own, up_moment, up_curvature, ())
    return tuple(sophia_half(far, turned_far, cot_far, up_moment, up_curvature, done))


def solution(mesh):
    fine = Mesh(mesh.devices.reshape(2, 4, 2, 4, 2), ("xl", "y", "core", "z", "xh"))
    dp = ("xl", "y", "core")
    tensor = ("z", "xh")
    both = P(dp, tensor)
    placed = (P(None, dp), both, both, P(tensor, dp), both, both, both, P(dp), P(dp))
    return jax.shard_map(
        on_device,
        mesh=fine,
        in_specs=placed,
        out_specs=(both, both, both),
        check_vma=False,
    )
```

```python
import itertools

import jax
import jax.numpy as jnp
from jax import lax
from jax.experimental import pallas as pl
from jax.experimental.pallas import tpu as pltpu
from jax.sharding import Mesh, PartitionSpec as P

D = 8192
FF_HALF = 896
V_HALF = 1024
BLOCK = 64
CHIPS = 8
PAD = 128
N_STATS = 8
STEP = 16384.0
TINY = 1e-30

beta_one = 0.965
beta_two = 0.95
rho_scale = 0.05
eps_norm = 1e-05

WIDTH_CHIPS = ("xl", "y")
UNIT_CHIPS = ("z", "xh")
MESH_SIZES = {"xl": 2, "y": 4, "core": 2, "z": 4, "xh": 2}
f32 = jnp.float32
bf16 = jnp.bfloat16
VMEM_LIMIT = 24 * 1024 * 1024


def other_core(value):
    return lax.ppermute(value, "core", [(0, 1), (1, 0)])


def partners(axes):
    names = tuple(MESH_SIZES)
    places = list(itertools.product(*(range(size) for size in MESH_SIZES.values())))
    groups = {}
    for number, place in enumerate(places):
        fixed = tuple(value for name, value in zip(names, place) if name not in axes)
        groups.setdefault(fixed, []).append(number)
    core = names.index("core")
    return [members[::-1] if places[members[0]][core] else members for members in groups.values()]


def exchange(blocks, axes):
    return lax.all_to_all(
        blocks, tuple(MESH_SIZES), split_axis=0, concat_axis=0, tiled=True, axis_index_groups=partners(axes)
    )


def to_all(block, axes):
    copies = jnp.broadcast_to(block[None], (CHIPS,) + block.shape)
    return exchange(copies, axes)


def block_rows(block):
    return slice(block * BLOCK, (block + 1) * BLOCK)


def join_cores(own, far):
    return jnp.concatenate(
        [own[block_rows(block)] + far[block_rows(CHIPS - 1 - block)] for block in range(CHIPS)], axis=0
    )


def reverse_rows(rows):
    return jnp.concatenate([rows[block_rows(CHIPS - 1 - block)] for block in range(CHIPS)], axis=0)


def reverse_blocks(rows):
    return rows.reshape((CHIPS, BLOCK) + rows.shape[1:])[::-1].reshape(rows.shape)


def together(*values):
    return lax.optimization_barrier(values)


def dot(left, right):
    return jnp.dot(left, right, preferred_element_type=f32)


def dot_rows(left, right):
    return lax.dot_general(left, right, (((1,), (1,)), ((), ())), preferred_element_type=f32)


def from_three(parts, count):
    parts = parts.astype(f32)
    return parts[..., :count] + parts[..., count : 2 * count] + parts[..., 2 * count : 3 * count]


def whole(array):
    return pl.BlockSpec(array.shape, lambda step, half: (0,) * array.ndim)


def columns_of(array, count):
    return pl.BlockSpec((array.shape[0], count), lambda step, half: (0, half[0]))


def rows_of(array, count):
    return pl.BlockSpec((count, array.shape[1]), lambda step, half: (half[0], 0))


def on_core(kernel, half, operands, specs, outs, flops, limit=VMEM_LIMIT):
    size = sum(operand.size * operand.dtype.itemsize for operand in operands)
    results = pl.pallas_call(
        kernel,
        out_shape=tuple(jax.ShapeDtypeStruct(shape, dtype) for shape, dtype in outs),
        grid_spec=pltpu.PrefetchScalarGridSpec(
            num_scalar_prefetch=1,
            grid=(1,),
            in_specs=specs,
            out_specs=tuple(whole(jax.ShapeDtypeStruct(*out)) for out in outs),
        ),
        compiler_params=pltpu.CompilerParams(vmem_limit_bytes=limit),
        cost_estimate=pl.CostEstimate(flops=flops, bytes_accessed=size, transcendentals=0),
    )(half.reshape(1), *operands)
    return results if len(outs) > 1 else results[0]


def gate_up_pack(half_ref, own_gate, own_up, got_gate, got_up, labels, out):
    core = half_ref[0]
    gate_sum = (own_gate[...] + got_gate[...].astype(f32)).astype(bf16)
    up_sum = (own_up[...] + got_up[...].astype(f32)).astype(bf16)
    for block in range(CHIPS):
        place = block + core * (CHIPS - 1 - 2 * block)
        rows = pl.ds(pl.multiple_of(place * BLOCK, BLOCK), BLOCK)
        out[rows, :FF_HALF] = gate_sum[block_rows(block)]
        out[rows, FF_HALF : 2 * FF_HALF] = up_sum[block_rows(block)]
        out[rows, 2 * FF_HALF :] = labels[...]


def branch_kernel(half_ref, own, far, down_own, down_far, out):
    out[...] = join_cores(dot(own[...], down_own[...]), dot(far[...], down_far[...])).astype(bf16)


def hidden_kernel(half_ref, both, hidden, silu_out):
    gate = jnp.zeros((BLOCK, FF_HALF), f32)
    upper = jnp.zeros((BLOCK, FF_HALF), f32)
    for chip in range(CHIPS):
        gate = gate + both[chip, :, :FF_HALF].astype(f32)
        upper = upper + both[chip, :, FF_HALF : 2 * FF_HALF].astype(f32)
    silu_gate = gate / (1.0 + jnp.exp(-gate))
    silu_out[...] = silu_gate
    rounded = (silu_gate * upper).astype(bf16)
    for chip in range(CHIPS):
        hidden[chip] = rounded


def squares_of(rows):
    wide = rows[...].astype(f32)
    return jnp.sum(wide * wide, axis=1, keepdims=True)


def exponent_of(values):
    return jnp.ceil(jnp.log2(jnp.maximum(values, TINY)))


def logits_kernel(half_ref, rows, far_rows, head, head_got, out):
    raw = join_cores(dot(rows[...], head[...]), dot(far_rows[...], head_got[...]))
    squares = join_cores(squares_of(rows), squares_of(far_rows))
    level = exponent_of(jnp.max(jnp.abs(raw), axis=1, keepdims=True))
    out[:, :V_HALF] = jnp.round(raw * (STEP * jnp.exp2(-level))).astype(jnp.int32).astype(jnp.int16)
    square_level = exponent_of(squares)
    units = squares * (STEP * jnp.exp2(-square_level))
    high = jnp.floor(units)
    low = jnp.floor((units - high) * STEP)
    lane = lax.broadcasted_iota(jnp.int32, (rows.shape[0], PAD), 1)
    tail = jnp.where(lane == 0, level, jnp.where(lane == 1, high, jnp.where(lane == 2, low, square_level)))
    out[:, V_HALF:] = tail.astype(jnp.int32).astype(jnp.int16)


def pack_three(values):
    lane = lax.broadcasted_iota(jnp.int32, values.shape, 1)
    values = jnp.where(lane < N_STATS, values, 0.0)
    high = values.astype(bf16)
    rest = values - high.astype(f32)
    middle = rest.astype(bf16)
    low = (rest - middle.astype(f32)).astype(bf16)
    row = lax.broadcasted_iota(jnp.int32, (PAD, PAD), 0)
    lane = lax.broadcasted_iota(jnp.int32, (PAD, PAD), 1)
    by_one = (lane == row + N_STATS).astype(f32).astype(bf16)
    by_two = (lane == row + 2 * N_STATS).astype(f32).astype(bf16)
    return (high.astype(f32) + dot(middle, by_one) + dot(low, by_two)).astype(bf16)


def softmax_kernel(start_ref, raw, labels, out):
    total = jnp.zeros((BLOCK, V_HALF), f32)
    squares = jnp.zeros((BLOCK, 1), f32)
    for chip in range(CHIPS):
        tail = raw[chip, :, V_HALF:].astype(jnp.int32).astype(f32)
        scale = jnp.exp2(tail[:, 0:1]) / STEP
        total = total + raw[chip, :, :V_HALF].astype(jnp.int32).astype(f32) * scale
        square_scale = jnp.exp2(tail[:, 3:4]) / STEP
        squares = squares + (tail[:, 1:2] + tail[:, 2:3] / STEP) * square_scale
    inv_rms = lax.rsqrt(squares / D + eps_norm)
    logits = total * inv_rms
    top = jnp.max(logits, axis=1, keepdims=True)
    exp_terms = jnp.exp(logits - top)
    short = exp_terms.astype(bf16)
    rounded = short.astype(f32)
    ids = start_ref[0] + lax.broadcasted_iota(jnp.int32, (BLOCK, V_HALF), 1)
    stats = [
        top,
        inv_rms,
        jnp.sum(exp_terms, axis=1, keepdims=True),
        jnp.sum(rounded * logits, axis=1, keepdims=True),
    ]
    for which in range(2):
        hot = labels[:, which : which + 1] == ids
        stats.append(jnp.sum(jnp.where(hot, logits, 0.0), axis=1, keepdims=True))
        stats.append(jnp.sum(jnp.where(hot, exp_terms - rounded, 0.0), axis=1, keepdims=True))
    lane = lax.broadcasted_iota(jnp.int32, (BLOCK, PAD), 1)
    table = jnp.zeros((BLOCK, PAD), f32)
    for place, value in enumerate(stats):
        table = jnp.where(lane == place, value, table)
    packed = pack_three(table)
    for chip in range(CHIPS):
        out[chip, :, :V_HALF] = short
        out[chip, :, V_HALF:] = packed


def pull_back(half_ref, own, far, head_own, head_far, out):
    count = own.shape[0]
    row = lax.broadcasted_iota(jnp.int32, (PAD, PAD), 0)
    lane = lax.broadcasted_iota(jnp.int32, (PAD, PAD), 1)
    gather = ((row % N_STATS == lane) & (row < 3 * N_STATS)).astype(f32).astype(bf16)
    stats_own = dot(own[:, V_HALF:], gather)
    stats_far = reverse_rows(dot(far[:, V_HALF:], gather))
    top = jnp.maximum(stats_own[:, 0:1], stats_far[:, 0:1])
    scale_own = jnp.exp(stats_own[:, 0:1] - top)
    scale_far = jnp.exp(stats_far[:, 0:1] - top)
    pulled = scale_own * dot_rows(own[:, :V_HALF], head_own[...])
    pulled = pulled + scale_far * reverse_rows(dot_rows(far[:, :V_HALF], head_far[...]))
    width = pulled.shape[1]
    out[:, :width] = pulled.astype(bf16)
    lane = lax.broadcasted_iota(jnp.int32, (count, PAD), 1)
    is_sum = (lane == 2) | (lane == 3) | (lane == 5) | (lane == 7)
    both = jnp.where(is_sum, scale_own * stats_own + scale_far * stats_far, stats_own + stats_far)
    both = jnp.where(lane == 0, top, jnp.where(lane == 1, stats_own, both))
    out[:, width:] = pack_three(both)


def back_kernel(half_ref, dsummed, far_dsummed, down, down_got, out):
    width = down.shape[1]
    for which in range(2):
        place = slice(which * width, (which + 1) * width)
        part = join_cores(dot_rows(dsummed[:, place], down[...]), dot_rows(far_dsummed[:, place], down_got[...]))
        out[:, which * FF_HALF : (which + 1) * FF_HALF] = part.astype(bf16)


def step_kernel(half_ref, turned, cot, moment_ref, curve_ref, *rest):
    new_moment, new_curve, update = rest[-3:]
    grad_true = dot(turned[...], cot[:, :FF_HALF])
    grad_sampled = dot(turned[...], cot[:, FF_HALF:])
    moment = beta_one * moment_ref[...] + (1.0 - beta_one) * grad_true
    curve = beta_two * curve_ref[...] + (1.0 - beta_two) * grad_sampled * grad_sampled
    new_moment[...] = moment
    new_curve[...] = curve
    update[...] = jnp.clip(moment / (rho_scale * curve), -1.0, 1.0)


def sophia_half(half, turned, cot, moment, curve, done):
    tall = 128
    rows, count = turned.shape
    big = pl.BlockSpec((tall, FF_HALF), lambda step, half: (step, half[0]))
    shape = jax.ShapeDtypeStruct(moment.shape, f32)
    kept = [pl.BlockSpec(memory_space=pl.ANY) for _ in done]
    return pl.pallas_call(
        step_kernel,
        out_shape=(shape, shape, shape),
        grid_spec=pltpu.PrefetchScalarGridSpec(
            num_scalar_prefetch=1,
            grid=(rows // tall,),
            in_specs=[
                pl.BlockSpec((tall, count), lambda step, half: (step, 0)),
                whole(cot),
                big,
                big,
            ]
            + kept,
            out_specs=(big, big, big),
        ),
        input_output_aliases={5 + which: which for which in range(len(done))},
        compiler_params=pltpu.CompilerParams(vmem_limit_bytes=VMEM_LIMIT),
        cost_estimate=pl.CostEstimate(flops=950000000, bytes_accessed=11000000, transcendentals=0),
    )(half.reshape(1), turned, cot, moment, curve, *done)


def own_part(array, index, axis):
    keep = lax.dynamic_index_in_dim(array, index, axis, keepdims=False)
    send = lax.dynamic_index_in_dim(array, 1 - index, axis, keepdims=False)
    return keep, send


def label_rows(labels, head_weight, unit_chip):
    ids = unit_chip * (2 * V_HALF) + lax.broadcasted_iota(jnp.int32, (1, 2 * V_HALF), 1)
    parts = []
    for which in range(2):
        hot = (labels[:, which : which + 1] == ids).astype(bf16)
        parts.append(dot_rows(hot, head_weight).astype(bf16))
    return jnp.concatenate(parts, axis=1).reshape(2, 2, 2, BLOCK, -1)


def near_label_rows(rows):
    keep, send = own_part(rows, lax.axis_index("z") % 2, 1)
    return keep + lax.ppermute(send, "z", [(0, 1), (1, 0), (2, 3), (3, 2)])


def plane_label_rows(rows):
    keep, send = own_part(rows, lax.axis_index("z") // 2, 0)
    rows = keep + lax.ppermute(send, "z", [(0, 2), (2, 0), (1, 3), (3, 1)])
    return own_part(rows, lax.axis_index("xh"), 0)


def other_plane(rows):
    return lax.ppermute(rows, "xh", [(0, 1), (1, 0)])


def on_device(
    tokens,
    gate_weight,
    up_weight,
    down_weight,
    head_weight,
    up_moment,
    up_curvature,
    true_labels,
    sampled_labels,
):
    core = lax.axis_index("core").astype(jnp.int32)
    far = 1 - core
    unit_chip = lax.axis_index(UNIT_CHIPS)
    count, width = tokens.shape

    labels = jnp.stack([true_labels, sampled_labels], axis=1)
    far_labels = other_core(labels)
    labels = jnp.where(
        core == 0,
        jnp.concatenate([labels, far_labels], axis=0),
        jnp.concatenate([far_labels, labels], axis=0),
    )
    digits = jnp.concatenate([labels // PAD, labels % PAD], axis=1).astype(bf16)
    digits = jnp.pad(digits, ((0, 0), (0, PAD - 4)))

    gate_up_flops = 4 * count * width * FF_HALF

    def gate_up(half):
        gate = lax.dynamic_slice_in_dim(gate_weight, half * FF_HALF, FF_HALF, 1)
        upper = lax.dynamic_slice_in_dim(up_weight, half * FF_HALF, FF_HALF, 1)
        return dot(tokens, gate), dot(tokens, upper)

    far_gate, far_up = gate_up(far)
    got_gate, got_up = other_core(far_gate.astype(bf16)), other_core(far_up.astype(bf16))
    own_gate, own_up = gate_up(core)
    operands = (own_gate, own_up, got_gate, got_up, digits)
    both = on_core(
        gate_up_pack,
        core,
        operands,
        [whole(operand) for operand in operands],
        [((count, 2 * FF_HALF + PAD), bf16)],
        1000000,
    )
    both, sent_head, sent_down = together(both, head_weight, down_weight)
    head_send = lax.dynamic_slice_in_dim(sent_head, far * V_HALF, V_HALF, 1)
    down_send = lax.dynamic_slice_in_dim(sent_down, far * FF_HALF, FF_HALF, 0)
    both, head_got, down_got = together(
        exchange(both.reshape(CHIPS, BLOCK, 2 * FF_HALF + PAD), WIDTH_CHIPS),
        other_core(head_send),
        other_core(down_send),
    )
    hidden, silu_gate = on_core(
        hidden_kernel,
        core,
        (both,),
        [whole(both)],
        [((CHIPS, BLOCK, FF_HALF), bf16), ((BLOCK, FF_HALF), f32)],
        1000000,
    )

    hidden, digits = together(hidden, both)
    digits = digits[:, :, 2 * FF_HALF : 2 * FF_HALF + 4].astype(jnp.int32)
    all_labels = digits[:, :, :2] * PAD + digits[:, :, 2:]
    all_labels = jnp.where(core == 0, all_labels, all_labels[::-1]).reshape(count, 2)
    width_chip = lax.axis_index(WIDTH_CHIPS)
    hidden_own, label_row, labels = together(
        exchange(hidden, WIDTH_CHIPS),
        label_rows(all_labels, head_weight, unit_chip),
        lax.dynamic_slice_in_dim(all_labels, width_chip * BLOCK, BLOCK, 0),
    )
    hidden_own = hidden_own.reshape(count, FF_HALF)
    hidden_far = other_core(hidden_own)
    branch = on_core(
        branch_kernel,
        core,
        (hidden_own, hidden_far, down_weight, down_weight),
        [
            whole(hidden_own),
            whole(hidden_far),
            rows_of(down_weight, FF_HALF),
            pl.BlockSpec((FF_HALF, width), lambda step, half: (1 - half[0], 0)),
        ],
        [((count, width), bf16)],
        gate_up_flops,
    )
    branch = exchange(branch.reshape(CHIPS, BLOCK, width), UNIT_CHIPS)
    branch = jnp.sum(branch.astype(f32), axis=0)
    own_tokens = lax.dynamic_slice_in_dim(tokens, unit_chip * BLOCK, BLOCK, 0)
    summed = own_tokens.astype(f32) + branch
    rows = to_all(summed.astype(bf16), UNIT_CHIPS).reshape(count, width)

    far_rows = other_core(rows)
    logit_flops = 4 * count * width * V_HALF
    raw = on_core(
        logits_kernel,
        core,
        (rows, far_rows, head_weight, head_got),
        [whole(rows), whole(far_rows), columns_of(head_weight, V_HALF), whole(head_got)],
        [((count, V_HALF + PAD), jnp.int16)],
        logit_flops,
    )
    raw, label_row = together(raw, label_row)
    raw, label_row = together(
        exchange(raw.reshape(CHIPS, BLOCK, V_HALF + PAD), WIDTH_CHIPS), near_label_rows(label_row)
    )
    vocab_start = ((unit_chip * 2 + core) * V_HALF).astype(jnp.int32)
    packed = on_core(
        softmax_kernel,
        vocab_start,
        (raw, labels),
        [whole(raw), whole(labels)],
        [((CHIPS, BLOCK, V_HALF + PAD), bf16)],
        1000000,
    )
    packed, token_rows, label_row = together(packed, tokens, label_row)
    turned = token_rows.T
    turned_reverse = reverse_blocks(token_rows).T
    packed_own, turned_own, turned_far, label_row = together(
        exchange(packed, WIDTH_CHIPS),
        jnp.where(core == 0, turned, turned_reverse),
        jnp.where(core == 0, turned_reverse, turned),
        plane_label_rows(label_row),
    )
    label_row, label_sent = label_row
    label_row = label_row.astype(f32) + other_plane(label_sent).astype(f32)
    packed_own = packed_own.reshape(count, V_HALF + PAD)
    packed_far = other_core(packed_own)
    packed = on_core(
        pull_back,
        core,
        (packed_own, packed_far, head_weight, head_weight),
        [
            whole(packed_own),
            whole(packed_far),
            pl.BlockSpec((width, V_HALF), lambda step, half: (0, half[0])),
            pl.BlockSpec((width, V_HALF), lambda step, half: (0, 1 - half[0])),
        ],
        [((count, width + PAD), bf16)],
        logit_flops,
    )
    packed, label_row = together(packed, label_row)
    packed = exchange(packed.reshape(CHIPS, BLOCK, width + PAD), UNIT_CHIPS)
    stats = from_three(packed[:, :, width:], N_STATS)
    row_top = jnp.max(stats[:, :, 0:1], axis=0, keepdims=True)
    weight = jnp.exp(stats[:, :, 0:1] - row_top)
    weight = weight / jnp.sum(weight * stats[:, :, 2:3], axis=0, keepdims=True)
    pulled = jnp.sum(weight * packed[:, :, :width].astype(f32), axis=0)
    pull = jnp.sum(weight * stats[:, :, 3:4], axis=0)
    inv_rms = stats[0, :, 1:2]
    scaled = summed * inv_rms
    dsummed = []
    for which in range(2):
        label_logit = jnp.sum(stats[:, :, 4 + 2 * which : 5 + 2 * which], axis=0)
        rest = jnp.sum(weight * stats[:, :, 5 + 2 * which : 6 + 2 * which], axis=0)
        dnormed = pulled - (1.0 - rest) * label_row[:, which * width : (which + 1) * width]
        mean = (pull - (1.0 - rest) * label_logit) / D
        dsummed.append((inv_rms * (dnormed - scaled * mean)).astype(bf16))
    dsummed = to_all(jnp.concatenate(dsummed, axis=1), UNIT_CHIPS).reshape(count, 2 * width)

    far_dsummed = other_core(dsummed)
    dhidden = on_core(
        back_kernel,
        core,
        (dsummed, far_dsummed, down_weight, down_got),
        [whole(dsummed), whole(far_dsummed), rows_of(down_weight, FF_HALF), whole(down_got)],
        [((count, 2 * FF_HALF), bf16)],
        2 * gate_up_flops,
    )
    dhidden = exchange(dhidden.reshape(CHIPS, BLOCK, 2 * FF_HALF), WIDTH_CHIPS)
    dhidden = jnp.sum(dhidden.astype(f32), axis=0)
    cot = (dhidden * jnp.concatenate([silu_gate, silu_gate], axis=1)).astype(bf16)
    cot_own = to_all(cot, WIDTH_CHIPS).reshape(count, 2 * FF_HALF)
    cot_far = other_core(cot_own)
    done = sophia_half(core, turned_own, cot_own, up_moment, up_curvature, ())
    return tuple(sophia_half(far, turned_far, cot_far, up_moment, up_curvature, done))


def solution(mesh):
    fine = Mesh(mesh.devices.reshape(2, 4, 2, 4, 2), ("xl", "y", "core", "z", "xh"))
    dp = ("xl", "y", "core")
    tensor = ("z", "xh")
    both = P(dp, tensor)
    placed = (P(None, dp), both, both, P(tensor, dp), both, both, both, P(dp), P(dp))
    return jax.shard_map(
        on_device,
        mesh=fine,
        in_specs=placed,
        out_specs=(both, both, both),
        check_vma=False,
    )
```

```python
import itertools

import jax
import jax.numpy as jnp
from jax import lax
from jax.experimental import pallas as pl
from jax.experimental.pallas import tpu as pltpu
from jax.sharding import Mesh, PartitionSpec as P

D = 8192
FF_HALF = 896
V_HALF = 1024
BLOCK = 64
CHIPS = 8
PAD = 128
N_STATS = 8
STEP = 16384.0
TINY = 1e-30

beta_one = 0.965
beta_two = 0.95
rho_scale = 0.05
eps_norm = 1e-05

WIDTH_CHIPS = ("xl", "y")
UNIT_CHIPS = ("z", "xh")
MESH_SIZES = {"xl": 2, "y": 4, "core": 2, "z": 4, "xh": 2}
f32 = jnp.float32
bf16 = jnp.bfloat16
VMEM_LIMIT = 24 * 1024 * 1024


def other_core(value):
    return lax.ppermute(value, "core", [(0, 1), (1, 0)])


def partners(axes):
    names = tuple(MESH_SIZES)
    places = list(itertools.product(*(range(size) for size in MESH_SIZES.values())))
    groups = {}
    for number, place in enumerate(places):
        fixed = tuple(value for name, value in zip(names, place) if name not in axes)
        groups.setdefault(fixed, []).append(number)
    core = names.index("core")
    return [members[::-1] if places[members[0]][core] else members for members in groups.values()]


def exchange(blocks, axes):
    return lax.all_to_all(
        blocks, tuple(MESH_SIZES), split_axis=0, concat_axis=0, tiled=True, axis_index_groups=partners(axes)
    )


def to_all(block, axes):
    copies = jnp.broadcast_to(block[None], (CHIPS,) + block.shape)
    return exchange(copies, axes)


def block_rows(block):
    return slice(block * BLOCK, (block + 1) * BLOCK)


def join_cores(own, far):
    return jnp.concatenate(
        [own[block_rows(block)] + far[block_rows(CHIPS - 1 - block)] for block in range(CHIPS)], axis=0
    )


def reverse_rows(rows):
    return jnp.concatenate([rows[block_rows(CHIPS - 1 - block)] for block in range(CHIPS)], axis=0)


def reverse_blocks(rows):
    return rows.reshape((CHIPS, BLOCK) + rows.shape[1:])[::-1].reshape(rows.shape)


def together(*values):
    return lax.optimization_barrier(values)


def dot(left, right):
    return jnp.dot(left, right, preferred_element_type=f32)


def dot_rows(left, right):
    return lax.dot_general(left, right, (((1,), (1,)), ((), ())), preferred_element_type=f32)


def from_three(parts, count):
    parts = parts.astype(f32)
    return parts[..., :count] + parts[..., count : 2 * count] + parts[..., 2 * count : 3 * count]


def whole(array):
    return pl.BlockSpec(array.shape, lambda step, half: (0,) * array.ndim)


def columns_of(array, count):
    return pl.BlockSpec((array.shape[0], count), lambda step, half: (0, half[0]))


def rows_of(array, count):
    return pl.BlockSpec((count, array.shape[1]), lambda step, half: (half[0], 0))


def on_core(kernel, half, operands, specs, outs, flops, limit=VMEM_LIMIT):
    size = sum(operand.size * operand.dtype.itemsize for operand in operands)
    results = pl.pallas_call(
        kernel,
        out_shape=tuple(jax.ShapeDtypeStruct(shape, dtype) for shape, dtype in outs),
        grid_spec=pltpu.PrefetchScalarGridSpec(
            num_scalar_prefetch=1,
            grid=(1,),
            in_specs=specs,
            out_specs=tuple(whole(jax.ShapeDtypeStruct(*out)) for out in outs),
        ),
        compiler_params=pltpu.CompilerParams(vmem_limit_bytes=limit),
        cost_estimate=pl.CostEstimate(flops=flops, bytes_accessed=size, transcendentals=0),
    )(half.reshape(1), *operands)
    return results if len(outs) > 1 else results[0]


def gate_up_pack(half_ref, own_gate, own_up, got_gate, got_up, labels, out):
    core = half_ref[0]
    gate_sum = (own_gate[...].astype(f32) + got_gate[...].astype(f32)).astype(bf16)
    up_sum = (own_up[...].astype(f32) + got_up[...].astype(f32)).astype(bf16)
    for block in range(CHIPS):
        place = block + core * (CHIPS - 1 - 2 * block)
        rows = pl.ds(pl.multiple_of(place * BLOCK, BLOCK), BLOCK)
        out[rows, :FF_HALF] = gate_sum[block_rows(block)]
        out[rows, FF_HALF : 2 * FF_HALF] = up_sum[block_rows(block)]
        out[rows, 2 * FF_HALF :] = labels[...]


def branch_kernel(half_ref, own, far, down_own, down_far, out):
    out[...] = join_cores(dot(own[...], down_own[...]), dot(far[...], down_far[...])).astype(bf16)


def hidden_kernel(half_ref, both, hidden, silu_out):
    gate = jnp.zeros((BLOCK, FF_HALF), f32)
    upper = jnp.zeros((BLOCK, FF_HALF), f32)
    for chip in range(CHIPS):
        gate = gate + both[chip, :, :FF_HALF].astype(f32)
        upper = upper + both[chip, :, FF_HALF : 2 * FF_HALF].astype(f32)
    silu_gate = gate / (1.0 + jnp.exp(-gate))
    silu_out[...] = silu_gate
    rounded = (silu_gate * upper).astype(bf16)
    for chip in range(CHIPS):
        hidden[chip] = rounded


def squares_of(rows):
    wide = rows[...].astype(f32)
    return jnp.sum(wide * wide, axis=1, keepdims=True)


def exponent_of(values):
    return jnp.ceil(jnp.log2(jnp.maximum(values, TINY)))


def logits_kernel(half_ref, rows, far_rows, head, head_got, out):
    raw = join_cores(dot(rows[...], head[...]), dot(far_rows[...], head_got[...]))
    squares = join_cores(squares_of(rows), squares_of(far_rows))
    level = exponent_of(jnp.max(jnp.abs(raw), axis=1, keepdims=True))
    out[:, :V_HALF] = jnp.round(raw * (STEP * jnp.exp2(-level))).astype(jnp.int32).astype(jnp.int16)
    square_level = exponent_of(squares)
    units = squares * (STEP * jnp.exp2(-square_level))
    high = jnp.floor(units)
    low = jnp.floor((units - high) * STEP)
    lane = lax.broadcasted_iota(jnp.int32, (rows.shape[0], PAD), 1)
    tail = jnp.where(lane == 0, level, jnp.where(lane == 1, high, jnp.where(lane == 2, low, square_level)))
    out[:, V_HALF:] = tail.astype(jnp.int32).astype(jnp.int16)


def pack_three(values):
    lane = lax.broadcasted_iota(jnp.int32, values.shape, 1)
    values = jnp.where(lane < N_STATS, values, 0.0)
    high = values.astype(bf16)
    rest = values - high.astype(f32)
    middle = rest.astype(bf16)
    low = (rest - middle.astype(f32)).astype(bf16)
    row = lax.broadcasted_iota(jnp.int32, (PAD, PAD), 0)
    lane = lax.broadcasted_iota(jnp.int32, (PAD, PAD), 1)
    by_one = (lane == row + N_STATS).astype(f32).astype(bf16)
    by_two = (lane == row + 2 * N_STATS).astype(f32).astype(bf16)
    return (high.astype(f32) + dot(middle, by_one) + dot(low, by_two)).astype(bf16)


def softmax_kernel(start_ref, raw, labels, out):
    total = jnp.zeros((BLOCK, V_HALF), f32)
    squares = jnp.zeros((BLOCK, 1), f32)
    for chip in range(CHIPS):
        tail = raw[chip, :, V_HALF:].astype(jnp.int32).astype(f32)
        scale = jnp.exp2(tail[:, 0:1]) / STEP
        total = total + raw[chip, :, :V_HALF].astype(jnp.int32).astype(f32) * scale
        square_scale = jnp.exp2(tail[:, 3:4]) / STEP
        squares = squares + (tail[:, 1:2] + tail[:, 2:3] / STEP) * square_scale
    inv_rms = lax.rsqrt(squares / D + eps_norm)
    logits = total * inv_rms
    top = jnp.max(logits, axis=1, keepdims=True)
    exp_terms = jnp.exp(logits - top)
    short = exp_terms.astype(bf16)
    rounded = short.astype(f32)
    ids = start_ref[0] + lax.broadcasted_iota(jnp.int32, (BLOCK, V_HALF), 1)
    stats = [
        top,
        inv_rms,
        jnp.sum(exp_terms, axis=1, keepdims=True),
        jnp.sum(rounded * logits, axis=1, keepdims=True),
    ]
    for which in range(2):
        hot = labels[:, which : which + 1] == ids
        stats.append(jnp.sum(jnp.where(hot, logits, 0.0), axis=1, keepdims=True))
        stats.append(jnp.sum(jnp.where(hot, exp_terms - rounded, 0.0), axis=1, keepdims=True))
    lane = lax.broadcasted_iota(jnp.int32, (BLOCK, PAD), 1)
    table = jnp.zeros((BLOCK, PAD), f32)
    for place, value in enumerate(stats):
        table = jnp.where(lane == place, value, table)
    packed = pack_three(table)
    for chip in range(CHIPS):
        out[chip, :, :V_HALF] = short
        out[chip, :, V_HALF:] = packed


def pull_back(half_ref, own, far, head_own, head_far, out):
    count = own.shape[0]
    row = lax.broadcasted_iota(jnp.int32, (PAD, PAD), 0)
    lane = lax.broadcasted_iota(jnp.int32, (PAD, PAD), 1)
    gather = ((row % N_STATS == lane) & (row < 3 * N_STATS)).astype(f32).astype(bf16)
    stats_own = dot(own[:, V_HALF:], gather)
    stats_far = reverse_rows(dot(far[:, V_HALF:], gather))
    top = jnp.maximum(stats_own[:, 0:1], stats_far[:, 0:1])
    scale_own = jnp.exp(stats_own[:, 0:1] - top)
    scale_far = jnp.exp(stats_far[:, 0:1] - top)
    pulled = scale_own * dot_rows(own[:, :V_HALF], head_own[...])
    pulled = pulled + scale_far * reverse_rows(dot_rows(far[:, :V_HALF], head_far[...]))
    width = pulled.shape[1]
    out[:, :width] = pulled.astype(bf16)
    lane = lax.broadcasted_iota(jnp.int32, (count, PAD), 1)
    is_sum = (lane == 2) | (lane == 3) | (lane == 5) | (lane == 7)
    both = jnp.where(is_sum, scale_own * stats_own + scale_far * stats_far, stats_own + stats_far)
    both = jnp.where(lane == 0, top, jnp.where(lane == 1, stats_own, both))
    out[:, width:] = pack_three(both)


def back_kernel(half_ref, dsummed, far_dsummed, down, down_got, out):
    width = down.shape[1]
    for which in range(2):
        place = slice(which * width, (which + 1) * width)
        part = join_cores(dot_rows(dsummed[:, place], down[...]), dot_rows(far_dsummed[:, place], down_got[...]))
        out[:, which * FF_HALF : (which + 1) * FF_HALF] = part.astype(bf16)


def step_kernel(half_ref, turned, cot, moment_ref, curve_ref, *rest):
    new_moment, new_curve, update = rest[-3:]
    grad_true = dot(turned[...], cot[:, :FF_HALF])
    grad_sampled = dot(turned[...], cot[:, FF_HALF:])
    moment = beta_one * moment_ref[...] + (1.0 - beta_one) * grad_true
    curve = beta_two * curve_ref[...] + (1.0 - beta_two) * grad_sampled * grad_sampled
    new_moment[...] = moment
    new_curve[...] = curve
    update[...] = jnp.clip(moment / (rho_scale * curve), -1.0, 1.0)


def sophia_half(half, turned, cot, moment, curve, done):
    tall = 128
    rows, count = turned.shape
    big = pl.BlockSpec((tall, FF_HALF), lambda step, half: (step, half[0]))
    shape = jax.ShapeDtypeStruct(moment.shape, f32)
    kept = [pl.BlockSpec(memory_space=pl.ANY) for _ in done]
    return pl.pallas_call(
        step_kernel,
        out_shape=(shape, shape, shape),
        grid_spec=pltpu.PrefetchScalarGridSpec(
            num_scalar_prefetch=1,
            grid=(rows // tall,),
            in_specs=[
                pl.BlockSpec((tall, count), lambda step, half: (step, 0)),
                whole(cot),
                big,
                big,
            ]
            + kept,
            out_specs=(big, big, big),
        ),
        input_output_aliases={5 + which: which for which in range(len(done))},
        compiler_params=pltpu.CompilerParams(vmem_limit_bytes=VMEM_LIMIT),
        cost_estimate=pl.CostEstimate(flops=950000000, bytes_accessed=11000000, transcendentals=0),
    )(half.reshape(1), turned, cot, moment, curve, *done)


def own_part(array, index, axis):
    keep = lax.dynamic_index_in_dim(array, index, axis, keepdims=False)
    send = lax.dynamic_index_in_dim(array, 1 - index, axis, keepdims=False)
    return keep, send


def label_rows(labels, head_weight, unit_chip):
    ids = unit_chip * (2 * V_HALF) + lax.broadcasted_iota(jnp.int32, (1, 2 * V_HALF), 1)
    parts = []
    for which in range(2):
        hot = (labels[:, which : which + 1] == ids).astype(bf16)
        parts.append(dot_rows(hot, head_weight).astype(bf16))
    return jnp.concatenate(parts, axis=1).reshape(2, 2, 2, BLOCK, -1)


def near_label_rows(rows):
    keep, send = own_part(rows, lax.axis_index("z") % 2, 1)
    return keep, lax.ppermute(send, "z", [(0, 1), (1, 0), (2, 3), (3, 2)])


def plane_label_rows(near, got):
    rows = near + got
    keep, send = own_part(rows, lax.axis_index("z") // 2, 0)
    rows = keep + lax.ppermute(send, "z", [(0, 2), (2, 0), (1, 3), (3, 1)])
    return own_part(rows, lax.axis_index("xh"), 0)


def other_plane(rows):
    return lax.ppermute(rows, "xh", [(0, 1), (1, 0)])


def on_device(
    tokens,
    gate_weight,
    up_weight,
    down_weight,
    head_weight,
    up_moment,
    up_curvature,
    true_labels,
    sampled_labels,
):
    core = lax.axis_index("core").astype(jnp.int32)
    far = 1 - core
    unit_chip = lax.axis_index(UNIT_CHIPS)
    count, width = tokens.shape

    labels = jnp.stack([true_labels, sampled_labels], axis=1)
    far_labels = other_core(labels)
    labels = jnp.where(
        core == 0,
        jnp.concatenate([labels, far_labels], axis=0),
        jnp.concatenate([far_labels, labels], axis=0),
    )
    digits = jnp.concatenate([labels // PAD, labels % PAD], axis=1).astype(bf16)
    digits = jnp.pad(digits, ((0, 0), (0, PAD - 4)))

    gate_up_flops = 4 * count * width * FF_HALF

    def gate_up(half):
        gate = lax.dynamic_slice_in_dim(gate_weight, half * FF_HALF, FF_HALF, 1)
        upper = lax.dynamic_slice_in_dim(up_weight, half * FF_HALF, FF_HALF, 1)
        return dot(tokens, gate).astype(bf16), dot(tokens, upper).astype(bf16)

    far_gate, far_up = gate_up(far)
    got_gate, got_up = other_core(far_gate), other_core(far_up)
    own_gate, own_up = gate_up(core)
    operands = (own_gate, own_up, got_gate, got_up, digits)
    both = on_core(
        gate_up_pack,
        core,
        operands,
        [whole(operand) for operand in operands],
        [((count, 2 * FF_HALF + PAD), bf16)],
        1000000,
    )
    both, sent_head, sent_down = together(both, head_weight, down_weight)
    head_send = lax.dynamic_slice_in_dim(sent_head, far * V_HALF, V_HALF, 1)
    down_send = lax.dynamic_slice_in_dim(sent_down, far * FF_HALF, FF_HALF, 0)
    both, head_got, down_got = together(
        exchange(both.reshape(CHIPS, BLOCK, 2 * FF_HALF + PAD), WIDTH_CHIPS),
        other_core(head_send),
        other_core(down_send),
    )
    hidden, silu_gate = on_core(
        hidden_kernel,
        core,
        (both,),
        [whole(both)],
        [((CHIPS, BLOCK, FF_HALF), bf16), ((BLOCK, FF_HALF), f32)],
        1000000,
    )

    hidden, digits = together(hidden, both)
    digits = digits[:, :, 2 * FF_HALF : 2 * FF_HALF + 4].astype(jnp.int32)
    all_labels = digits[:, :, :2] * PAD + digits[:, :, 2:]
    all_labels = jnp.where(core == 0, all_labels, all_labels[::-1]).reshape(count, 2)
    width_chip = lax.axis_index(WIDTH_CHIPS)
    hidden_own, label_row, labels = together(
        exchange(hidden, WIDTH_CHIPS),
        label_rows(all_labels, head_weight, unit_chip),
        lax.dynamic_slice_in_dim(all_labels, width_chip * BLOCK, BLOCK, 0),
    )
    hidden_own = hidden_own.reshape(count, FF_HALF)
    hidden_far = other_core(hidden_own)
    branch = on_core(
        branch_kernel,
        core,
        (hidden_own, hidden_far, down_weight, down_weight),
        [
            whole(hidden_own),
            whole(hidden_far),
            rows_of(down_weight, FF_HALF),
            pl.BlockSpec((FF_HALF, width), lambda step, half: (1 - half[0], 0)),
        ],
        [((count, width), bf16)],
        gate_up_flops,
    )
    branch = exchange(branch.reshape(CHIPS, BLOCK, width), UNIT_CHIPS)
    branch = jnp.sum(branch.astype(f32), axis=0)
    own_tokens = lax.dynamic_slice_in_dim(tokens, unit_chip * BLOCK, BLOCK, 0)
    summed = own_tokens.astype(f32) + branch
    rows = to_all(summed.astype(bf16), UNIT_CHIPS).reshape(count, width)

    far_rows = other_core(rows)
    logit_flops = 4 * count * width * V_HALF
    raw = on_core(
        logits_kernel,
        core,
        (rows, far_rows, head_weight, head_got),
        [whole(rows), whole(far_rows), columns_of(head_weight, V_HALF), whole(head_got)],
        [((count, V_HALF + PAD), jnp.int16)],
        logit_flops,
    )
    raw, label_row = together(raw, label_row)
    raw, label_row = together(
        exchange(raw.reshape(CHIPS, BLOCK, V_HALF + PAD), WIDTH_CHIPS), near_label_rows(label_row)
    )
    vocab_start = ((unit_chip * 2 + core) * V_HALF).astype(jnp.int32)
    packed = on_core(
        softmax_kernel,
        vocab_start,
        (raw, labels),
        [whole(raw), whole(labels)],
        [((CHIPS, BLOCK, V_HALF + PAD), bf16)],
        1000000,
    )
    packed, token_rows, label_row = together(packed, tokens, label_row)
    turned = token_rows.T
    turned_reverse = reverse_blocks(token_rows).T
    packed_own, turned_own, turned_far, label_row = together(
        exchange(packed, WIDTH_CHIPS),
        jnp.where(core == 0, turned, turned_reverse),
        jnp.where(core == 0, turned_reverse, turned),
        plane_label_rows(*label_row),
    )
    label_row, label_sent = label_row
    packed_own = packed_own.reshape(count, V_HALF + PAD)
    packed_far = other_core(packed_own)
    packed = on_core(
        pull_back,
        core,
        (packed_own, packed_far, head_weight, head_weight),
        [
            whole(packed_own),
            whole(packed_far),
            pl.BlockSpec((width, V_HALF), lambda step, half: (0, half[0])),
            pl.BlockSpec((width, V_HALF), lambda step, half: (0, 1 - half[0])),
        ],
        [((count, width + PAD), bf16)],
        logit_flops,
    )
    packed, label_sent = together(packed, label_sent)
    packed, label_got = together(
        exchange(packed.reshape(CHIPS, BLOCK, width + PAD), UNIT_CHIPS), other_plane(label_sent)
    )
    label_row = label_row.astype(f32) + label_got.astype(f32)
    stats = from_three(packed[:, :, width:], N_STATS)
    row_top = jnp.max(stats[:, :, 0:1], axis=0, keepdims=True)
    weight = jnp.exp(stats[:, :, 0:1] - row_top)
    weight = weight / jnp.sum(weight * stats[:, :, 2:3], axis=0, keepdims=True)
    pulled = jnp.sum(weight * packed[:, :, :width].astype(f32), axis=0)
    pull = jnp.sum(weight * stats[:, :, 3:4], axis=0)
    inv_rms = stats[0, :, 1:2]
    scaled = summed * inv_rms
    dsummed = []
    for which in range(2):
        label_logit = jnp.sum(stats[:, :, 4 + 2 * which : 5 + 2 * which], axis=0)
        rest = jnp.sum(weight * stats[:, :, 5 + 2 * which : 6 + 2 * which], axis=0)
        dnormed = pulled - (1.0 - rest) * label_row[:, which * width : (which + 1) * width]
        mean = (pull - (1.0 - rest) * label_logit) / D
        dsummed.append((inv_rms * (dnormed - scaled * mean)).astype(bf16))
    dsummed = to_all(jnp.concatenate(dsummed, axis=1), UNIT_CHIPS).reshape(count, 2 * width)

    far_dsummed = other_core(dsummed)
    dhidden = on_core(
        back_kernel,
        core,
        (dsummed, far_dsummed, down_weight, down_got),
        [whole(dsummed), whole(far_dsummed), rows_of(down_weight, FF_HALF), whole(down_got)],
        [((count, 2 * FF_HALF), bf16)],
        2 * gate_up_flops,
    )
    dhidden = exchange(dhidden.reshape(CHIPS, BLOCK, 2 * FF_HALF), WIDTH_CHIPS)
    dhidden = jnp.sum(dhidden.astype(f32), axis=0)
    cot = (dhidden * jnp.concatenate([silu_gate, silu_gate], axis=1)).astype(bf16)
    cot_own = to_all(cot, WIDTH_CHIPS).reshape(count, 2 * FF_HALF)
    cot_far = other_core(cot_own)
    done = sophia_half(core, turned_own, cot_own, up_moment, up_curvature, ())
    return tuple(sophia_half(far, turned_far, cot_far, up_moment, up_curvature, done))


def solution(mesh):
    fine = Mesh(mesh.devices.reshape(2, 4, 2, 4, 2), ("xl", "y", "core", "z", "xh"))
    dp = ("xl", "y", "core")
    tensor = ("z", "xh")
    both = P(dp, tensor)
    placed = (P(None, dp), both, both, P(tensor, dp), both, both, both, P(dp), P(dp))
    return jax.shard_map(
        on_device,
        mesh=fine,
        in_specs=placed,
        out_specs=(both, both, both),
        check_vma=False,
    )
```

```python
import itertools

import jax
import jax.numpy as jnp
from jax import lax
from jax.experimental import pallas as pl
from jax.experimental.pallas import tpu as pltpu
from jax.sharding import Mesh, PartitionSpec as P

D = 8192
FF_HALF = 896
V_HALF = 1024
BLOCK = 64
CHIPS = 8
PAD = 128
N_STATS = 8
STEP = 16384.0
TINY = 1e-30

beta_one = 0.965
beta_two = 0.95
rho_scale = 0.05
eps_norm = 1e-05

WIDTH_CHIPS = ("xl", "y")
UNIT_CHIPS = ("z", "xh")
MESH_SIZES = {"xl": 2, "y": 4, "core": 2, "z": 4, "xh": 2}
f32 = jnp.float32
bf16 = jnp.bfloat16
VMEM_LIMIT = 24 * 1024 * 1024


def other_core(value):
    return lax.ppermute(value, "core", [(0, 1), (1, 0)])


def partners(axes):
    names = tuple(MESH_SIZES)
    places = list(itertools.product(*(range(size) for size in MESH_SIZES.values())))
    groups = {}
    for number, place in enumerate(places):
        fixed = tuple(value for name, value in zip(names, place) if name not in axes)
        groups.setdefault(fixed, []).append(number)
    core = names.index("core")
    return [members[::-1] if places[members[0]][core] else members for members in groups.values()]


def exchange(blocks, axes):
    return lax.all_to_all(
        blocks, tuple(MESH_SIZES), split_axis=0, concat_axis=0, tiled=True, axis_index_groups=partners(axes)
    )


def to_all(block, axes):
    copies = jnp.broadcast_to(block[None], (CHIPS,) + block.shape)
    return exchange(copies, axes)


def block_rows(block):
    return slice(block * BLOCK, (block + 1) * BLOCK)


def join_cores(own, far):
    return jnp.concatenate(
        [own[block_rows(block)] + far[block_rows(CHIPS - 1 - block)] for block in range(CHIPS)], axis=0
    )


def reverse_rows(rows):
    return jnp.concatenate([rows[block_rows(CHIPS - 1 - block)] for block in range(CHIPS)], axis=0)


def reverse_blocks(rows):
    return rows.reshape((CHIPS, BLOCK) + rows.shape[1:])[::-1].reshape(rows.shape)


def together(*values):
    return lax.optimization_barrier(values)


def dot(left, right):
    return jnp.dot(left, right, preferred_element_type=f32)


def dot_rows(left, right):
    return lax.dot_general(left, right, (((1,), (1,)), ((), ())), preferred_element_type=f32)


def from_three(parts, count):
    parts = parts.astype(f32)
    return parts[..., :count] + parts[..., count : 2 * count] + parts[..., 2 * count : 3 * count]


def whole(array):
    return pl.BlockSpec(array.shape, lambda step, half: (0,) * array.ndim)


def columns_of(array, count):
    return pl.BlockSpec((array.shape[0], count), lambda step, half: (0, half[0]))


def rows_of(array, count):
    return pl.BlockSpec((count, array.shape[1]), lambda step, half: (half[0], 0))


def on_core(kernel, half, operands, specs, outs, flops, limit=VMEM_LIMIT):
    size = sum(operand.size * operand.dtype.itemsize for operand in operands)
    results = pl.pallas_call(
        kernel,
        out_shape=tuple(jax.ShapeDtypeStruct(shape, dtype) for shape, dtype in outs),
        grid_spec=pltpu.PrefetchScalarGridSpec(
            num_scalar_prefetch=1,
            grid=(1,),
            in_specs=specs,
            out_specs=tuple(whole(jax.ShapeDtypeStruct(*out)) for out in outs),
        ),
        compiler_params=pltpu.CompilerParams(vmem_limit_bytes=limit),
        cost_estimate=pl.CostEstimate(flops=flops, bytes_accessed=size, transcendentals=0),
    )(half.reshape(1), *operands)
    return results if len(outs) > 1 else results[0]


def gate_up_pack(half_ref, own_gate, own_up, got_gate, got_up, labels, out):
    core = half_ref[0]
    gate_sum = (own_gate[...].astype(f32) + got_gate[...].astype(f32)).astype(bf16)
    up_sum = (own_up[...].astype(f32) + got_up[...].astype(f32)).astype(bf16)
    blocks = own_gate.shape[0] // BLOCK
    for block in range(blocks):
        place = block + core * (blocks - 1 - 2 * block)
        rows = pl.ds(pl.multiple_of(place * BLOCK, BLOCK), BLOCK)
        out[rows, :FF_HALF] = gate_sum[block_rows(block)]
        out[rows, FF_HALF : 2 * FF_HALF] = up_sum[block_rows(block)]
        out[rows, 2 * FF_HALF :] = labels[...]


def pack_gate_up(core, own_gate, own_up, got_gate, got_up, labels):
    steps = 4
    count = own_gate.shape[0]
    part = pl.BlockSpec((count // steps, FF_HALF), lambda step, half: (step, 0))
    wide = 2 * FF_HALF + PAD
    return pl.pallas_call(
        gate_up_pack,
        out_shape=jax.ShapeDtypeStruct((count, wide), bf16),
        grid_spec=pltpu.PrefetchScalarGridSpec(
            num_scalar_prefetch=1,
            grid=(steps,),
            in_specs=[part, part, part, part, whole(labels)],
            out_specs=pl.BlockSpec(
                (count // steps, wide), lambda step, half: (step + half[0] * (steps - 1 - 2 * step), 0)
            ),
        ),
        compiler_params=pltpu.CompilerParams(vmem_limit_bytes=60 * 1024 * 1024),
        cost_estimate=pl.CostEstimate(flops=2000000, bytes_accessed=6000000, transcendentals=0),
    )(core.reshape(1), own_gate, own_up, got_gate, got_up, labels)


def branch_kernel(half_ref, own_part, far, down_far, out):
    out[...] = join_cores(own_part[...], dot(far[...], down_far[...])).astype(bf16)


def hidden_kernel(half_ref, both, hidden, silu_out):
    gate = jnp.zeros((BLOCK, FF_HALF), f32)
    upper = jnp.zeros((BLOCK, FF_HALF), f32)
    for chip in range(CHIPS):
        gate = gate + both[chip, :, :FF_HALF].astype(f32)
        upper = upper + both[chip, :, FF_HALF : 2 * FF_HALF].astype(f32)
    silu_gate = gate / (1.0 + jnp.exp(-gate))
    silu_out[...] = silu_gate
    rounded = (silu_gate * upper).astype(bf16)
    for chip in range(CHIPS):
        hidden[chip] = rounded


def squares_of(rows):
    wide = rows[...].astype(f32)
    return jnp.sum(wide * wide, axis=1, keepdims=True)


def exponent_of(values):
    return jnp.ceil(jnp.log2(jnp.maximum(values, TINY)))


def logits_kernel(half_ref, rows, far_rows, head, head_got, out):
    raw = join_cores(dot(rows[...], head[...]), dot(far_rows[...], head_got[...]))
    squares = join_cores(squares_of(rows), squares_of(far_rows))
    level = exponent_of(jnp.max(jnp.abs(raw), axis=1, keepdims=True))
    out[:, :V_HALF] = jnp.round(raw * (STEP * jnp.exp2(-level))).astype(jnp.int32).astype(jnp.int16)
    square_level = exponent_of(squares)
    units = squares * (STEP * jnp.exp2(-square_level))
    high = jnp.floor(units)
    low = jnp.floor((units - high) * STEP)
    lane = lax.broadcasted_iota(jnp.int32, (rows.shape[0], PAD), 1)
    tail = jnp.where(lane == 0, level, jnp.where(lane == 1, high, jnp.where(lane == 2, low, square_level)))
    out[:, V_HALF:] = tail.astype(jnp.int32).astype(jnp.int16)


def pack_three(values):
    lane = lax.broadcasted_iota(jnp.int32, values.shape, 1)
    values = jnp.where(lane < N_STATS, values, 0.0)
    high = values.astype(bf16)
    rest = values - high.astype(f32)
    middle = rest.astype(bf16)
    low = (rest - middle.astype(f32)).astype(bf16)
    row = lax.broadcasted_iota(jnp.int32, (PAD, PAD), 0)
    lane = lax.broadcasted_iota(jnp.int32, (PAD, PAD), 1)
    by_one = (lane == row + N_STATS).astype(f32).astype(bf16)
    by_two = (lane == row + 2 * N_STATS).astype(f32).astype(bf16)
    return (high.astype(f32) + dot(middle, by_one) + dot(low, by_two)).astype(bf16)


def softmax_kernel(start_ref, raw, labels, out):
    total = jnp.zeros((BLOCK, V_HALF), f32)
    squares = jnp.zeros((BLOCK, 1), f32)
    for chip in range(CHIPS):
        tail = raw[chip, :, V_HALF:].astype(jnp.int32).astype(f32)
        scale = jnp.exp2(tail[:, 0:1]) / STEP
        total = total + raw[chip, :, :V_HALF].astype(jnp.int32).astype(f32) * scale
        square_scale = jnp.exp2(tail[:, 3:4]) / STEP
        squares = squares + (tail[:, 1:2] + tail[:, 2:3] / STEP) * square_scale
    inv_rms = lax.rsqrt(squares / D + eps_norm)
    logits = total * inv_rms
    top = jnp.max(logits, axis=1, keepdims=True)
    exp_terms = jnp.exp(logits - top)
    short = exp_terms.astype(bf16)
    rounded = short.astype(f32)
    ids = start_ref[0] + lax.broadcasted_iota(jnp.int32, (BLOCK, V_HALF), 1)
    stats = [
        top,
        inv_rms,
        jnp.sum(exp_terms, axis=1, keepdims=True),
        jnp.sum(rounded * logits, axis=1, keepdims=True),
    ]
    for which in range(2):
        hot = labels[:, which : which + 1] == ids
        stats.append(jnp.sum(jnp.where(hot, logits, 0.0), axis=1, keepdims=True))
        stats.append(jnp.sum(jnp.where(hot, exp_terms - rounded, 0.0), axis=1, keepdims=True))
    lane = lax.broadcasted_iota(jnp.int32, (BLOCK, PAD), 1)
    table = jnp.zeros((BLOCK, PAD), f32)
    for place, value in enumerate(stats):
        table = jnp.where(lane == place, value, table)
    packed = pack_three(table)
    for chip in range(CHIPS):
        out[chip, :, :V_HALF] = short
        out[chip, :, V_HALF:] = packed


def pull_back(half_ref, own, far, head_own, head_far, out):
    count = own.shape[0]
    row = lax.broadcasted_iota(jnp.int32, (PAD, PAD), 0)
    lane = lax.broadcasted_iota(jnp.int32, (PAD, PAD), 1)
    gather = ((row % N_STATS == lane) & (row < 3 * N_STATS)).astype(f32).astype(bf16)
    stats_own = dot(own[:, V_HALF:], gather)
    stats_far = reverse_rows(dot(far[:, V_HALF:], gather))
    top = jnp.maximum(stats_own[:, 0:1], stats_far[:, 0:1])
    scale_own = jnp.exp(stats_own[:, 0:1] - top)
    scale_far = jnp.exp(stats_far[:, 0:1] - top)
    pulled = scale_own * dot_rows(own[:, :V_HALF], head_own[...])
    pulled = pulled + scale_far * reverse_rows(dot_rows(far[:, :V_HALF], head_far[...]))
    width = pulled.shape[1]
    out[:, :width] = pulled.astype(bf16)
    lane = lax.broadcasted_iota(jnp.int32, (count, PAD), 1)
    is_sum = (lane == 2) | (lane == 3) | (lane == 5) | (lane == 7)
    both = jnp.where(is_sum, scale_own * stats_own + scale_far * stats_far, stats_own + stats_far)
    both = jnp.where(lane == 0, top, jnp.where(lane == 1, stats_own, both))
    out[:, width:] = pack_three(both)


def back_kernel(half_ref, dsummed, far_dsummed, down, down_got, out):
    width = down.shape[1]
    for which in range(2):
        place = slice(which * width, (which + 1) * width)
        part = join_cores(dot_rows(dsummed[:, place], down[...]), dot_rows(far_dsummed[:, place], down_got[...]))
        out[:, which * FF_HALF : (which + 1) * FF_HALF] = part.astype(bf16)


def step_kernel(half_ref, turned, cot, moment_ref, curve_ref, *rest):
    new_moment, new_curve, update = rest[-3:]
    grad_true = dot(turned[...], cot[:, :FF_HALF])
    grad_sampled = dot(turned[...], cot[:, FF_HALF:])
    moment = beta_one * moment_ref[...] + (1.0 - beta_one) * grad_true
    curve = beta_two * curve_ref[...] + (1.0 - beta_two) * grad_sampled * grad_sampled
    new_moment[...] = moment
    new_curve[...] = curve
    update[...] = jnp.clip(moment / (rho_scale * curve), -1.0, 1.0)


def sophia_half(half, turned, cot, moment, curve, done):
    tall = 128
    rows, count = turned.shape
    big = pl.BlockSpec((tall, FF_HALF), lambda step, half: (step, half[0]))
    shape = jax.ShapeDtypeStruct(moment.shape, f32)
    kept = [pl.BlockSpec(memory_space=pl.ANY) for _ in done]
    return pl.pallas_call(
        step_kernel,
        out_shape=(shape, shape, shape),
        grid_spec=pltpu.PrefetchScalarGridSpec(
            num_scalar_prefetch=1,
            grid=(rows // tall,),
            in_specs=[
                pl.BlockSpec((tall, count), lambda step, half: (step, 0)),
                whole(cot),
                big,
                big,
            ]
            + kept,
            out_specs=(big, big, big),
        ),
        input_output_aliases={5 + which: which for which in range(len(done))},
        compiler_params=pltpu.CompilerParams(vmem_limit_bytes=VMEM_LIMIT),
        cost_estimate=pl.CostEstimate(flops=950000000, bytes_accessed=11000000, transcendentals=0),
    )(half.reshape(1), turned, cot, moment, curve, *done)


def own_part(array, index, axis):
    keep = lax.dynamic_index_in_dim(array, index, axis, keepdims=False)
    send = lax.dynamic_index_in_dim(array, 1 - index, axis, keepdims=False)
    return keep, send


def label_rows(labels, head_weight, unit_chip):
    ids = unit_chip * (2 * V_HALF) + lax.broadcasted_iota(jnp.int32, (1, 2 * V_HALF), 1)
    parts = []
    for which in range(2):
        hot = (labels[:, which : which + 1] == ids).astype(bf16)
        parts.append(dot_rows(hot, head_weight).astype(bf16))
    return jnp.concatenate(parts, axis=1).reshape(2, 2, 2, BLOCK, -1)


def near_label_rows(rows):
    keep, send = own_part(rows, lax.axis_index("z") % 2, 1)
    return keep, lax.ppermute(send, "z", [(0, 1), (1, 0), (2, 3), (3, 2)])


def plane_label_rows(near, got):
    rows = near + got
    keep, send = own_part(rows, lax.axis_index("z") // 2, 0)
    rows = keep + lax.ppermute(send, "z", [(0, 2), (2, 0), (1, 3), (3, 1)])
    return own_part(rows, lax.axis_index("xh"), 0)


def other_plane(rows):
    return lax.ppermute(rows, "xh", [(0, 1), (1, 0)])


def on_device(
    tokens,
    gate_weight,
    up_weight,
    down_weight,
    head_weight,
    up_moment,
    up_curvature,
    true_labels,
    sampled_labels,
):
    core = lax.axis_index("core").astype(jnp.int32)
    far = 1 - core
    unit_chip = lax.axis_index(UNIT_CHIPS)
    count, width = tokens.shape

    gate_up_flops = 4 * count * width * FF_HALF

    def gate_up(half):
        gate = lax.dynamic_slice_in_dim(gate_weight, half * FF_HALF, FF_HALF, 1)
        upper = lax.dynamic_slice_in_dim(up_weight, half * FF_HALF, FF_HALF, 1)
        return dot(tokens, gate).astype(bf16), dot(tokens, upper).astype(bf16)

    far_gate, far_up = gate_up(far)
    far_gate, true_labels, sampled_labels = together(far_gate, true_labels, sampled_labels)
    got_gate, got_up = other_core(far_gate), other_core(far_up)
    own_gate, own_up = gate_up(core)
    labels = jnp.stack([true_labels, sampled_labels], axis=1)
    far_labels = other_core(labels)
    labels = jnp.where(
        core == 0,
        jnp.concatenate([labels, far_labels], axis=0),
        jnp.concatenate([far_labels, labels], axis=0),
    )
    digits = jnp.concatenate([labels // PAD, labels % PAD], axis=1).astype(bf16)
    digits = jnp.pad(digits, ((0, 0), (0, PAD - 4)))

    both = pack_gate_up(core, own_gate, own_up, got_gate, got_up, digits)
    both, sent_head, sent_down = together(both, head_weight, down_weight)
    head_send = lax.dynamic_slice_in_dim(sent_head, far * V_HALF, V_HALF, 1)
    down_send = lax.dynamic_slice_in_dim(sent_down, far * FF_HALF, FF_HALF, 0)
    both, head_got, down_got = together(
        exchange(both.reshape(CHIPS, BLOCK, 2 * FF_HALF + PAD), WIDTH_CHIPS),
        other_core(head_send),
        other_core(down_send),
    )
    hidden, silu_gate = on_core(
        hidden_kernel,
        core,
        (both,),
        [whole(both)],
        [((CHIPS, BLOCK, FF_HALF), bf16), ((BLOCK, FF_HALF), f32)],
        1000000,
    )

    hidden, digits = together(hidden, both)
    digits = digits[:, :, 2 * FF_HALF : 2 * FF_HALF + 4].astype(jnp.int32)
    all_labels = digits[:, :, :2] * PAD + digits[:, :, 2:]
    all_labels = jnp.where(core == 0, all_labels, all_labels[::-1]).reshape(count, 2)
    width_chip = lax.axis_index(WIDTH_CHIPS)
    hidden_own, label_row, labels = together(
        exchange(hidden, WIDTH_CHIPS),
        label_rows(all_labels, head_weight, unit_chip),
        lax.dynamic_slice_in_dim(all_labels, width_chip * BLOCK, BLOCK, 0),
    )
    hidden_own = hidden_own.reshape(count, FF_HALF)
    hidden_far = other_core(hidden_own)
    own_part = dot(hidden_own, lax.dynamic_slice_in_dim(down_weight, core * FF_HALF, FF_HALF, 0))
    branch = on_core(
        branch_kernel,
        core,
        (own_part, hidden_far, down_weight),
        [
            whole(own_part),
            whole(hidden_far),
            pl.BlockSpec((FF_HALF, width), lambda step, half: (1 - half[0], 0)),
        ],
        [((count, width), bf16)],
        gate_up_flops,
    )
    branch = exchange(branch.reshape(CHIPS, BLOCK, width), UNIT_CHIPS)
    branch = jnp.sum(branch.astype(f32), axis=0)
    own_tokens = lax.dynamic_slice_in_dim(tokens, unit_chip * BLOCK, BLOCK, 0)
    summed = own_tokens.astype(f32) + branch
    rows = to_all(summed.astype(bf16), UNIT_CHIPS).reshape(count, width)

    far_rows = other_core(rows)
    logit_flops = 4 * count * width * V_HALF
    raw = on_core(
        logits_kernel,
        core,
        (rows, far_rows, head_weight, head_got),
        [whole(rows), whole(far_rows), columns_of(head_weight, V_HALF), whole(head_got)],
        [((count, V_HALF + PAD), jnp.int16)],
        logit_flops,
    )
    raw, label_row = together(raw, label_row)
    raw, label_row = together(
        exchange(raw.reshape(CHIPS, BLOCK, V_HALF + PAD), WIDTH_CHIPS), near_label_rows(label_row)
    )
    vocab_start = ((unit_chip * 2 + core) * V_HALF).astype(jnp.int32)
    packed = on_core(
        softmax_kernel,
        vocab_start,
        (raw, labels),
        [whole(raw), whole(labels)],
        [((CHIPS, BLOCK, V_HALF + PAD), bf16)],
        1000000,
    )
    packed, token_rows, label_row = together(packed, tokens, label_row)
    turned = token_rows.T
    turned_reverse = reverse_blocks(token_rows).T
    packed_own, turned_own, turned_far, label_row = together(
        exchange(packed, WIDTH_CHIPS),
        jnp.where(core == 0, turned, turned_reverse),
        jnp.where(core == 0, turned_reverse, turned),
        plane_label_rows(*label_row),
    )
    label_row, label_sent = label_row
    packed_own = packed_own.reshape(count, V_HALF + PAD)
    packed_far = other_core(packed_own)
    packed = on_core(
        pull_back,
        core,
        (packed_own, packed_far, head_weight, head_weight),
        [
            whole(packed_own),
            whole(packed_far),
            pl.BlockSpec((width, V_HALF), lambda step, half: (0, half[0])),
            pl.BlockSpec((width, V_HALF), lambda step, half: (0, 1 - half[0])),
        ],
        [((count, width + PAD), bf16)],
        logit_flops,
    )
    packed, label_sent = together(packed, label_sent)
    packed, label_got = together(
        exchange(packed.reshape(CHIPS, BLOCK, width + PAD), UNIT_CHIPS), other_plane(label_sent)
    )
    label_row = label_row.astype(f32) + label_got.astype(f32)
    stats = from_three(packed[:, :, width:], N_STATS)
    row_top = jnp.max(stats[:, :, 0:1], axis=0, keepdims=True)
    weight = jnp.exp(stats[:, :, 0:1] - row_top)
    weight = weight / jnp.sum(weight * stats[:, :, 2:3], axis=0, keepdims=True)
    pulled = jnp.sum(weight * packed[:, :, :width].astype(f32), axis=0)
    pull = jnp.sum(weight * stats[:, :, 3:4], axis=0)
    inv_rms = stats[0, :, 1:2]
    scaled = summed * inv_rms
    dsummed = []
    for which in range(2):
        label_logit = jnp.sum(stats[:, :, 4 + 2 * which : 5 + 2 * which], axis=0)
        rest = jnp.sum(weight * stats[:, :, 5 + 2 * which : 6 + 2 * which], axis=0)
        dnormed = pulled - (1.0 - rest) * label_row[:, which * width : (which + 1) * width]
        mean = (pull - (1.0 - rest) * label_logit) / D
        dsummed.append((inv_rms * (dnormed - scaled * mean)).astype(bf16))
    dsummed = to_all(jnp.concatenate(dsummed, axis=1), UNIT_CHIPS).reshape(count, 2 * width)

    far_dsummed = other_core(dsummed)
    dhidden = on_core(
        back_kernel,
        core,
        (dsummed, far_dsummed, down_weight, down_got),
        [whole(dsummed), whole(far_dsummed), rows_of(down_weight, FF_HALF), whole(down_got)],
        [((count, 2 * FF_HALF), bf16)],
        2 * gate_up_flops,
    )
    dhidden = exchange(dhidden.reshape(CHIPS, BLOCK, 2 * FF_HALF), WIDTH_CHIPS)
    dhidden = jnp.sum(dhidden.astype(f32), axis=0)
    cot = (dhidden * jnp.concatenate([silu_gate, silu_gate], axis=1)).astype(bf16)
    cot_own = to_all(cot, WIDTH_CHIPS).reshape(count, 2 * FF_HALF)
    cot_far = other_core(cot_own)
    done = sophia_half(core, turned_own, cot_own, up_moment, up_curvature, ())
    return tuple(sophia_half(far, turned_far, cot_far, up_moment, up_curvature, done))


def solution(mesh):
    fine = Mesh(mesh.devices.reshape(2, 4, 2, 4, 2), ("xl", "y", "core", "z", "xh"))
    dp = ("xl", "y", "core")
    tensor = ("z", "xh")
    both = P(dp, tensor)
    placed = (P(None, dp), both, both, P(tensor, dp), both, both, both, P(dp), P(dp))
    return jax.shard_map(
        on_device,
        mesh=fine,
        in_specs=placed,
        out_specs=(both, both, both),
        check_vma=False,
    )
```

```python
import itertools

import jax
import jax.numpy as jnp
from jax import lax
from jax.experimental import pallas as pl
from jax.experimental.pallas import tpu as pltpu
from jax.sharding import Mesh, PartitionSpec as P

D = 8192
FF_HALF = 896
V_HALF = 1024
BLOCK = 64
CHIPS = 8
PAD = 128
N_STATS = 8
STEP = 16384.0
TINY = 1e-30

beta_one = 0.965
beta_two = 0.95
rho_scale = 0.05
eps_norm = 1e-05

WIDTH_CHIPS = ("xl", "y")
UNIT_CHIPS = ("z", "xh")
MESH_SIZES = {"xl": 2, "y": 4, "core": 2, "z": 4, "xh": 2}
f32 = jnp.float32
bf16 = jnp.bfloat16
VMEM_LIMIT = 24 * 1024 * 1024


def other_core(value):
    return lax.ppermute(value, "core", [(0, 1), (1, 0)])


def partners(axes):
    names = tuple(MESH_SIZES)
    places = list(itertools.product(*(range(size) for size in MESH_SIZES.values())))
    groups = {}
    for number, place in enumerate(places):
        fixed = tuple(value for name, value in zip(names, place) if name not in axes)
        groups.setdefault(fixed, []).append(number)
    core = names.index("core")
    return [members[::-1] if places[members[0]][core] else members for members in groups.values()]


def exchange(blocks, axes):
    return lax.all_to_all(
        blocks, tuple(MESH_SIZES), split_axis=0, concat_axis=0, tiled=True, axis_index_groups=partners(axes)
    )


def to_all(block, axes):
    copies = jnp.broadcast_to(block[None], (CHIPS,) + block.shape)
    return exchange(copies, axes)


def block_rows(block):
    return slice(block * BLOCK, (block + 1) * BLOCK)


def join_cores(own, far):
    return jnp.concatenate(
        [own[block_rows(block)] + far[block_rows(CHIPS - 1 - block)] for block in range(CHIPS)], axis=0
    )


def reverse_rows(rows):
    return jnp.concatenate([rows[block_rows(CHIPS - 1 - block)] for block in range(CHIPS)], axis=0)


def reverse_blocks(rows):
    return rows.reshape((CHIPS, BLOCK) + rows.shape[1:])[::-1].reshape(rows.shape)


def together(*values):
    return lax.optimization_barrier(values)


def dot(left, right):
    return jnp.dot(left, right, preferred_element_type=f32)


def dot_rows(left, right):
    return lax.dot_general(left, right, (((1,), (1,)), ((), ())), preferred_element_type=f32)


def from_three(parts, count):
    parts = parts.astype(f32)
    return parts[..., :count] + parts[..., count : 2 * count] + parts[..., 2 * count : 3 * count]


def whole(array):
    return pl.BlockSpec(array.shape, lambda step, half: (0,) * array.ndim)


def columns_of(array, count):
    return pl.BlockSpec((array.shape[0], count), lambda step, half: (0, half[0]))


def rows_of(array, count):
    return pl.BlockSpec((count, array.shape[1]), lambda step, half: (half[0], 0))


def on_core(kernel, half, operands, specs, outs, flops, limit=VMEM_LIMIT):
    size = sum(operand.size * operand.dtype.itemsize for operand in operands)
    results = pl.pallas_call(
        kernel,
        out_shape=tuple(jax.ShapeDtypeStruct(shape, dtype) for shape, dtype in outs),
        grid_spec=pltpu.PrefetchScalarGridSpec(
            num_scalar_prefetch=1,
            grid=(1,),
            in_specs=specs,
            out_specs=tuple(whole(jax.ShapeDtypeStruct(*out)) for out in outs),
        ),
        compiler_params=pltpu.CompilerParams(vmem_limit_bytes=limit),
        cost_estimate=pl.CostEstimate(flops=flops, bytes_accessed=size, transcendentals=0),
    )(half.reshape(1), *operands)
    return results if len(outs) > 1 else results[0]


def gate_up_pack(half_ref, own_gate, own_up, got_gate, got_up, labels, out):
    core = half_ref[0]
    gate_sum = (own_gate[...].astype(f32) + got_gate[...].astype(f32)).astype(bf16)
    up_sum = (own_up[...].astype(f32) + got_up[...].astype(f32)).astype(bf16)
    for block in range(CHIPS):
        place = block + core * (CHIPS - 1 - 2 * block)
        rows = pl.ds(pl.multiple_of(place * BLOCK, BLOCK), BLOCK)
        out[rows, :FF_HALF] = gate_sum[block_rows(block)]
        out[rows, FF_HALF : 2 * FF_HALF] = up_sum[block_rows(block)]
        out[rows, 2 * FF_HALF :] = labels[...]


def branch_kernel(half_ref, own_part, far, down_far, out):
    out[...] = join_cores(own_part[...], dot(far[...], down_far[...])).astype(bf16)


def hidden_kernel(half_ref, both, hidden, silu_out):
    gate = jnp.zeros((BLOCK, FF_HALF), f32)
    upper = jnp.zeros((BLOCK, FF_HALF), f32)
    for chip in range(CHIPS):
        gate = gate + both[chip, :, :FF_HALF].astype(f32)
        upper = upper + both[chip, :, FF_HALF : 2 * FF_HALF].astype(f32)
    silu_gate = gate / (1.0 + jnp.exp(-gate))
    silu_out[...] = silu_gate
    rounded = (silu_gate * upper).astype(bf16)
    for chip in range(CHIPS):
        hidden[chip] = rounded


def squares_of(rows):
    wide = rows[...].astype(f32)
    return jnp.sum(wide * wide, axis=1, keepdims=True)


def exponent_of(values):
    return jnp.ceil(jnp.log2(jnp.maximum(values, TINY)))


def logits_kernel(half_ref, rows, far_rows, head, head_got, out):
    raw = join_cores(dot(rows[...], head[...]), dot(far_rows[...], head_got[...]))
    squares = join_cores(squares_of(rows), squares_of(far_rows))
    level = exponent_of(jnp.max(jnp.abs(raw), axis=1, keepdims=True))
    out[:, :V_HALF] = jnp.round(raw * (STEP * jnp.exp2(-level))).astype(jnp.int32).astype(jnp.int16)
    square_level = exponent_of(squares)
    units = squares * (STEP * jnp.exp2(-square_level))
    high = jnp.floor(units)
    low = jnp.floor((units - high) * STEP)
    lane = lax.broadcasted_iota(jnp.int32, (rows.shape[0], PAD), 1)
    tail = jnp.where(lane == 0, level, jnp.where(lane == 1, high, jnp.where(lane == 2, low, square_level)))
    out[:, V_HALF:] = tail.astype(jnp.int32).astype(jnp.int16)


def pack_three(values):
    lane = lax.broadcasted_iota(jnp.int32, values.shape, 1)
    values = jnp.where(lane < N_STATS, values, 0.0)
    high = values.astype(bf16)
    rest = values - high.astype(f32)
    middle = rest.astype(bf16)
    low = (rest - middle.astype(f32)).astype(bf16)
    row = lax.broadcasted_iota(jnp.int32, (PAD, PAD), 0)
    lane = lax.broadcasted_iota(jnp.int32, (PAD, PAD), 1)
    by_one = (lane == row + N_STATS).astype(f32).astype(bf16)
    by_two = (lane == row + 2 * N_STATS).astype(f32).astype(bf16)
    return (high.astype(f32) + dot(middle, by_one) + dot(low, by_two)).astype(bf16)


def softmax_kernel(start_ref, raw, labels, out):
    total = jnp.zeros((BLOCK, V_HALF), f32)
    squares = jnp.zeros((BLOCK, 1), f32)
    for chip in range(CHIPS):
        tail = raw[chip, :, V_HALF:].astype(jnp.int32).astype(f32)
        scale = jnp.exp2(tail[:, 0:1]) / STEP
        total = total + raw[chip, :, :V_HALF].astype(jnp.int32).astype(f32) * scale
        square_scale = jnp.exp2(tail[:, 3:4]) / STEP
        squares = squares + (tail[:, 1:2] + tail[:, 2:3] / STEP) * square_scale
    inv_rms = lax.rsqrt(squares / D + eps_norm)
    logits = total * inv_rms
    top = jnp.max(logits, axis=1, keepdims=True)
    exp_terms = jnp.exp(logits - top)
    short = exp_terms.astype(bf16)
    rounded = short.astype(f32)
    ids = start_ref[0] + lax.broadcasted_iota(jnp.int32, (BLOCK, V_HALF), 1)
    stats = [
        top,
        inv_rms,
        jnp.sum(exp_terms, axis=1, keepdims=True),
        jnp.sum(rounded * logits, axis=1, keepdims=True),
    ]
    for which in range(2):
        hot = labels[:, which : which + 1] == ids
        stats.append(jnp.sum(jnp.where(hot, logits, 0.0), axis=1, keepdims=True))
        stats.append(jnp.sum(jnp.where(hot, exp_terms - rounded, 0.0), axis=1, keepdims=True))
    lane = lax.broadcasted_iota(jnp.int32, (BLOCK, PAD), 1)
    table = jnp.zeros((BLOCK, PAD), f32)
    for place, value in enumerate(stats):
        table = jnp.where(lane == place, value, table)
    packed = pack_three(table)
    for chip in range(CHIPS):
        out[chip, :, :V_HALF] = short
        out[chip, :, V_HALF:] = packed


def pull_back(half_ref, own, far, head_own, head_far, out):
    count = own.shape[0]
    row = lax.broadcasted_iota(jnp.int32, (PAD, PAD), 0)
    lane = lax.broadcasted_iota(jnp.int32, (PAD, PAD), 1)
    gather = ((row % N_STATS == lane) & (row < 3 * N_STATS)).astype(f32).astype(bf16)
    stats_own = dot(own[:, V_HALF:], gather)
    stats_far = reverse_rows(dot(far[:, V_HALF:], gather))
    top = jnp.maximum(stats_own[:, 0:1], stats_far[:, 0:1])
    scale_own = jnp.exp(stats_own[:, 0:1] - top)
    scale_far = jnp.exp(stats_far[:, 0:1] - top)
    pulled = scale_own * dot_rows(own[:, :V_HALF], head_own[...])
    pulled = pulled + scale_far * reverse_rows(dot_rows(far[:, :V_HALF], head_far[...]))
    width = pulled.shape[1]
    out[:, :width] = pulled.astype(bf16)
    lane = lax.broadcasted_iota(jnp.int32, (count, PAD), 1)
    is_sum = (lane == 2) | (lane == 3) | (lane == 5) | (lane == 7)
    both = jnp.where(is_sum, scale_own * stats_own + scale_far * stats_far, stats_own + stats_far)
    both = jnp.where(lane == 0, top, jnp.where(lane == 1, stats_own, both))
    out[:, width:] = pack_three(both)


def back_kernel(half_ref, dsummed, far_dsummed, down, down_got, out):
    width = down.shape[1]
    for which in range(2):
        place = slice(which * width, (which + 1) * width)
        part = join_cores(dot_rows(dsummed[:, place], down[...]), dot_rows(far_dsummed[:, place], down_got[...]))
        out[:, which * FF_HALF : (which + 1) * FF_HALF] = part.astype(bf16)


def step_kernel(half_ref, turned, cot, moment_ref, curve_ref, *rest):
    new_moment, new_curve, update = rest[-3:]
    grad_true = dot(turned[...], cot[:, :FF_HALF])
    grad_sampled = dot(turned[...], cot[:, FF_HALF:])
    moment = beta_one * moment_ref[...] + (1.0 - beta_one) * grad_true
    curve = beta_two * curve_ref[...] + (1.0 - beta_two) * grad_sampled * grad_sampled
    new_moment[...] = moment
    new_curve[...] = curve
    divisor = rho_scale * curve
    inverse = pl.reciprocal(divisor, approx=True)
    inverse = inverse * (2.0 - divisor * inverse)
    update[...] = jnp.clip(moment * inverse, -1.0, 1.0)


def sophia_half(half, turned, cot, moment, curve, done):
    tall = 128
    rows, count = turned.shape
    big = pl.BlockSpec((tall, FF_HALF), lambda step, half: (step, half[0]))
    shape = jax.ShapeDtypeStruct(moment.shape, f32)
    kept = [pl.BlockSpec(memory_space=pl.ANY) for _ in done]
    return pl.pallas_call(
        step_kernel,
        out_shape=(shape, shape, shape),
        grid_spec=pltpu.PrefetchScalarGridSpec(
            num_scalar_prefetch=1,
            grid=(rows // tall,),
            in_specs=[
                pl.BlockSpec((tall, count), lambda step, half: (step, 0)),
                whole(cot),
                big,
                big,
            ]
            + kept,
            out_specs=(big, big, big),
        ),
        input_output_aliases={5 + which: which for which in range(len(done))},
        compiler_params=pltpu.CompilerParams(vmem_limit_bytes=VMEM_LIMIT),
        cost_estimate=pl.CostEstimate(flops=950000000, bytes_accessed=11000000, transcendentals=0),
    )(half.reshape(1), turned, cot, moment, curve, *done)


def own_part(array, index, axis):
    keep = lax.dynamic_index_in_dim(array, index, axis, keepdims=False)
    send = lax.dynamic_index_in_dim(array, 1 - index, axis, keepdims=False)
    return keep, send


def label_rows(labels, head_weight, unit_chip):
    ids = unit_chip * (2 * V_HALF) + lax.broadcasted_iota(jnp.int32, (1, 2 * V_HALF), 1)
    parts = []
    for which in range(2):
        hot = (labels[:, which : which + 1] == ids).astype(bf16)
        parts.append(dot_rows(hot, head_weight).astype(bf16))
    return jnp.concatenate(parts, axis=1).reshape(2, 2, 2, BLOCK, -1)


def near_label_rows(rows):
    keep, send = own_part(rows, lax.axis_index("z") % 2, 1)
    return keep, lax.ppermute(send, "z", [(0, 1), (1, 0), (2, 3), (3, 2)])


def plane_label_rows(near, got):
    rows = near + got
    keep, send = own_part(rows, lax.axis_index("z") // 2, 0)
    rows = keep + lax.ppermute(send, "z", [(0, 2), (2, 0), (1, 3), (3, 1)])
    return own_part(rows, lax.axis_index("xh"), 0)


def other_plane(rows):
    return lax.ppermute(rows, "xh", [(0, 1), (1, 0)])


def on_device(
    tokens,
    gate_weight,
    up_weight,
    down_weight,
    head_weight,
    up_moment,
    up_curvature,
    true_labels,
    sampled_labels,
):
    core = lax.axis_index("core").astype(jnp.int32)
    far = 1 - core
    unit_chip = lax.axis_index(UNIT_CHIPS)
    count, width = tokens.shape

    labels = jnp.stack([true_labels, sampled_labels], axis=1)
    far_labels = other_core(labels)
    labels = jnp.where(
        core == 0,
        jnp.concatenate([labels, far_labels], axis=0),
        jnp.concatenate([far_labels, labels], axis=0),
    )
    digits = jnp.concatenate([labels // PAD, labels % PAD], axis=1).astype(bf16)
    digits = jnp.pad(digits, ((0, 0), (0, PAD - 4)))

    gate_up_flops = 4 * count * width * FF_HALF

    def gate_up(half):
        gate = lax.dynamic_slice_in_dim(gate_weight, half * FF_HALF, FF_HALF, 1)
        upper = lax.dynamic_slice_in_dim(up_weight, half * FF_HALF, FF_HALF, 1)
        return dot(tokens, gate).astype(bf16), dot(tokens, upper).astype(bf16)

    far_gate, far_up = gate_up(far)
    got_gate, got_up = other_core(far_gate), other_core(far_up)
    own_gate, own_up = gate_up(core)
    operands = (own_gate, own_up, got_gate, got_up, digits)
    both = on_core(
        gate_up_pack,
        core,
        operands,
        [whole(operand) for operand in operands],
        [((count, 2 * FF_HALF + PAD), bf16)],
        1000000,
    )
    both, sent_head, sent_down = together(both, head_weight, down_weight)
    head_send = lax.dynamic_slice_in_dim(sent_head, far * V_HALF, V_HALF, 1)
    down_send = lax.dynamic_slice_in_dim(sent_down, far * FF_HALF, FF_HALF, 0)
    both, head_got, down_got = together(
        exchange(both.reshape(CHIPS, BLOCK, 2 * FF_HALF + PAD), WIDTH_CHIPS),
        other_core(head_send),
        other_core(down_send),
    )
    hidden, silu_gate = on_core(
        hidden_kernel,
        core,
        (both,),
        [whole(both)],
        [((CHIPS, BLOCK, FF_HALF), bf16), ((BLOCK, FF_HALF), f32)],
        1000000,
    )

    hidden, digits = together(hidden, both)
    digits = digits[:, :, 2 * FF_HALF : 2 * FF_HALF + 4].astype(jnp.int32)
    all_labels = digits[:, :, :2] * PAD + digits[:, :, 2:]
    all_labels = jnp.where(core == 0, all_labels, all_labels[::-1]).reshape(count, 2)
    width_chip = lax.axis_index(WIDTH_CHIPS)
    hidden_own, label_row, labels = together(
        exchange(hidden, WIDTH_CHIPS),
        label_rows(all_labels, head_weight, unit_chip),
        lax.dynamic_slice_in_dim(all_labels, width_chip * BLOCK, BLOCK, 0),
    )
    hidden_own = hidden_own.reshape(count, FF_HALF)
    hidden_far = other_core(hidden_own)
    own_part = dot(hidden_own, lax.dynamic_slice_in_dim(down_weight, core * FF_HALF, FF_HALF, 0))
    branch = on_core(
        branch_kernel,
        core,
        (own_part, hidden_far, down_weight),
        [
            whole(own_part),
            whole(hidden_far),
            pl.BlockSpec((FF_HALF, width), lambda step, half: (1 - half[0], 0)),
        ],
        [((count, width), bf16)],
        gate_up_flops,
    )
    branch = exchange(branch.reshape(CHIPS, BLOCK, width), UNIT_CHIPS)
    branch = jnp.sum(branch.astype(f32), axis=0)
    own_tokens = lax.dynamic_slice_in_dim(tokens, unit_chip * BLOCK, BLOCK, 0)
    summed = own_tokens.astype(f32) + branch
    rows = to_all(summed.astype(bf16), UNIT_CHIPS).reshape(count, width)

    far_rows = other_core(rows)
    logit_flops = 4 * count * width * V_HALF
    raw = on_core(
        logits_kernel,
        core,
        (rows, far_rows, head_weight, head_got),
        [whole(rows), whole(far_rows), columns_of(head_weight, V_HALF), whole(head_got)],
        [((count, V_HALF + PAD), jnp.int16)],
        logit_flops,
    )
    raw, label_row = together(raw, label_row)
    raw, label_row = together(
        exchange(raw.reshape(CHIPS, BLOCK, V_HALF + PAD), WIDTH_CHIPS), near_label_rows(label_row)
    )
    vocab_start = ((unit_chip * 2 + core) * V_HALF).astype(jnp.int32)
    packed = on_core(
        softmax_kernel,
        vocab_start,
        (raw, labels),
        [whole(raw), whole(labels)],
        [((CHIPS, BLOCK, V_HALF + PAD), bf16)],
        1000000,
    )
    packed, token_rows, label_row = together(packed, tokens, label_row)
    turned = token_rows.T
    turned_reverse = reverse_blocks(token_rows).T
    packed_own, turned_own, turned_far, label_row = together(
        exchange(packed, WIDTH_CHIPS),
        jnp.where(core == 0, turned, turned_reverse),
        jnp.where(core == 0, turned_reverse, turned),
        plane_label_rows(*label_row),
    )
    label_row, label_sent = label_row
    packed_own = packed_own.reshape(count, V_HALF + PAD)
    packed_far = other_core(packed_own)
    packed = on_core(
        pull_back,
        core,
        (packed_own, packed_far, head_weight, head_weight),
        [
            whole(packed_own),
            whole(packed_far),
            pl.BlockSpec((width, V_HALF), lambda step, half: (0, half[0])),
            pl.BlockSpec((width, V_HALF), lambda step, half: (0, 1 - half[0])),
        ],
        [((count, width + PAD), bf16)],
        logit_flops,
    )
    packed, label_sent = together(packed, label_sent)
    packed, label_got = together(
        exchange(packed.reshape(CHIPS, BLOCK, width + PAD), UNIT_CHIPS), other_plane(label_sent)
    )
    label_row = label_row.astype(f32) + label_got.astype(f32)
    stats = from_three(packed[:, :, width:], N_STATS)
    row_top = jnp.max(stats[:, :, 0:1], axis=0, keepdims=True)
    weight = jnp.exp(stats[:, :, 0:1] - row_top)
    weight = weight / jnp.sum(weight * stats[:, :, 2:3], axis=0, keepdims=True)
    pulled = jnp.sum(weight * packed[:, :, :width].astype(f32), axis=0)
    pull = jnp.sum(weight * stats[:, :, 3:4], axis=0)
    inv_rms = stats[0, :, 1:2]
    scaled = summed * inv_rms
    dsummed = []
    for which in range(2):
        label_logit = jnp.sum(stats[:, :, 4 + 2 * which : 5 + 2 * which], axis=0)
        rest = jnp.sum(weight * stats[:, :, 5 + 2 * which : 6 + 2 * which], axis=0)
        dnormed = pulled - (1.0 - rest) * label_row[:, which * width : (which + 1) * width]
        mean = (pull - (1.0 - rest) * label_logit) / D
        dsummed.append((inv_rms * (dnormed - scaled * mean)).astype(bf16))
    dsummed = to_all(jnp.concatenate(dsummed, axis=1), UNIT_CHIPS).reshape(count, 2 * width)

    far_dsummed = other_core(dsummed)
    dhidden = on_core(
        back_kernel,
        core,
        (dsummed, far_dsummed, down_weight, down_got),
        [whole(dsummed), whole(far_dsummed), rows_of(down_weight, FF_HALF), whole(down_got)],
        [((count, 2 * FF_HALF), bf16)],
        2 * gate_up_flops,
    )
    dhidden = exchange(dhidden.reshape(CHIPS, BLOCK, 2 * FF_HALF), WIDTH_CHIPS)
    dhidden = jnp.sum(dhidden.astype(f32), axis=0)
    cot = (dhidden * jnp.concatenate([silu_gate, silu_gate], axis=1)).astype(bf16)
    cot_own = to_all(cot, WIDTH_CHIPS).reshape(count, 2 * FF_HALF)
    cot_far = other_core(cot_own)
    done = sophia_half(core, turned_own, cot_own, up_moment, up_curvature, ())
    return tuple(sophia_half(far, turned_far, cot_far, up_moment, up_curvature, done))


def solution(mesh):
    fine = Mesh(mesh.devices.reshape(2, 4, 2, 4, 2), ("xl", "y", "core", "z", "xh"))
    dp = ("xl", "y", "core")
    tensor = ("z", "xh")
    both = P(dp, tensor)
    placed = (P(None, dp), both, both, P(tensor, dp), both, both, both, P(dp), P(dp))
    return jax.shard_map(
        on_device,
        mesh=fine,
        in_specs=placed,
        out_specs=(both, both, both),
        check_vma=False,
    )
```

```python
import itertools

import jax
import jax.numpy as jnp
from jax import lax
from jax.experimental import pallas as pl
from jax.experimental.pallas import tpu as pltpu
from jax.sharding import Mesh, PartitionSpec as P

D = 8192
FF_HALF = 896
V_HALF = 1024
BLOCK = 64
CHIPS = 8
PAD = 128
N_STATS = 8
STEP = 16384.0
TINY = 1e-30

beta_one = 0.965
beta_two = 0.95
rho_scale = 0.05
eps_norm = 1e-05

WIDTH_CHIPS = ("xl", "y")
UNIT_CHIPS = ("z", "xh")
MESH_SIZES = {"xl": 2, "y": 4, "core": 2, "z": 4, "xh": 2}
f32 = jnp.float32
bf16 = jnp.bfloat16
VMEM_LIMIT = 24 * 1024 * 1024


def other_core(value):
    return lax.ppermute(value, "core", [(0, 1), (1, 0)])


def partners(axes):
    names = tuple(MESH_SIZES)
    places = list(itertools.product(*(range(size) for size in MESH_SIZES.values())))
    groups = {}
    for number, place in enumerate(places):
        fixed = tuple(value for name, value in zip(names, place) if name not in axes)
        groups.setdefault(fixed, []).append(number)
    core = names.index("core")
    return [members[::-1] if places[members[0]][core] else members for members in groups.values()]


def exchange(blocks, axes):
    return lax.all_to_all(
        blocks, tuple(MESH_SIZES), split_axis=0, concat_axis=0, tiled=True, axis_index_groups=partners(axes)
    )


def to_all(block, axes):
    copies = jnp.broadcast_to(block[None], (CHIPS,) + block.shape)
    return exchange(copies, axes)


def block_rows(block):
    return slice(block * BLOCK, (block + 1) * BLOCK)


def join_cores(own, far):
    return jnp.concatenate(
        [own[block_rows(block)] + far[block_rows(CHIPS - 1 - block)] for block in range(CHIPS)], axis=0
    )


def reverse_rows(rows):
    return jnp.concatenate([rows[block_rows(CHIPS - 1 - block)] for block in range(CHIPS)], axis=0)


def reverse_blocks(rows):
    return rows.reshape((CHIPS, BLOCK) + rows.shape[1:])[::-1].reshape(rows.shape)


def together(*values):
    return lax.optimization_barrier(values)


def dot(left, right):
    return jnp.dot(left, right, preferred_element_type=f32)


def dot_rows(left, right):
    return lax.dot_general(left, right, (((1,), (1,)), ((), ())), preferred_element_type=f32)


def from_three(parts, count):
    parts = parts.astype(f32)
    return parts[..., :count] + parts[..., count : 2 * count] + parts[..., 2 * count : 3 * count]


def whole(array):
    return pl.BlockSpec(array.shape, lambda step, half: (0,) * array.ndim)


def columns_of(array, count):
    return pl.BlockSpec((array.shape[0], count), lambda step, half: (0, half[0]))


def rows_of(array, count):
    return pl.BlockSpec((count, array.shape[1]), lambda step, half: (half[0], 0))


def on_core(kernel, half, operands, specs, outs, flops, limit=VMEM_LIMIT):
    size = sum(operand.size * operand.dtype.itemsize for operand in operands)
    results = pl.pallas_call(
        kernel,
        out_shape=tuple(jax.ShapeDtypeStruct(shape, dtype) for shape, dtype in outs),
        grid_spec=pltpu.PrefetchScalarGridSpec(
            num_scalar_prefetch=1,
            grid=(1,),
            in_specs=specs,
            out_specs=tuple(whole(jax.ShapeDtypeStruct(*out)) for out in outs),
        ),
        compiler_params=pltpu.CompilerParams(vmem_limit_bytes=limit),
        cost_estimate=pl.CostEstimate(flops=flops, bytes_accessed=size, transcendentals=0),
    )(half.reshape(1), *operands)
    return results if len(outs) > 1 else results[0]


def gate_up_pack(half_ref, own_gate, own_up, got_gate, got_up, out):
    core = half_ref[0]
    gate_sum = (own_gate[...].astype(f32) + got_gate[...].astype(f32)).astype(bf16)
    up_sum = (own_up[...].astype(f32) + got_up[...].astype(f32)).astype(bf16)
    for block in range(CHIPS):
        place = block + core * (CHIPS - 1 - 2 * block)
        rows = pl.ds(pl.multiple_of(place * BLOCK, BLOCK), BLOCK)
        out[rows, :FF_HALF] = gate_sum[block_rows(block)]
        out[rows, FF_HALF : 2 * FF_HALF] = up_sum[block_rows(block)]


def branch_kernel(half_ref, own_part, far, down_far, out):
    out[...] = join_cores(own_part[...], dot(far[:, :FF_HALF], down_far[...])).astype(bf16)


def hidden_kernel(half_ref, both, labels, hidden, silu_out):
    gate = jnp.zeros((BLOCK, FF_HALF), f32)
    upper = jnp.zeros((BLOCK, FF_HALF), f32)
    for chip in range(CHIPS):
        gate = gate + both[chip, :, :FF_HALF].astype(f32)
        upper = upper + both[chip, :, FF_HALF : 2 * FF_HALF].astype(f32)
    silu_gate = gate / (1.0 + jnp.exp(-gate))
    silu_out[...] = silu_gate
    rounded = (silu_gate * upper).astype(bf16)
    for chip in range(CHIPS):
        hidden[chip, :, :FF_HALF] = rounded
        hidden[chip, :, FF_HALF:] = labels[...]


def squares_of(rows):
    wide = rows[...].astype(f32)
    return jnp.sum(wide * wide, axis=1, keepdims=True)


def exponent_of(values):
    return jnp.ceil(jnp.log2(jnp.maximum(values, TINY)))


def logits_kernel(half_ref, rows, far_rows, head, head_got, out):
    raw = join_cores(dot(rows[...], head[...]), dot(far_rows[...], head_got[...]))
    squares = join_cores(squares_of(rows), squares_of(far_rows))
    level = exponent_of(jnp.max(jnp.abs(raw), axis=1, keepdims=True))
    out[:, :V_HALF] = jnp.round(raw * (STEP * jnp.exp2(-level))).astype(jnp.int32).astype(jnp.int16)
    square_level = exponent_of(squares)
    units = squares * (STEP * jnp.exp2(-square_level))
    high = jnp.floor(units)
    low = jnp.floor((units - high) * STEP)
    lane = lax.broadcasted_iota(jnp.int32, (rows.shape[0], PAD), 1)
    tail = jnp.where(lane == 0, level, jnp.where(lane == 1, high, jnp.where(lane == 2, low, square_level)))
    out[:, V_HALF:] = tail.astype(jnp.int32).astype(jnp.int16)


def pack_three(values):
    lane = lax.broadcasted_iota(jnp.int32, values.shape, 1)
    values = jnp.where(lane < N_STATS, values, 0.0)
    high = values.astype(bf16)
    rest = values - high.astype(f32)
    middle = rest.astype(bf16)
    low = (rest - middle.astype(f32)).astype(bf16)
    row = lax.broadcasted_iota(jnp.int32, (PAD, PAD), 0)
    lane = lax.broadcasted_iota(jnp.int32, (PAD, PAD), 1)
    by_one = (lane == row + N_STATS).astype(f32).astype(bf16)
    by_two = (lane == row + 2 * N_STATS).astype(f32).astype(bf16)
    return (high.astype(f32) + dot(middle, by_one) + dot(low, by_two)).astype(bf16)


def softmax_kernel(start_ref, raw, labels, out):
    total = jnp.zeros((BLOCK, V_HALF), f32)
    squares = jnp.zeros((BLOCK, 1), f32)
    for chip in range(CHIPS):
        tail = raw[chip, :, V_HALF:].astype(jnp.int32).astype(f32)
        scale = jnp.exp2(tail[:, 0:1]) / STEP
        total = total + raw[chip, :, :V_HALF].astype(jnp.int32).astype(f32) * scale
        square_scale = jnp.exp2(tail[:, 3:4]) / STEP
        squares = squares + (tail[:, 1:2] + tail[:, 2:3] / STEP) * square_scale
    inv_rms = lax.rsqrt(squares / D + eps_norm)
    logits = total * inv_rms
    top = jnp.max(logits, axis=1, keepdims=True)
    exp_terms = jnp.exp(logits - top)
    short = exp_terms.astype(bf16)
    rounded = short.astype(f32)
    ids = start_ref[0] + lax.broadcasted_iota(jnp.int32, (BLOCK, V_HALF), 1)
    stats = [
        top,
        inv_rms,
        jnp.sum(exp_terms, axis=1, keepdims=True),
        jnp.sum(rounded * logits, axis=1, keepdims=True),
    ]
    for which in range(2):
        hot = labels[:, which : which + 1] == ids
        stats.append(jnp.sum(jnp.where(hot, logits, 0.0), axis=1, keepdims=True))
        stats.append(jnp.sum(jnp.where(hot, exp_terms - rounded, 0.0), axis=1, keepdims=True))
    lane = lax.broadcasted_iota(jnp.int32, (BLOCK, PAD), 1)
    table = jnp.zeros((BLOCK, PAD), f32)
    for place, value in enumerate(stats):
        table = jnp.where(lane == place, value, table)
    packed = pack_three(table)
    for chip in range(CHIPS):
        out[chip, :, :V_HALF] = short
        out[chip, :, V_HALF:] = packed


def pull_back(half_ref, own, far, head_own, head_far, out):
    count = own.shape[0]
    row = lax.broadcasted_iota(jnp.int32, (PAD, PAD), 0)
    lane = lax.broadcasted_iota(jnp.int32, (PAD, PAD), 1)
    gather = ((row % N_STATS == lane) & (row < 3 * N_STATS)).astype(f32).astype(bf16)
    stats_own = dot(own[:, V_HALF:], gather)
    stats_far = reverse_rows(dot(far[:, V_HALF:], gather))
    top = jnp.maximum(stats_own[:, 0:1], stats_far[:, 0:1])
    scale_own = jnp.exp(stats_own[:, 0:1] - top)
    scale_far = jnp.exp(stats_far[:, 0:1] - top)
    pulled = scale_own * dot_rows(own[:, :V_HALF], head_own[...])
    pulled = pulled + scale_far * reverse_rows(dot_rows(far[:, :V_HALF], head_far[...]))
    width = pulled.shape[1]
    out[:, :width] = pulled.astype(bf16)
    lane = lax.broadcasted_iota(jnp.int32, (count, PAD), 1)
    is_sum = (lane == 2) | (lane == 3) | (lane == 5) | (lane == 7)
    both = jnp.where(is_sum, scale_own * stats_own + scale_far * stats_far, stats_own + stats_far)
    both = jnp.where(lane == 0, top, jnp.where(lane == 1, stats_own, both))
    out[:, width:] = pack_three(both)


def back_kernel(half_ref, dsummed, far_dsummed, down, down_got, out):
    width = down.shape[1]
    for which in range(2):
        place = slice(which * width, (which + 1) * width)
        part = join_cores(dot_rows(dsummed[:, place], down[...]), dot_rows(far_dsummed[:, place], down_got[...]))
        out[:, which * FF_HALF : (which + 1) * FF_HALF] = part.astype(bf16)


def step_kernel(half_ref, turned, cot, moment_ref, curve_ref, *rest):
    new_moment, new_curve, update = rest[-3:]
    grad_true = dot(turned[...], cot[:, :FF_HALF])
    grad_sampled = dot(turned[...], cot[:, FF_HALF:])
    moment = beta_one * moment_ref[...] + (1.0 - beta_one) * grad_true
    curve = beta_two * curve_ref[...] + (1.0 - beta_two) * grad_sampled * grad_sampled
    new_moment[...] = moment
    new_curve[...] = curve
    divisor = rho_scale * curve
    inverse = pl.reciprocal(divisor, approx=True)
    inverse = inverse * (2.0 - divisor * inverse)
    update[...] = jnp.clip(moment * inverse, -1.0, 1.0)


def sophia_half(half, turned, cot, moment, curve, done):
    tall = 128
    rows, count = turned.shape
    big = pl.BlockSpec((tall, FF_HALF), lambda step, half: (step, half[0]))
    shape = jax.ShapeDtypeStruct(moment.shape, f32)
    kept = [pl.BlockSpec(memory_space=pl.ANY) for _ in done]
    return pl.pallas_call(
        step_kernel,
        out_shape=(shape, shape, shape),
        grid_spec=pltpu.PrefetchScalarGridSpec(
            num_scalar_prefetch=1,
            grid=(rows // tall,),
            in_specs=[
                pl.BlockSpec((tall, count), lambda step, half: (step, 0)),
                whole(cot),
                big,
                big,
            ]
            + kept,
            out_specs=(big, big, big),
        ),
        input_output_aliases={5 + which: which for which in range(len(done))},
        compiler_params=pltpu.CompilerParams(vmem_limit_bytes=VMEM_LIMIT),
        cost_estimate=pl.CostEstimate(flops=950000000, bytes_accessed=11000000, transcendentals=0),
    )(half.reshape(1), turned, cot, moment, curve, *done)


def own_part(array, index, axis):
    keep = lax.dynamic_index_in_dim(array, index, axis, keepdims=False)
    send = lax.dynamic_index_in_dim(array, 1 - index, axis, keepdims=False)
    return keep, send


def label_rows(labels, head_weight, unit_chip):
    ids = unit_chip * (2 * V_HALF) + lax.broadcasted_iota(jnp.int32, (1, 2 * V_HALF), 1)
    parts = []
    for which in range(2):
        hot = (labels[:, which : which + 1] == ids).astype(bf16)
        parts.append(dot_rows(hot, head_weight).astype(bf16))
    return jnp.concatenate(parts, axis=1).reshape(2, 2, 2, BLOCK, -1)


def near_label_rows(rows):
    keep, send = own_part(rows, lax.axis_index("z") % 2, 1)
    return keep, lax.ppermute(send, "z", [(0, 1), (1, 0), (2, 3), (3, 2)])


def plane_label_rows(near, got):
    rows = near + got
    keep, send = own_part(rows, lax.axis_index("z") // 2, 0)
    rows = keep + lax.ppermute(send, "z", [(0, 2), (2, 0), (1, 3), (3, 1)])
    return own_part(rows, lax.axis_index("xh"), 0)


def other_plane(rows):
    return lax.ppermute(rows, "xh", [(0, 1), (1, 0)])


def on_device(
    tokens,
    gate_weight,
    up_weight,
    down_weight,
    head_weight,
    up_moment,
    up_curvature,
    true_labels,
    sampled_labels,
):
    core = lax.axis_index("core").astype(jnp.int32)
    far = 1 - core
    unit_chip = lax.axis_index(UNIT_CHIPS)
    count, width = tokens.shape

    labels = jnp.stack([true_labels, sampled_labels], axis=1)
    far_labels = other_core(labels)
    labels = jnp.where(
        core == 0,
        jnp.concatenate([labels, far_labels], axis=0),
        jnp.concatenate([far_labels, labels], axis=0),
    )
    digits = jnp.concatenate([labels // PAD, labels % PAD], axis=1).astype(bf16)
    digits = jnp.pad(digits, ((0, 0), (0, PAD - 4)))

    gate_up_flops = 4 * count * width * FF_HALF

    def gate_up(half):
        gate = lax.dynamic_slice_in_dim(gate_weight, half * FF_HALF, FF_HALF, 1)
        upper = lax.dynamic_slice_in_dim(up_weight, half * FF_HALF, FF_HALF, 1)
        return dot(tokens, gate).astype(bf16), dot(tokens, upper).astype(bf16)

    far_gate, far_up = gate_up(far)
    got_gate, got_up = other_core(far_gate), other_core(far_up)
    own_gate, own_up = gate_up(core)
    operands = (own_gate, own_up, got_gate, got_up)
    both = on_core(
        gate_up_pack,
        core,
        operands,
        [whole(operand) for operand in operands],
        [((count, 2 * FF_HALF), bf16)],
        1000000,
    )
    both, sent_head, sent_down = together(both, head_weight, down_weight)
    head_send = lax.dynamic_slice_in_dim(sent_head, far * V_HALF, V_HALF, 1)
    down_send = lax.dynamic_slice_in_dim(sent_down, far * FF_HALF, FF_HALF, 0)
    both, head_got, down_got = together(
        exchange(both.reshape(CHIPS, BLOCK, 2 * FF_HALF), WIDTH_CHIPS),
        other_core(head_send),
        other_core(down_send),
    )
    hidden, silu_gate = on_core(
        hidden_kernel,
        core,
        (both, digits),
        [whole(both), whole(digits)],
        [((CHIPS, BLOCK, FF_HALF + PAD), bf16), ((BLOCK, FF_HALF), f32)],
        1000000,
    )

    hidden_own = exchange(hidden, WIDTH_CHIPS).reshape(count, FF_HALF + PAD)
    hidden_far = other_core(hidden_own)
    own_part = dot(hidden_own[:, :FF_HALF], lax.dynamic_slice_in_dim(down_weight, core * FF_HALF, FF_HALF, 0))
    branch = on_core(
        branch_kernel,
        core,
        (own_part, hidden_far, down_weight),
        [
            whole(own_part),
            whole(hidden_far),
            pl.BlockSpec((FF_HALF, width), lambda step, half: (1 - half[0], 0)),
        ],
        [((count, width), bf16)],
        gate_up_flops,
    )
    branch, hidden_own = together(branch, hidden_own)
    digits = hidden_own[:, FF_HALF : FF_HALF + 4].astype(jnp.int32)
    all_labels = digits[:, :2] * PAD + digits[:, 2:]
    all_labels = jnp.where(core == 0, all_labels, reverse_blocks(all_labels))
    width_chip = lax.axis_index(WIDTH_CHIPS)
    branch, label_row, labels = together(
        exchange(branch.reshape(CHIPS, BLOCK, width), UNIT_CHIPS),
        label_rows(all_labels, head_weight, unit_chip),
        lax.dynamic_slice_in_dim(all_labels, width_chip * BLOCK, BLOCK, 0),
    )
    branch = jnp.sum(branch.astype(f32), axis=0)
    own_tokens = lax.dynamic_slice_in_dim(tokens, unit_chip * BLOCK, BLOCK, 0)
    summed = own_tokens.astype(f32) + branch
    rows = to_all(summed.astype(bf16), UNIT_CHIPS).reshape(count, width)

    far_rows = other_core(rows)
    logit_flops = 4 * count * width * V_HALF
    raw = on_core(
        logits_kernel,
        core,
        (rows, far_rows, head_weight, head_got),
        [whole(rows), whole(far_rows), columns_of(head_weight, V_HALF), whole(head_got)],
        [((count, V_HALF + PAD), jnp.int16)],
        logit_flops,
    )
    raw, label_row = together(raw, label_row)
    raw, label_row = together(
        exchange(raw.reshape(CHIPS, BLOCK, V_HALF + PAD), WIDTH_CHIPS), near_label_rows(label_row)
    )
    vocab_start = ((unit_chip * 2 + core) * V_HALF).astype(jnp.int32)
    packed = on_core(
        softmax_kernel,
        vocab_start,
        (raw, labels),
        [whole(raw), whole(labels)],
        [((CHIPS, BLOCK, V_HALF + PAD), bf16)],
        1000000,
    )
    packed, token_rows, label_row = together(packed, tokens, label_row)
    turned = token_rows.T
    turned_reverse = reverse_blocks(token_rows).T
    packed_own, turned_own, turned_far, label_row = together(
        exchange(packed, WIDTH_CHIPS),
        jnp.where(core == 0, turned, turned_reverse),
        jnp.where(core == 0, turned_reverse, turned),
        plane_label_rows(*label_row),
    )
    label_row, label_sent = label_row
    packed_own = packed_own.reshape(count, V_HALF + PAD)
    packed_far = other_core(packed_own)
    packed = on_core(
        pull_back,
        core,
        (packed_own, packed_far, head_weight, head_weight),
        [
            whole(packed_own),
            whole(packed_far),
            pl.BlockSpec((width, V_HALF), lambda step, half: (0, half[0])),
            pl.BlockSpec((width, V_HALF), lambda step, half: (0, 1 - half[0])),
        ],
        [((count, width + PAD), bf16)],
        logit_flops,
    )
    packed, label_sent = together(packed, label_sent)
    packed, label_got = together(
        exchange(packed.reshape(CHIPS, BLOCK, width + PAD), UNIT_CHIPS), other_plane(label_sent)
    )
    label_row = label_row.astype(f32) + label_got.astype(f32)
    stats = from_three(packed[:, :, width:], N_STATS)
    row_top = jnp.max(stats[:, :, 0:1], axis=0, keepdims=True)
    weight = jnp.exp(stats[:, :, 0:1] - row_top)
    weight = weight / jnp.sum(weight * stats[:, :, 2:3], axis=0, keepdims=True)
    pulled = jnp.sum(weight * packed[:, :, :width].astype(f32), axis=0)
    pull = jnp.sum(weight * stats[:, :, 3:4], axis=0)
    inv_rms = stats[0, :, 1:2]
    scaled = summed * inv_rms
    dsummed = []
    for which in range(2):
        label_logit = jnp.sum(stats[:, :, 4 + 2 * which : 5 + 2 * which], axis=0)
        rest = jnp.sum(weight * stats[:, :, 5 + 2 * which : 6 + 2 * which], axis=0)
        dnormed = pulled - (1.0 - rest) * label_row[:, which * width : (which + 1) * width]
        mean = (pull - (1.0 - rest) * label_logit) / D
        dsummed.append((inv_rms * (dnormed - scaled * mean)).astype(bf16))
    dsummed = to_all(jnp.concatenate(dsummed, axis=1), UNIT_CHIPS).reshape(count, 2 * width)

    far_dsummed = other_core(dsummed)
    dhidden = on_core(
        back_kernel,
        core,
        (dsummed, far_dsummed, down_weight, down_got),
        [whole(dsummed), whole(far_dsummed), rows_of(down_weight, FF_HALF), whole(down_got)],
        [((count, 2 * FF_HALF), bf16)],
        2 * gate_up_flops,
    )
    dhidden = exchange(dhidden.reshape(CHIPS, BLOCK, 2 * FF_HALF), WIDTH_CHIPS)
    dhidden = jnp.sum(dhidden.astype(f32), axis=0)
    cot = (dhidden * jnp.concatenate([silu_gate, silu_gate], axis=1)).astype(bf16)
    cot_own = to_all(cot, WIDTH_CHIPS).reshape(count, 2 * FF_HALF)
    cot_far = other_core(cot_own)
    done = sophia_half(core, turned_own, cot_own, up_moment, up_curvature, ())
    return tuple(sophia_half(far, turned_far, cot_far, up_moment, up_curvature, done))


def solution(mesh):
    fine = Mesh(mesh.devices.reshape(2, 4, 2, 4, 2), ("xl", "y", "core", "z", "xh"))
    dp = ("xl", "y", "core")
    tensor = ("z", "xh")
    both = P(dp, tensor)
    placed = (P(None, dp), both, both, P(tensor, dp), both, both, both, P(dp), P(dp))
    return jax.shard_map(
        on_device,
        mesh=fine,
        in_specs=placed,
        out_specs=(both, both, both),
        check_vma=False,
    )
```

```python
import itertools

import jax
import jax.numpy as jnp
from jax import lax
from jax.experimental import pallas as pl
from jax.experimental.pallas import tpu as pltpu
from jax.sharding import Mesh, PartitionSpec as P

D = 8192
FF_HALF = 896
V_HALF = 1024
BLOCK = 64
CHIPS = 8
PAD = 128
N_STATS = 8
STEP = 16384.0
TINY = 1e-30

beta_one = 0.965
beta_two = 0.95
rho_scale = 0.05
eps_norm = 1e-05

WIDTH_CHIPS = ("xl", "y")
UNIT_CHIPS = ("z", "xh")
MESH_SIZES = {"xl": 2, "y": 4, "core": 2, "z": 4, "xh": 2}
f32 = jnp.float32
bf16 = jnp.bfloat16
VMEM_LIMIT = 24 * 1024 * 1024


def other_core(value):
    return lax.ppermute(value, "core", [(0, 1), (1, 0)])


def partners(axes):
    names = tuple(MESH_SIZES)
    places = list(itertools.product(*(range(size) for size in MESH_SIZES.values())))
    groups = {}
    for number, place in enumerate(places):
        fixed = tuple(value for name, value in zip(names, place) if name not in axes)
        groups.setdefault(fixed, []).append(number)
    core = names.index("core")
    return [members[::-1] if places[members[0]][core] else members for members in groups.values()]


def exchange(blocks, axes):
    return lax.all_to_all(
        blocks, tuple(MESH_SIZES), split_axis=0, concat_axis=0, tiled=True, axis_index_groups=partners(axes)
    )


def to_all(block, axes):
    copies = jnp.broadcast_to(block[None], (CHIPS,) + block.shape)
    return exchange(copies, axes)


def block_rows(block):
    return slice(block * BLOCK, (block + 1) * BLOCK)


def join_cores(own, far):
    return jnp.concatenate(
        [own[block_rows(block)] + far[block_rows(CHIPS - 1 - block)] for block in range(CHIPS)], axis=0
    )


def reverse_rows(rows):
    return jnp.concatenate([rows[block_rows(CHIPS - 1 - block)] for block in range(CHIPS)], axis=0)


def reverse_blocks(rows):
    return rows.reshape((CHIPS, BLOCK) + rows.shape[1:])[::-1].reshape(rows.shape)


def together(*values):
    return lax.optimization_barrier(values)


def dot(left, right):
    return jnp.dot(left, right, preferred_element_type=f32)


def dot_rows(left, right):
    return lax.dot_general(left, right, (((1,), (1,)), ((), ())), preferred_element_type=f32)


def from_three(parts, count):
    parts = parts.astype(f32)
    return parts[..., :count] + parts[..., count : 2 * count] + parts[..., 2 * count : 3 * count]


def whole(array):
    return pl.BlockSpec(array.shape, lambda step, half: (0,) * array.ndim)


def columns_of(array, count):
    return pl.BlockSpec((array.shape[0], count), lambda step, half: (0, half[0]))


def rows_of(array, count):
    return pl.BlockSpec((count, array.shape[1]), lambda step, half: (half[0], 0))


def on_core(kernel, half, operands, specs, outs, flops, limit=VMEM_LIMIT):
    size = sum(operand.size * operand.dtype.itemsize for operand in operands)
    results = pl.pallas_call(
        kernel,
        out_shape=tuple(jax.ShapeDtypeStruct(shape, dtype) for shape, dtype in outs),
        grid_spec=pltpu.PrefetchScalarGridSpec(
            num_scalar_prefetch=1,
            grid=(1,),
            in_specs=specs,
            out_specs=tuple(whole(jax.ShapeDtypeStruct(*out)) for out in outs),
        ),
        compiler_params=pltpu.CompilerParams(vmem_limit_bytes=limit),
        cost_estimate=pl.CostEstimate(flops=flops, bytes_accessed=size, transcendentals=0),
    )(half.reshape(1), *operands)
    return results if len(outs) > 1 else results[0]


def gate_up_pack(half_ref, own_gate, own_up, got_gate, got_up, out):
    core = half_ref[0]
    gate_sum = (own_gate[...].astype(f32) + got_gate[...].astype(f32)).astype(bf16)
    up_sum = (own_up[...].astype(f32) + got_up[...].astype(f32)).astype(bf16)
    for block in range(CHIPS):
        place = block + core * (CHIPS - 1 - 2 * block)
        rows = pl.ds(pl.multiple_of(place * BLOCK, BLOCK), BLOCK)
        out[rows, :FF_HALF] = gate_sum[block_rows(block)]
        out[rows, FF_HALF : 2 * FF_HALF] = up_sum[block_rows(block)]


def branch_kernel(half_ref, own_part, far, down_far, out):
    out[...] = join_cores(own_part[...], dot(far[:, :FF_HALF], down_far[...])).astype(bf16)


def hidden_kernel(half_ref, both, labels, hidden, silu_out):
    gate = jnp.zeros((BLOCK, FF_HALF), f32)
    upper = jnp.zeros((BLOCK, FF_HALF), f32)
    for chip in range(CHIPS):
        gate = gate + both[chip, :, :FF_HALF].astype(f32)
        upper = upper + both[chip, :, FF_HALF : 2 * FF_HALF].astype(f32)
    silu_gate = gate / (1.0 + jnp.exp(-gate))
    silu_out[...] = silu_gate
    rounded = (silu_gate * upper).astype(bf16)
    for chip in range(CHIPS):
        hidden[chip, :, :FF_HALF] = rounded
        hidden[chip, :, FF_HALF:] = labels[...]


def squares_of(rows):
    wide = rows[...].astype(f32)
    return jnp.sum(wide * wide, axis=1, keepdims=True)


def exponent_of(values):
    return jnp.ceil(jnp.log2(jnp.maximum(values, TINY)))


def logits_kernel(half_ref, rows, far_rows, head, head_got, out):
    raw = join_cores(dot(rows[...], head[...]), dot(far_rows[...], head_got[...]))
    squares = join_cores(squares_of(rows), squares_of(far_rows))
    level = exponent_of(jnp.max(jnp.abs(raw), axis=1, keepdims=True))
    out[:, :V_HALF] = jnp.round(raw * (STEP * jnp.exp2(-level))).astype(jnp.int32).astype(jnp.int16)
    square_level = exponent_of(squares)
    units = squares * (STEP * jnp.exp2(-square_level))
    high = jnp.floor(units)
    low = jnp.floor((units - high) * STEP)
    lane = lax.broadcasted_iota(jnp.int32, (rows.shape[0], PAD), 1)
    tail = jnp.where(lane == 0, level, jnp.where(lane == 1, high, jnp.where(lane == 2, low, square_level)))
    out[:, V_HALF:] = tail.astype(jnp.int32).astype(jnp.int16)


def pack_three(values):
    lane = lax.broadcasted_iota(jnp.int32, values.shape, 1)
    values = jnp.where(lane < N_STATS, values, 0.0)
    high = values.astype(bf16)
    rest = values - high.astype(f32)
    middle = rest.astype(bf16)
    low = (rest - middle.astype(f32)).astype(bf16)
    row = lax.broadcasted_iota(jnp.int32, (PAD, PAD), 0)
    lane = lax.broadcasted_iota(jnp.int32, (PAD, PAD), 1)
    by_one = (lane == row + N_STATS).astype(f32).astype(bf16)
    by_two = (lane == row + 2 * N_STATS).astype(f32).astype(bf16)
    return (high.astype(f32) + dot(middle, by_one) + dot(low, by_two)).astype(bf16)


def softmax_kernel(start_ref, raw, labels, out):
    total = jnp.zeros((BLOCK, V_HALF), f32)
    squares = jnp.zeros((BLOCK, 1), f32)
    for chip in range(CHIPS):
        tail = raw[chip, :, V_HALF:].astype(jnp.int32).astype(f32)
        scale = jnp.exp2(tail[:, 0:1]) / STEP
        total = total + raw[chip, :, :V_HALF].astype(jnp.int32).astype(f32) * scale
        square_scale = jnp.exp2(tail[:, 3:4]) / STEP
        squares = squares + (tail[:, 1:2] + tail[:, 2:3] / STEP) * square_scale
    inv_rms = lax.rsqrt(squares / D + eps_norm)
    logits = total * inv_rms
    top = jnp.max(logits, axis=1, keepdims=True)
    exp_terms = jnp.exp(logits - top)
    short = exp_terms.astype(bf16)
    rounded = short.astype(f32)
    ids = start_ref[0] + lax.broadcasted_iota(jnp.int32, (BLOCK, V_HALF), 1)
    stats = [
        top,
        inv_rms,
        jnp.sum(exp_terms, axis=1, keepdims=True),
        jnp.sum(rounded * logits, axis=1, keepdims=True),
    ]
    for which in range(2):
        hot = labels[:, which : which + 1] == ids
        stats.append(jnp.sum(jnp.where(hot, logits, 0.0), axis=1, keepdims=True))
        stats.append(jnp.sum(jnp.where(hot, exp_terms - rounded, 0.0), axis=1, keepdims=True))
    lane = lax.broadcasted_iota(jnp.int32, (BLOCK, PAD), 1)
    table = jnp.zeros((BLOCK, PAD), f32)
    for place, value in enumerate(stats):
        table = jnp.where(lane == place, value, table)
    packed = pack_three(table)
    for chip in range(CHIPS):
        out[chip, :, :V_HALF] = short
        out[chip, :, V_HALF:] = packed


def pull_back(half_ref, own, far, head_own, head_far, out):
    count = own.shape[0]
    row = lax.broadcasted_iota(jnp.int32, (PAD, PAD), 0)
    lane = lax.broadcasted_iota(jnp.int32, (PAD, PAD), 1)
    gather = ((row % N_STATS == lane) & (row < 3 * N_STATS)).astype(f32).astype(bf16)
    stats_own = dot(own[:, V_HALF:], gather)
    stats_far = reverse_rows(dot(far[:, V_HALF:], gather))
    top = jnp.maximum(stats_own[:, 0:1], stats_far[:, 0:1])
    scale_own = jnp.exp(stats_own[:, 0:1] - top)
    scale_far = jnp.exp(stats_far[:, 0:1] - top)
    pulled = scale_own * dot_rows(own[:, :V_HALF], head_own[...])
    pulled = pulled + scale_far * reverse_rows(dot_rows(far[:, :V_HALF], head_far[...]))
    width = pulled.shape[1]
    out[:, :width] = pulled.astype(bf16)
    lane = lax.broadcasted_iota(jnp.int32, (count, PAD), 1)
    is_sum = (lane == 2) | (lane == 3) | (lane == 5) | (lane == 7)
    both = jnp.where(is_sum, scale_own * stats_own + scale_far * stats_far, stats_own + stats_far)
    both = jnp.where(lane == 0, top, jnp.where(lane == 1, stats_own, both))
    out[:, width:] = pack_three(both)


def back_kernel(half_ref, dsummed, far_dsummed, down, down_got, out):
    width = down.shape[1]
    for which in range(2):
        place = slice(which * width, (which + 1) * width)
        part = join_cores(dot_rows(dsummed[:, place], down[...]), dot_rows(far_dsummed[:, place], down_got[...]))
        out[:, which * FF_HALF : (which + 1) * FF_HALF] = part.astype(bf16)


def step_kernel(half_ref, turned, cot, moment_ref, curve_ref, *rest):
    new_moment, new_curve, update = rest[-3:]
    grad_true = dot(turned[...], cot[:, :FF_HALF])
    grad_sampled = dot(turned[...], cot[:, FF_HALF:])
    moment = beta_one * moment_ref[...] + (1.0 - beta_one) * grad_true
    curve = beta_two * curve_ref[...] + (1.0 - beta_two) * grad_sampled * grad_sampled
    new_moment[...] = moment
    new_curve[...] = curve
    divisor = rho_scale * curve
    inverse = pl.reciprocal(divisor, approx=True)
    inverse = inverse * (2.0 - divisor * inverse)
    update[...] = jnp.clip(moment * inverse, -1.0, 1.0)


def sophia_half(half, turned, cot, moment, curve, done):
    tall = 128
    rows, count = turned.shape
    big = pl.BlockSpec((tall, FF_HALF), lambda step, half: (step, half[0]))
    shape = jax.ShapeDtypeStruct(moment.shape, f32)
    kept = [pl.BlockSpec(memory_space=pl.ANY) for _ in done]
    return pl.pallas_call(
        step_kernel,
        out_shape=(shape, shape, shape),
        grid_spec=pltpu.PrefetchScalarGridSpec(
            num_scalar_prefetch=1,
            grid=(rows // tall,),
            in_specs=[
                pl.BlockSpec((tall, count), lambda step, half: (step, 0)),
                whole(cot),
                big,
                big,
            ]
            + kept,
            out_specs=(big, big, big),
        ),
        input_output_aliases={5 + which: which for which in range(len(done))},
        compiler_params=pltpu.CompilerParams(vmem_limit_bytes=VMEM_LIMIT),
        cost_estimate=pl.CostEstimate(flops=950000000, bytes_accessed=11000000, transcendentals=0),
    )(half.reshape(1), turned, cot, moment, curve, *done)


def own_part(array, index, axis):
    keep = lax.dynamic_index_in_dim(array, index, axis, keepdims=False)
    send = lax.dynamic_index_in_dim(array, 1 - index, axis, keepdims=False)
    return keep, send


def label_rows(labels, head_weight, unit_chip):
    ids = unit_chip * (2 * V_HALF) + lax.broadcasted_iota(jnp.int32, (1, 2 * V_HALF), 1)
    parts = []
    for which in range(2):
        hot = (labels[:, which : which + 1] == ids).astype(bf16)
        parts.append(dot_rows(hot, head_weight).astype(bf16))
    return jnp.concatenate(parts, axis=1).reshape(2, 2, 2, BLOCK, -1)


def near_label_rows(rows):
    keep, send = own_part(rows, lax.axis_index("z") % 2, 1)
    return keep, lax.ppermute(send, "z", [(0, 1), (1, 0), (2, 3), (3, 2)])


def plane_label_rows(near, got):
    rows = near + got
    keep, send = own_part(rows, lax.axis_index("z") // 2, 0)
    rows = keep + lax.ppermute(send, "z", [(0, 2), (2, 0), (1, 3), (3, 1)])
    return own_part(rows, lax.axis_index("xh"), 0)


def other_plane(rows):
    return lax.ppermute(rows, "xh", [(0, 1), (1, 0)])


def on_device(
    tokens,
    gate_weight,
    up_weight,
    down_weight,
    head_weight,
    up_moment,
    up_curvature,
    true_labels,
    sampled_labels,
):
    core = lax.axis_index("core").astype(jnp.int32)
    far = 1 - core
    unit_chip = lax.axis_index(UNIT_CHIPS)
    count, width = tokens.shape

    labels = jnp.stack([true_labels, sampled_labels], axis=1)
    far_labels = other_core(labels)
    labels = jnp.where(
        core == 0,
        jnp.concatenate([labels, far_labels], axis=0),
        jnp.concatenate([far_labels, labels], axis=0),
    )
    digits = jnp.concatenate([labels // PAD, labels % PAD], axis=1).astype(bf16)
    digits = jnp.pad(digits, ((0, 0), (0, PAD - 4)))

    gate_up_flops = 4 * count * width * FF_HALF

    def gate_up(half):
        gate = lax.dynamic_slice_in_dim(gate_weight, half * FF_HALF, FF_HALF, 1)
        upper = lax.dynamic_slice_in_dim(up_weight, half * FF_HALF, FF_HALF, 1)
        return dot(tokens, gate).astype(bf16), dot(tokens, upper).astype(bf16)

    far_gate, far_up = gate_up(far)
    got_gate, got_up = other_core(far_gate), other_core(far_up)
    own_gate, own_up = gate_up(core)
    operands = (own_gate, own_up, got_gate, got_up)
    both = on_core(
        gate_up_pack,
        core,
        operands,
        [whole(operand) for operand in operands],
        [((count, 2 * FF_HALF), bf16)],
        1000000,
    )
    both, sent_head, sent_down = together(both, head_weight, down_weight)
    head_send = lax.dynamic_slice_in_dim(sent_head, far * V_HALF, V_HALF, 1)
    down_send = lax.dynamic_slice_in_dim(sent_down, far * FF_HALF, FF_HALF, 0)
    both, head_got, down_got = together(
        exchange(both.reshape(CHIPS, BLOCK, 2 * FF_HALF), WIDTH_CHIPS),
        other_core(head_send),
        other_core(down_send),
    )
    hidden, silu_gate = on_core(
        hidden_kernel,
        core,
        (both, digits),
        [whole(both), whole(digits)],
        [((CHIPS, BLOCK, FF_HALF + PAD), bf16), ((BLOCK, FF_HALF), f32)],
        1000000,
    )

    hidden_own = exchange(hidden, WIDTH_CHIPS).reshape(count, FF_HALF + PAD)
    hidden_far = other_core(hidden_own)
    own_part = dot(hidden_own[:, :FF_HALF], lax.dynamic_slice_in_dim(down_weight, core * FF_HALF, FF_HALF, 0))
    branch = on_core(
        branch_kernel,
        core,
        (own_part, hidden_far, down_weight),
        [
            whole(own_part),
            whole(hidden_far),
            pl.BlockSpec((FF_HALF, width), lambda step, half: (1 - half[0], 0)),
        ],
        [((count, width), bf16)],
        gate_up_flops,
    )
    branch, hidden_own = together(branch, hidden_own)
    digits = hidden_own[:, FF_HALF : FF_HALF + 4].astype(jnp.int32)
    all_labels = digits[:, :2] * PAD + digits[:, 2:]
    all_labels = jnp.where(core == 0, all_labels, reverse_blocks(all_labels))
    width_chip = lax.axis_index(WIDTH_CHIPS)
    branch, label_row, labels = together(
        exchange(branch.reshape(CHIPS, BLOCK, width), UNIT_CHIPS),
        label_rows(all_labels, head_weight, unit_chip),
        lax.dynamic_slice_in_dim(all_labels, width_chip * BLOCK, BLOCK, 0),
    )
    branch = jnp.sum(branch.astype(f32), axis=0)
    own_tokens = lax.dynamic_slice_in_dim(tokens, unit_chip * BLOCK, BLOCK, 0)
    summed = own_tokens.astype(f32) + branch
    rows = to_all(summed.astype(bf16), UNIT_CHIPS).reshape(count, width)

    far_rows = other_core(rows)
    logit_flops = 4 * count * width * V_HALF
    raw = on_core(
        logits_kernel,
        core,
        (rows, far_rows, head_weight, head_got),
        [whole(rows), whole(far_rows), columns_of(head_weight, V_HALF), whole(head_got)],
        [((count, V_HALF + PAD), jnp.int16)],
        logit_flops,
    )
    raw, label_row = together(raw, label_row)
    raw, label_row = together(
        exchange(raw.reshape(CHIPS, BLOCK, V_HALF + PAD), WIDTH_CHIPS), near_label_rows(label_row)
    )
    vocab_start = ((unit_chip * 2 + core) * V_HALF).astype(jnp.int32)
    packed = on_core(
        softmax_kernel,
        vocab_start,
        (raw, labels),
        [whole(raw), whole(labels)],
        [((CHIPS, BLOCK, V_HALF + PAD), bf16)],
        1000000,
    )
    packed, token_rows, label_row = together(packed, tokens, label_row)
    turned = token_rows.T
    turned_reverse = reverse_blocks(token_rows).T
    packed_own, turned_own, turned_far, label_row = together(
        exchange(packed, WIDTH_CHIPS),
        jnp.where(core == 0, turned, turned_reverse),
        jnp.where(core == 0, turned_reverse, turned),
        plane_label_rows(*label_row),
    )
    label_row, label_sent = label_row
    packed_own = packed_own.reshape(count, V_HALF + PAD)
    packed_far = other_core(packed_own)
    packed = on_core(
        pull_back,
        core,
        (packed_own, packed_far, head_weight, head_weight),
        [
            whole(packed_own),
            whole(packed_far),
            pl.BlockSpec((width, V_HALF), lambda step, half: (0, half[0])),
            pl.BlockSpec((width, V_HALF), lambda step, half: (0, 1 - half[0])),
        ],
        [((count, width + PAD), bf16)],
        logit_flops,
    )
    packed, label_sent = together(packed, label_sent)
    label_got = other_plane(label_sent)
    packed = exchange(packed.reshape(CHIPS, BLOCK, width + PAD), UNIT_CHIPS)
    label_row = label_row.astype(f32) + label_got.astype(f32)
    stats = from_three(packed[:, :, width:], N_STATS)
    row_top = jnp.max(stats[:, :, 0:1], axis=0, keepdims=True)
    weight = jnp.exp(stats[:, :, 0:1] - row_top)
    weight = weight / jnp.sum(weight * stats[:, :, 2:3], axis=0, keepdims=True)
    pulled = jnp.sum(weight * packed[:, :, :width].astype(f32), axis=0)
    pull = jnp.sum(weight * stats[:, :, 3:4], axis=0)
    inv_rms = stats[0, :, 1:2]
    scaled = summed * inv_rms
    dsummed = []
    for which in range(2):
        label_logit = jnp.sum(stats[:, :, 4 + 2 * which : 5 + 2 * which], axis=0)
        rest = jnp.sum(weight * stats[:, :, 5 + 2 * which : 6 + 2 * which], axis=0)
        dnormed = pulled - (1.0 - rest) * label_row[:, which * width : (which + 1) * width]
        mean = (pull - (1.0 - rest) * label_logit) / D
        dsummed.append((inv_rms * (dnormed - scaled * mean)).astype(bf16))
    dsummed = to_all(jnp.concatenate(dsummed, axis=1), UNIT_CHIPS).reshape(count, 2 * width)

    far_dsummed = other_core(dsummed)
    dhidden = on_core(
        back_kernel,
        core,
        (dsummed, far_dsummed, down_weight, down_got),
        [whole(dsummed), whole(far_dsummed), rows_of(down_weight, FF_HALF), whole(down_got)],
        [((count, 2 * FF_HALF), bf16)],
        2 * gate_up_flops,
    )
    dhidden = exchange(dhidden.reshape(CHIPS, BLOCK, 2 * FF_HALF), WIDTH_CHIPS)
    dhidden = jnp.sum(dhidden.astype(f32), axis=0)
    cot = (dhidden * jnp.concatenate([silu_gate, silu_gate], axis=1)).astype(bf16)
    cot_own = to_all(cot, WIDTH_CHIPS).reshape(count, 2 * FF_HALF)
    cot_far = other_core(cot_own)
    done = sophia_half(core, turned_own, cot_own, up_moment, up_curvature, ())
    return tuple(sophia_half(far, turned_far, cot_far, up_moment, up_curvature, done))


def solution(mesh):
    fine = Mesh(mesh.devices.reshape(2, 4, 2, 4, 2), ("xl", "y", "core", "z", "xh"))
    dp = ("xl", "y", "core")
    tensor = ("z", "xh")
    both = P(dp, tensor)
    placed = (P(None, dp), both, both, P(tensor, dp), both, both, both, P(dp), P(dp))
    return jax.shard_map(
        on_device,
        mesh=fine,
        in_specs=placed,
        out_specs=(both, both, both),
        check_vma=False,
    )
```
